32 devices in a mesh: fsdp: 16 (over z, y, x), vocab: 2 (over core).
Axes of the slice: x: 2, y: 2, z: 4, core: 2. Of those that a mesh axis runs over, the one named last changes fastest.
Arguments:
- token_ids: int32 [32, 512], P('fsdp'), may hold values from 0 to 30719
- lengths: int32 [32], replicated, may hold values from 32 to 512, as said below
- masked_pos: int32 [32, 80], replicated, may hold values from 0 to 511, as said below
- teacher: bfloat16 [2560, 30720], P('fsdp', 'vocab'), may hold values from -12 to 12
- stack_index: int32 [6144, 48], P(('fsdp', 'vocab')), may hold values from 17476 to 61166, as said below
- down_index: int32 [768, 192], P(('fsdp', 'vocab')), may hold values from 17476 to 61166, as said below
- stack_next: int32 [6144, 48], P(('fsdp', 'vocab')), may hold values from 17476 to 61166, as said below
- down_next: int32 [768, 192], P(('fsdp', 'vocab')), may hold values from 17476 to 61166, as said below
- word_table: float32 [30720, 768], P('vocab', 'fsdp')
- table_first: float32 [30720, 768], P('vocab', 'fsdp'), may hold values from -1.4305115e-06 to 1.4305115e-06
- table_second: float32 [30720, 768], P('vocab', 'fsdp'), may hold values from 8.0371547e-16 to 3.2148619e-15
- pos_table: float32 [512, 768], P(None, ('fsdp', 'vocab')), may hold values from -6 to 6
- pos_first: float32 [512, 768], P(None, ('fsdp', 'vocab')), may hold values from -1.4305115e-06 to 1.4305115e-06
- pos_second: float32 [512, 768], P(None, ('fsdp', 'vocab')), may hold values from 8.0371547e-16 to 3.2148619e-15
- proj_stack: float32 [6144, 768], P(('fsdp', 'vocab')), may hold values from -0.21875 to 0.21875
- stack_first: float32 [6144, 768], P(('fsdp', 'vocab')), may hold values from -1.4305115e-06 to 1.4305115e-06
- stack_second: float32 [6144, 768], P(('fsdp', 'vocab')), may hold values from 8.0371547e-16 to 3.2148619e-15
- ffn_down: float32 [768, 3072], P(('fsdp', 'vocab')), may hold values from -0.109375 to 0.109375
- down_first: float32 [768, 3072], P(('fsdp', 'vocab')), may hold values from -1.4305115e-06 to 1.4305115e-06
- down_second: float32 [768, 3072], P(('fsdp', 'vocab')), may hold values from 8.0371547e-16 to 3.2148619e-15
- vectors: float32 [10752], P(('fsdp', 'vocab'))
- vectors_first: float32 [10752], P(('fsdp', 'vocab')), may hold values from -7.6293945e-06 to 7.6293945e-06
- vectors_second: float32 [10752], P(('fsdp', 'vocab')), may hold values from 2.0092887e-14 to 8.037155e-14
- head_bias: float32 [30720], P('vocab'), may hold values from -6 to 6
- bias_first: float32 [30720], P('vocab'), may hold values from -7.6293945e-06 to 7.6293945e-06
- bias_second_moment: float32 [30720], P('vocab'), may hold values from 2.0092887e-14 to 8.037155e-14
Outputs:
- table_moment: float32 [30720, 768], P('vocab', 'fsdp')
- table_square: float32 [30720, 768], P('vocab', 'fsdp')
- table_new: float32 [30720, 768], P('vocab', 'fsdp')
- pos_moment: float32 [512, 768], P(None, ('fsdp', 'vocab'))
- pos_square: float32 [512, 768], P(None, ('fsdp', 'vocab'))
- pos_new: float32 [512, 768], P(None, ('fsdp', 'vocab'))
- stack_moment: float32 [6144, 768], P(('fsdp', 'vocab'))
- stack_square: float32 [6144, 768], P(('fsdp', 'vocab'))
- updated_stack: float32 [6144, 768], P(('fsdp', 'vocab'))
- down_moment: float32 [768, 3072], P(('fsdp', 'vocab'))
- down_square: float32 [768, 3072], P(('fsdp', 'vocab'))
- down_new: float32 [768, 3072], P(('fsdp', 'vocab'))
- vectors_moment: float32 [10752], P(('fsdp', 'vocab'))
- vectors_square: float32 [10752], P(('fsdp', 'vocab'))
- vectors_new: float32 [10752], P(('fsdp', 'vocab'))
- bias_moment: float32 [30720], P('vocab')
- bias_square: float32 [30720], P('vocab')
- bias_new: float32 [30720], P('vocab')
- loss_sum: float32 [], replicated
- masked_slot_count: float32 [], replicated
- grad_norm: float32 [], replicated
- mask_changes: int32 [], replicated
The draws below stay inside these ranges and needn't reach their ends.
Inputs may be any that keep to these rules, and one draw needn't show every extreme that they name: Sequence s has its first lengths[s] slots live; one sequence has exactly 512 and one exactly 32. `masked_pos`: within a sequence the slots are distinct; the first is below 32. `stack_index`: each word packs 8 digits; the two digits of a group are distinct, the first the smaller. `down_index`: as stack_index. `stack_next`: as stack_index. `down_next`: as stack_index.
All inputs are finite; a program needn't handle non-finite values.
Results may differ from the reference program's by a relative error of at most 0.004.
The reference program's roundings to bfloat16 on the way count: a program that leaves them out, or rounds other values in their place, can miss the bound.
Values may be sent and summed in bfloat16 or wider, within the bound.
No kernel may reach another device: no remote copies, remote signals or barrier semaphores. Data moves between devices by JAX's collectives and lax.ppermute only.
A program may use at most 320 MiB of HBM per device.

```python
import math
import jax
import jax.numpy as jnp
import numpy as np
from jax import lax

D = 768
HEAD_DIM = 64
FF = 3072
VOCAB = 30720
LEN = 512
MIN_LEN = 32
MASK_SEQ = 80
STEP = 10
SEQ_DEV = 1
SEQS = 32
ROWS_A = 6144
SMALL = 10752
PARAMS = 31105536


def pack_slots(key, count_rows, width):
    pattern = jax.random.randint(key, (count_rows, width // 4), 0, 6)
    first_table = jnp.array([0, 0, 0, 1, 1, 2], jnp.int32)
    second_table = jnp.array([1, 2, 3, 2, 3, 3], jnp.int32)
    slots = jnp.stack([first_table[pattern], second_table[pattern]], -1).reshape(count_rows, width // 16, 8)
    powers = 4 ** jnp.arange(8, dtype=jnp.int32)
    return jnp.sum(slots * powers, -1).astype(jnp.int32)


def draw_stack_index(key, part):
    key = jax.random.fold_in(key, 11)
    return pack_slots(key, 4 * D + FF, D)


def draw_down_index(key, part):
    key = jax.random.fold_in(key, 13)
    return pack_slots(key, D, FF)


def draw_stack_next(key, part):
    key = jax.random.fold_in(key, 17)
    return pack_slots(key, 4 * D + FF, D)


def draw_down_next(key, part):
    key = jax.random.fold_in(key, 19)
    return pack_slots(key, D, FF)


def draw_lengths(key, part):
    key = jax.random.fold_in(key, 3)
    roll_key, long_key, short_key = jax.random.split(key, 3)
    devices = SEQS // SEQ_DEV
    rank = jnp.arange(SEQS, dtype=jnp.int32) // SEQ_DEV
    reach = (LEN - MIN_LEN) * (devices - 1 + 2 * rank) // (3 * max(devices - 1, 1))
    roll = jax.random.randint(roll_key, (SEQS,), 0, 1001)
    sized = MIN_LEN + roll * roll // 1000 * reach // 1000
    longest = jax.random.randint(long_key, (), 0, SEQS)
    shortest = (longest + 1 + jax.random.randint(short_key, (), 0, SEQS - 1)) % SEQS
    place = jnp.arange(SEQS, dtype=jnp.int32)
    sized = jnp.where(place == longest, LEN, sized)
    sized = jnp.where(place == shortest, MIN_LEN, sized)
    return sized.astype(jnp.int32)


def draw_masked_pos(key, part):
    key = jax.random.fold_in(key, 5)
    lead_key, rest_key = jax.random.split(key)
    lead = jax.random.randint(lead_key, (SEQS,), 0, MIN_LEN)
    subkeys = jax.random.split(rest_key, SEQS)

    def shuffled_order(subkey):
        return jax.random.permutation(subkey, LEN - 1)[:MASK_SEQ - 1]
    order = jax.vmap(shuffled_order)(subkeys)
    rest = order + (order >= lead[:, None]).astype(jnp.int32)
    return jnp.concatenate([lead[:, None], rest], 1).astype(jnp.int32)


def draw_word_table(key, part):
    key = jax.random.fold_in(key, 7)
    rise = jnp.arange(VOCAB, dtype=jnp.float32)[:, None] / VOCAB
    base = jax.random.normal(key, (VOCAB, D), jnp.float32)
    return base * (1.0 + 2.0 * rise) / math.sqrt(D)


def draw_vectors(key, part):
    key = jax.random.fold_in(key, 9)
    total = 10 * D + FF
    place = jnp.arange(total, dtype=jnp.int32)
    noise = jax.random.normal(key, (total,), jnp.float32)
    feature = (place % D).astype(jnp.float32) / D
    is_gain = (place < 6 * D) & (place // D % 2 == 0)
    gains = (0.6 + 1.2 * feature) * (1.0 + 0.1 * noise)
    return jnp.where(is_gain, gains, 0.3 * noise)


def touch_ends(values, key, least, high):
    longest = values.shape.index(max(values.shape))
    spots = []
    for shift in (0, 1):
        where = [jax.random.randint(jax.random.fold_in(key, axis), (), 0, length) for axis, length in enumerate(values.shape)]
        where[longest] = (where[longest] + shift) % values.shape[longest]
        spots.append(tuple(where))
    return values.at[spots[0]].set(least).at[spots[1]].set(high)


def block_scale(own_key, extent, shards, low, top_value):
    loudness = 1.0
    for position, blocks in shards:
        steps = jax.random.uniform(jax.random.fold_in(jax.random.fold_in(own_key, 6), position), (blocks,), jnp.float32, low / len(shards), top_value / len(shards))
        loudness = loudness * jnp.repeat(jnp.exp(steps), extent[position] // blocks).reshape((-1,) + (1,) * (len(extent) - 1 - position))
    return loudness


def rank_table(number_of, skew):
    portions = [(1 << 20) // math.isqrt(rank ** skew) + 1 for rank in range(1, number_of + 1)]
    scale = 1 + sum(portions) // (1 << 30)
    return np.cumsum(np.array([max(1, weight // scale) for weight in portions]))


def ranked(stream_key, shape, count, skew):
    table = rank_table(count, skew)
    pick = jax.random.randint(jax.random.fold_in(stream_key, 1), shape, 0, int(table[count - 1]))
    grade = jnp.searchsorted(jnp.asarray(table, jnp.int32), pick, side="right")
    return jax.random.permutation(jax.random.fold_in(stream_key, 2), count)[grade].astype(jnp.int32)


def normal_values(rng, extent, scale, limit, cuts=(), held_as=jnp.bfloat16):
    entries = scale * jax.random.normal(rng, extent, jnp.float32)
    if cuts:
        entries = entries * block_scale(rng, extent, cuts, -0.22, 0.18)
    return jnp.clip(entries, -limit, limit).astype(held_as)


def setup_inputs(seed: int = 0) -> dict:
    keys = jax.random.split(jax.random.key(seed), 27)
    return {
        "token_ids": touch_ends(ranked(keys[0], (SEQS, LEN), VOCAB, 2), jax.random.fold_in(keys[0], 3), 0, VOCAB - 1).astype(jnp.int32),
        "lengths": draw_lengths(jax.random.fold_in(keys[26], 71), 0),
        "masked_pos": draw_masked_pos(jax.random.fold_in(keys[26], 71), 0),
        "teacher": normal_values(keys[3], (SEQS * MASK_SEQ, VOCAB), 2.0, 12.0, ((0, 16), (1, 2))),
        "stack_index": draw_stack_index(jax.random.fold_in(keys[26], 71), 0),
        "down_index": draw_down_index(jax.random.fold_in(keys[26], 71), 0),
        "stack_next": draw_stack_next(jax.random.fold_in(keys[26], 71), 0),
        "down_next": draw_down_next(jax.random.fold_in(keys[26], 71), 0),
        "word_table": draw_word_table(jax.random.fold_in(keys[26], 71), 0),
        "table_first": normal_values(keys[9], (VOCAB, D), (0.000555 / PARAMS ** 0.5), 1.430511474609375e-06, ((0, 2), (1, 16)), jnp.float32),
        "table_second": jnp.clip(jnp.exp(math.log(3.2148618822939144e-15) - 1.3862944 * jax.random.uniform(keys[10], (VOCAB, D), jnp.float32) ** block_scale(keys[10], (VOCAB, D), ((0, 2), (1, 16)), -0.2, 0.2)), 8.037154705734786e-16, 3.2148618822939144e-15),
        "pos_table": normal_values(keys[11], (LEN, D), 0.5, 6.0, ((1, 32),), jnp.float32),
        "pos_first": normal_values(keys[12], (LEN, D), (0.000555 / PARAMS ** 0.5), 1.430511474609375e-06, ((1, 32),), jnp.float32),
        "pos_second": jnp.clip(jnp.exp(math.log(3.2148618822939144e-15) - 1.3862944 * jax.random.uniform(keys[13], (LEN, D), jnp.float32) ** block_scale(keys[13], (LEN, D), ((1, 32),), -0.2, 0.2)), 8.037154705734786e-16, 3.2148618822939144e-15),
        "proj_stack": normal_values(keys[14], (ROWS_A, D), D ** -0.5, 0.21875, ((0, 32),), jnp.float32),
        "stack_first": normal_values(keys[15], (ROWS_A, D), (0.000555 / PARAMS ** 0.5), 1.430511474609375e-06, ((0, 32),), jnp.float32),
        "stack_second": jnp.clip(jnp.exp(math.log(3.2148618822939144e-15) - 1.3862944 * jax.random.uniform(keys[16], (ROWS_A, D), jnp.float32) ** block_scale(keys[16], (ROWS_A, D), ((0, 32),), -0.2, 0.2)), 8.037154705734786e-16, 3.2148618822939144e-15),
        "ffn_down": normal_values(keys[17], (D, FF), FF ** -0.5, 0.109375, ((0, 32),), jnp.float32),
        "down_first": normal_values(keys[18], (D, FF), (0.000555 / PARAMS ** 0.5), 1.430511474609375e-06, ((0, 32),), jnp.float32),
        "down_second": jnp.clip(jnp.exp(math.log(3.2148618822939144e-15) - 1.3862944 * jax.random.uniform(keys[19], (D, FF), jnp.float32) ** block_scale(keys[19], (D, FF), ((0, 32),), -0.2, 0.2)), 8.037154705734786e-16, 3.2148618822939144e-15),
        "vectors": draw_vectors(jax.random.fold_in(keys[26], 71), 0),
        "vectors_first": normal_values(keys[21], (SMALL,), (0.002775 / PARAMS ** 0.5), 7.62939453125e-06, ((0, 32),), jnp.float32),
        "vectors_second": jnp.clip(jnp.exp(math.log(8.037154790438081e-14) - 1.3862944 * jax.random.uniform(keys[22], (SMALL,), jnp.float32) ** block_scale(keys[22], (SMALL,), ((0, 32),), -0.2, 0.2)), 2.0092886976095202e-14, 8.037154790438081e-14),
        "head_bias": normal_values(keys[23], (VOCAB,), 0.5, 6.0, ((0, 2),), jnp.float32),
        "bias_first": normal_values(keys[24], (VOCAB,), (0.002775 / PARAMS ** 0.5), 7.62939453125e-06, ((0, 2),), jnp.float32),
        "bias_second_moment": jnp.clip(jnp.exp(math.log(8.037154790438081e-14) - 1.3862944 * jax.random.uniform(keys[25], (VOCAB,), jnp.float32) ** block_scale(keys[25], (VOCAB,), ((0, 2),), -0.2, 0.2)), 2.0092886976095202e-14, 8.037154790438081e-14),
    }


@jax.custom_vjp
def low(v):
    return lax.optimization_barrier(v.astype(jnp.bfloat16)).astype(jnp.float32)

@jax.custom_vjp
def low_back(v):
    return v

def low_keep(v):
    return (low(v), None)

def low_pass(kept, grad):
    return (grad,)

def back_keep(v):
    return (v, None)

def back_low(kept, grad):
    return (low(grad),)
low.defvjp(low_keep, low_pass)
low_back.defvjp(back_keep, back_low)
NORM_EPS = 1e-05
CLIP = 0.005
PRUNE_DECAY = 0.0002
BETA_ONE = 0.9
BETA_TWO = 0.999
ADAM_EPS = 1e-08
WEIGHT_DECAY = 0.01
RATE_MATRIX = 0.1
RATE_VECTOR = 1.0
SCORE_SCALE = 0.125
HIGH = lax.Precision.HIGHEST

def unpack(words):
    powers = 4 ** jnp.arange(8, dtype=jnp.int32)
    digits = words[..., None] // powers % 4
    return digits.reshape(words.shape[0], words.shape[1] * 8)

def keep_mask(words):
    count_rows = words.shape[0]
    groups = words.shape[1] * 4
    places = unpack(words).reshape(count_rows, groups, 2)
    spots = jnp.arange(4, dtype=jnp.int32)
    chosen = (places[:, :, 0:1] == spots) | (places[:, :, 1:2] == spots)
    return chosen.reshape(count_rows, groups * 4).astype(jnp.float32)

def split_vectors(vectors_all, width):
    hidden_units = vectors_all.shape[0] - 10 * width
    pieces = []
    offset = 0
    for piece_len in [width] * 9 + [hidden_units, width]:
        pieces.append(vectors_all[offset:offset + piece_len])
        offset = offset + piece_len
    return pieces

def layer_norm(input_batch, gain, shift):
    center = input_batch - lax.optimization_barrier(jnp.mean(input_batch, axis=-1, keepdims=True))
    spread = lax.optimization_barrier(jnp.mean(center * center, axis=-1, keepdims=True))
    return center * lax.rsqrt(spread + NORM_EPS) * gain + shift

def project(input_batch, weight_matrix):
    return jnp.einsum('gtd,nd->gtn', input_batch, weight_matrix, precision=HIGH)

def encoder(table_low, pos_low, stack_low, down_low, parts, token_ids, lengths):
    gain_embed, shift_embed, gain_attn, shift_attn, gain_ffn, shift_ffn, bias_query, bias_value, bias_out, bias_hidden, bias_down = parts
    width = stack_low.shape[1]
    heads = width // HEAD_DIM
    group = math.gcd(8, token_ids.shape[0])

    def block(pieces):
        tok_ids, seq_lengths = pieces
        normed = layer_norm(table_low[tok_ids] + pos_low[None], gain_embed, shift_embed)
        normed_low = low(normed)
        qkv_bias = jnp.concatenate([bias_query, jnp.zeros_like(bias_query), bias_value])
        qkv = low(low_back(project(normed_low, stack_low[:3 * width]) + qkv_bias))
        split = qkv.reshape(group, LEN, 3, heads, HEAD_DIM)
        raw = low_back(jnp.einsum('gqhe,gkhe->ghqk', split[:, :, 0], split[:, :, 1], precision=HIGH) * SCORE_SCALE)
        live = jnp.arange(LEN)[None, :] < seq_lengths[:, None]
        scores = jnp.where(live[:, None, None, :], raw, -1e+30)
        prob = low(jax.nn.softmax(scores, axis=-1))
        context = jnp.einsum('ghqk,gkhe->gqhe', prob, split[:, :, 2], precision=HIGH)
        context = low(low_back(context)).reshape(group, LEN, width)
        attn = low_back(project(context, stack_low[3 * width:4 * width]) + bias_out)
        first_out = layer_norm(normed + attn, gain_attn, shift_attn)
        pre_act = low_back(project(low(first_out), stack_low[4 * width:]) + bias_hidden)
        ffn = low_back(project(low(jax.nn.gelu(pre_act, approximate=False)), down_low) + bias_down)
        return layer_norm(first_out + ffn, gain_ffn, shift_ffn)
    outs = lax.map(jax.checkpoint(block), (token_ids.reshape(-1, group, LEN), lengths.reshape(-1, group)))
    return outs.reshape(-1, LEN, width)

def objective(table, pos_table, stack, down, vectors, head_bias, token_ids, lengths, masked_pos, teach, valid, count):
    width = stack.shape[1]
    table_low = low(table)
    parts = split_vectors(low(vectors), width)
    final = encoder(table_low, low(pos_table), low(stack), low(down), parts, token_ids, lengths)
    picked = jnp.take_along_axis(final, masked_pos[:, :, None], axis=1)
    picked = low(picked.reshape(-1, width))
    block_rows = math.gcd(512, picked.shape[0])

    def head(pieces):
        rows_low, teach_rows, weight_rows = pieces
        output_logits = low_back(jnp.dot(rows_low, table_low.T, precision=HIGH) + head_bias)
        teach_log = jax.nn.log_softmax(teach_rows, axis=-1)
        student_log = jax.nn.log_softmax(output_logits, axis=-1)
        return lax.optimization_barrier(jnp.sum(jnp.exp(teach_log) * (teach_log - student_log), axis=-1)) * weight_rows
    losses = lax.map(jax.checkpoint(head), (picked.reshape(-1, block_rows, width), teach.reshape(-1, block_rows, teach.shape[1]), valid.reshape(-1, block_rows)))
    loss_sum = jnp.sum(losses)
    return (loss_sum / count, loss_sum)

def adam(weight_matrix, grad, first, second, rate):
    first = BETA_ONE * first + (1.0 - BETA_ONE) * grad
    second = BETA_TWO * second + (1.0 - BETA_TWO) * grad * grad
    first_hat = first / (1.0 - BETA_ONE ** STEP)
    second_hat = second / (1.0 - BETA_TWO ** STEP)
    new = weight_matrix - rate * (first_hat / (jnp.sqrt(second_hat) + ADAM_EPS) + WEIGHT_DECAY * weight_matrix)
    return (first, second, new)

def reference(token_ids, lengths, masked_pos, teacher, stack_index, down_index, stack_next, down_next, word_table, table_first, table_second, pos_table, pos_first, pos_second, proj_stack, stack_first, stack_second, ffn_down, down_first, down_second, vectors, vectors_first, vectors_second, head_bias, bias_first, bias_second_moment):
    stack_mask = keep_mask(stack_index)
    down_mask = keep_mask(down_index)
    valid = (masked_pos < lengths[:, None]).astype(jnp.float32).reshape(-1)
    count = jnp.sum(valid)
    teach = teacher.astype(jnp.float32)

    def loss_fn(table, positions, stack, down, vecs, bias):
        return objective(table, positions, stack, down, vecs, bias, token_ids, lengths, masked_pos, teach, valid, count)
    primal, pull, loss_sum = jax.vjp(loss_fn, word_table, pos_table, proj_stack * stack_mask, ffn_down * down_mask, vectors, head_bias, has_aux=True)
    table_grad, pos_grad, stack_grad, down_grad, vectors_grad, bias_grad = pull(jnp.ones_like(primal))
    stack_grad = stack_grad + PRUNE_DECAY * (1.0 - stack_mask) * proj_stack
    down_grad = down_grad + PRUNE_DECAY * (1.0 - down_mask) * ffn_down
    every = (table_grad, pos_grad, stack_grad, down_grad, vectors_grad, bias_grad)
    squares = jnp.zeros((), jnp.float32)
    for gradient in every:
        squares = squares + jnp.sum(gradient * gradient)
    grad_norm = jnp.sqrt(squares)
    factor = jnp.minimum(1.0, CLIP / (grad_norm + 1e-06))
    table_out = adam(word_table, table_grad * factor, table_first, table_second, RATE_MATRIX)
    pos_out = adam(pos_table, pos_grad * factor, pos_first, pos_second, RATE_MATRIX)
    stack_out = adam(proj_stack, stack_grad * factor, stack_first, stack_second, RATE_MATRIX)
    down_out = adam(ffn_down, down_grad * factor, down_first, down_second, RATE_MATRIX)
    vectors_out = adam(vectors, vectors_grad * factor, vectors_first, vectors_second, RATE_VECTOR)
    bias_out = adam(head_bias, bias_grad * factor, bias_first, bias_second_moment, RATE_VECTOR)
    changes = jnp.sum((stack_mask != keep_mask(stack_next)).astype(jnp.int32)) + jnp.sum((down_mask != keep_mask(down_next)).astype(jnp.int32))
    return (table_out[0], table_out[1], table_out[2], pos_out[0], pos_out[1], pos_out[2], stack_out[0], stack_out[1], stack_out[2], down_out[0], down_out[1], down_out[2], vectors_out[0], vectors_out[1], vectors_out[2], bias_out[0], bias_out[1], bias_out[2], loss_sum, count, grad_norm, changes.astype(jnp.int32))
```

```python
import functools
import math

import jax
import jax.numpy as jnp
from jax import lax
from jax.experimental import pallas as pl
from jax.experimental.pallas import tpu as pltpu
from jax.sharding import PartitionSpec as P

HEAD_DIM = 64
STEP = 10


NORM_EPS = 1e-05
CLIP = 0.005
PRUNE_DECAY = 0.0002
BETA_ONE = 0.9
BETA_TWO = 0.999
ADAM_EPS = 1e-08
WEIGHT_DECAY = 0.01
RATE_MATRIX = 0.1
RATE_VECTOR = 1.0
SCORE_SCALE = 0.125


HIGH_COUNT = 512
BOTH = ("fsdp", "vocab")


def kept(words):
    columns = words.shape[1] * 16
    place = lax.broadcasted_iota(jnp.int32, (2 * words.shape[1], columns), 0)
    column = lax.broadcasted_iota(jnp.int32, (2 * words.shape[1], columns), 1)
    spread = (place % words.shape[1] * 2 + place // words.shape[1] == column // 8).astype(
        jnp.bfloat16
    )
    bytes_low = jnp.concatenate([words & 255, words >> 8], 1).astype(jnp.bfloat16)
    byte = jnp.dot(bytes_low, spread, preferred_element_type=jnp.float32).astype(jnp.int32)
    spot = lax.broadcasted_iota(jnp.int32, byte.shape, 1)
    nibble = jnp.where(spot % 8 < 4, byte & 15, byte >> 4)
    spot = spot % 4
    return ((nibble & 3) == spot) | ((nibble >> 2) == spot)


def swap(x, axis, bit):
    size = lax.axis_size(axis)
    return lax.ppermute(x, axis, [(i, i ^ bit) for i in range(size)])


def my_bit(axis, bit):
    return lax.axis_index(axis) // bit % 2


def bits_of(size):
    return [1 << k for k in range(size.bit_length() - 1)]


def sum_all(x, axis, bits):
    for bit in bits:
        x = jax.tree.map(lambda part: part + swap(part, axis, bit), x)
    return x


def join(x, axis, bit):
    other = swap(x, axis, bit)
    upper = my_bit(axis, bit) == 1
    return jnp.stack([jnp.where(upper, other, x), jnp.where(upper, x, other)])


def halve(x, axis, bit):
    mine = my_bit(axis, bit)
    return lax.dynamic_index_in_dim(x, mine, 0, False) + swap(
        lax.dynamic_index_in_dim(x, 1 - mine, 0, False), axis, bit
    )


def near_exchange(take, near):
    size = lax.axis_size("fsdp")
    p = lax.axis_index("fsdp") % near
    return [take(p)] + [
        lax.ppermute(take(p ^ k), "fsdp", [(i, i ^ k) for i in range(size)]) for k in range(1, near)
    ]


def far_groups(near):
    size = lax.axis_size("fsdp")
    return [list(range(q, size, near)) for q in range(near)]


def far_gather(x, near):
    size = lax.axis_size("fsdp")
    far = size // near
    if far != 4:
        return lax.all_gather(x, "fsdp", axis=0, tiled=True, axis_index_groups=far_groups(near))
    z = lax.axis_index("fsdp") // near
    up, down = [], []
    send_up = send_down = x
    for k in range(1, far):
        send_up = lax.ppermute(
            send_up, "fsdp", [(i, i + near) for i in range((k - 1) * near, size - near)]
        )
        send_down = lax.ppermute(
            send_down, "fsdp", [(i, i - near) for i in range(near, size - (k - 1) * near)]
        )
        up.append(send_up)
        down.append(send_down)
    line = jnp.concatenate(up[::-1] + [x] + down, 0)
    rows = x.shape[0]
    return lax.dynamic_slice_in_dim(line, (far - 1 - z) * rows, far * rows, 0)


def far_scatter(x, near):
    size = lax.axis_size("fsdp")
    far = size // near
    if far != 4:
        flat = lax.psum_scatter(
            x, "fsdp", scatter_dimension=0, tiled=True, axis_index_groups=far_groups(near)
        )
        return flat[0]
    z = lax.axis_index("fsdp") // near

    def entry(j):
        return lax.dynamic_index_in_dim(x, jnp.clip(j, 0, far - 1), 0, False)

    up = down = None
    for k in range(1, far):
        send_up, send_down = entry(far - k + z), entry(z - far + k)
        if up is not None:
            send_up, send_down = send_up + up, send_down + down
        up = lax.ppermute(send_up, "fsdp", [(i, i + near) for i in range(k * near)])
        down = lax.ppermute(
            send_down, "fsdp", [(i, i - near) for i in range(size - k * near, size)]
        )
    return entry(z) + up + down


def lookup_kernel(low_count, ids_ref, table_ref, out_ref, spread):
    width = table_ref.shape[0]

    @pl.when(pl.program_id(0) == 0)
    def _():
        for low in range(low_count):
            spread[low * width : (low + 1) * width, :] = table_ref[
                :, low * HIGH_COUNT : (low + 1) * HIGH_COUNT
            ].astype(jnp.bfloat16)

    ids = ids_ref[0]
    low_ids = ids >> 9
    row = lax.broadcasted_iota(jnp.int32, (HIGH_COUNT, ids.shape[1]), 0)
    match = (row == (ids & (HIGH_COUNT - 1))).astype(jnp.bfloat16)
    found = jnp.dot(spread[...], match, preferred_element_type=jnp.float32)
    total = jnp.zeros((width, ids.shape[1]), jnp.float32)
    for low in range(low_count):
        total = jnp.where(low_ids == low, found[low * width : (low + 1) * width, :], total)
    out_ref[0] = total.astype(out_ref.dtype)


def lookup(table_t, ids):
    rows = table_t.shape[0]
    table_t = jnp.pad(table_t, ((0, -rows % 16), (0, 0)))
    width, vocab = table_t.shape
    blocks, _, length = ids.shape
    low_count = vocab // HIGH_COUNT
    found = pl.pallas_call(
        functools.partial(lookup_kernel, low_count),
        grid=(blocks,),
        in_specs=[
            pl.BlockSpec((1, 1, length), lambda i: (i, 0, 0)),
            pl.BlockSpec((width, vocab), lambda i: (0, 0)),
        ],
        out_specs=pl.BlockSpec((1, width, length), lambda i: (i, 0, 0)),
        out_shape=jax.ShapeDtypeStruct((blocks, width, length), jnp.bfloat16),
        scratch_shapes=[pltpu.VMEM((low_count * width, HIGH_COUNT), jnp.bfloat16)],
        compiler_params=pltpu.CompilerParams(vmem_limit_bytes=40 * 1024 * 1024),
        cost_estimate=pl.CostEstimate(
            flops=2 * blocks * length * width * vocab,
            bytes_accessed=4 * width * vocab + 2 * blocks * width * length,
            transcendentals=0,
        ),
        name="lookup",
    )(ids, table_t)
    return found[:, :rows]


def spread_kernel(low_count, ids_ref, grad_ref, base_ref, out_ref, lhs, total):
    width = grad_ref.shape[1]
    step = pl.program_id(0)

    @pl.when(step == 0)
    def _():
        total[...] = jnp.zeros_like(total)

    ids = ids_ref[0]
    low_ids = ids >> 9
    grad = grad_ref[0].astype(jnp.float32)
    for low in range(low_count):
        lhs[low * width : (low + 1) * width, :] = jnp.where(low_ids == low, grad, 0.0).astype(
            jnp.bfloat16
        )
    row = lax.broadcasted_iota(jnp.int32, (HIGH_COUNT, ids.shape[1]), 0)
    match = (row == (ids & (HIGH_COUNT - 1))).astype(jnp.bfloat16)
    total[...] += lax.dot_general(
        lhs[...], match, (((1,), (1,)), ((), ())), preferred_element_type=jnp.float32
    )

    @pl.when(step == pl.num_programs(0) - 1)
    def _():
        for low in range(low_count):
            span = slice(low * HIGH_COUNT, (low + 1) * HIGH_COUNT)
            out_ref[:, span] = base_ref[:, span] + total[low * width : (low + 1) * width, :]


def spread_add(base_t, grads, ids):
    rows = base_t.shape[0]
    base_t = jnp.pad(base_t, ((0, -rows % 16), (0, 0)))
    grads = jnp.pad(grads, ((0, 0), (0, -rows % 16), (0, 0)))
    width, vocab = base_t.shape
    blocks, _, length = ids.shape
    low_count = vocab // HIGH_COUNT
    summed = pl.pallas_call(
        functools.partial(spread_kernel, low_count),
        grid=(blocks,),
        in_specs=[
            pl.BlockSpec((1, 1, length), lambda i: (i, 0, 0)),
            pl.BlockSpec((1, width, length), lambda i: (i, 0, 0)),
            pl.BlockSpec((width, vocab), lambda i: (0, 0)),
        ],
        out_specs=pl.BlockSpec((width, vocab), lambda i: (0, 0)),
        out_shape=jax.ShapeDtypeStruct((width, vocab), jnp.float32),
        scratch_shapes=[
            pltpu.VMEM((low_count * width, length), jnp.bfloat16),
            pltpu.VMEM((low_count * width, HIGH_COUNT), jnp.float32),
        ],
        compiler_params=pltpu.CompilerParams(vmem_limit_bytes=40 * 1024 * 1024),
        cost_estimate=pl.CostEstimate(
            flops=2 * blocks * length * width * vocab,
            bytes_accessed=8 * width * vocab + 2 * blocks * width * length,
            transcendentals=0,
        ),
        name="spread_add",
    )(ids, grads, base_t)
    return summed[:rows]


def split_vectors(vectors_all, width):
    hidden_units = vectors_all.shape[0] - 10 * width
    pieces = []
    offset = 0
    for piece_len in [width] * 9 + [hidden_units, width]:
        pieces.append(vectors_all[offset : offset + piece_len])
        offset = offset + piece_len
    return pieces


def layer_norm(input_batch, gain, shift):
    center = input_batch - jnp.mean(input_batch, axis=-1, keepdims=True)
    spread = jnp.mean(center * center, axis=-1, keepdims=True)
    return center * lax.rsqrt(spread + NORM_EPS) * gain + shift


def norm_back(input_batch, gain, shift, gradient_tree):
    unused, pull = jax.vjp(layer_norm, input_batch, gain, shift)
    return pull(gradient_tree)


def activate(input_batch):
    return jax.nn.gelu(input_batch, approximate=False)


def project(input_batch, weight_matrix):
    return jnp.einsum("ymh,ph->ymp", input_batch, weight_matrix, preferred_element_type=jnp.float32)


def project_back(gradient_tree, weight_matrix):
    return jnp.einsum(
        "faz,zh->fah", gradient_tree, weight_matrix, preferred_element_type=jnp.float32
    )


def weight_grad(gradient_tree, input_batch):
    return jnp.einsum("ebu,ebw->uw", gradient_tree, input_batch, preferred_element_type=jnp.float32)


def column_sum(gradient_tree):
    return jnp.sum(gradient_tree.astype(jnp.float32), axis=(0, 1))


def attend(pieces):
    query, key_rows, value_rows, live_row = pieces
    raw = (
        jnp.einsum("qhe,khe->hqk", query, key_rows, preferred_element_type=jnp.float32)
        * SCORE_SCALE
    )
    scores = jnp.where(live_row[None, None, :], raw, -1e30)
    top = jnp.max(scores, axis=-1, keepdims=True)
    total = jnp.sum(jnp.exp(scores - top), axis=-1, keepdims=True)
    lse = top + jnp.log(total)
    prob = jnp.exp(scores - lse).astype(jnp.bfloat16)
    context = jnp.einsum("hqk,khe->qhe", prob, value_rows, preferred_element_type=jnp.float32)
    return (context, lse)


def attend_back(pieces):
    query, key_rows, value_rows, grad_out, lse, live_row = pieces
    raw = (
        jnp.einsum("qhe,khe->hqk", query, key_rows, preferred_element_type=jnp.float32)
        * SCORE_SCALE
    )
    scores = jnp.where(live_row[None, None, :], raw, -1e30)
    prob = jnp.exp(scores - lse)
    grad_prob = jnp.einsum("qhe,khe->hqk", grad_out, value_rows, preferred_element_type=jnp.float32)
    grad_value = jnp.einsum(
        "hqk,qhe->khe", prob.astype(jnp.bfloat16), grad_out, preferred_element_type=jnp.float32
    )
    grad_score = (prob * (grad_prob - jnp.sum(prob * grad_prob, axis=-1, keepdims=True))).astype(
        jnp.bfloat16
    )
    grad_query = (
        jnp.einsum("hqk,khe->qhe", grad_score, key_rows, preferred_element_type=jnp.float32)
        * SCORE_SCALE
    )
    grad_key = (
        jnp.einsum("hqk,qhe->khe", grad_score, query, preferred_element_type=jnp.float32)
        * SCORE_SCALE
    )
    seq_len = query.shape[0]
    return jnp.concatenate(
        [
            grad_query.reshape(seq_len, -1),
            grad_key.reshape(seq_len, -1),
            grad_value.reshape(seq_len, -1),
        ],
        -1,
    )


def layer_forward(embedded, live, dense_stack, dense_down, parts):
    (
        gain_embed,
        shift_embed,
        gain_attn,
        shift_attn,
        gain_ffn,
        shift_ffn,
        bias_query,
        bias_value,
        bias_out,
        bias_hidden,
        bias_down,
    ) = parts
    seqs, seq_len, width = embedded.shape
    heads = width // HEAD_DIM
    normed = layer_norm(embedded, gain_embed, shift_embed)
    normed_low = normed.astype(jnp.bfloat16)
    qkv_bias = jnp.concatenate([bias_query, jnp.zeros_like(bias_query), bias_value])
    qkv_low = (project(normed_low, dense_stack[: 3 * width]) + qkv_bias).astype(jnp.bfloat16)
    split = qkv_low.reshape(seqs, seq_len, 3, heads, HEAD_DIM)
    context, lse = lax.map(attend, (split[:, :, 0], split[:, :, 1], split[:, :, 2], live))
    context_low = context.reshape(seqs, seq_len, width).astype(jnp.bfloat16)
    first_sum = normed + project(context_low, dense_stack[3 * width : 4 * width]) + bias_out
    first_out = layer_norm(first_sum, gain_attn, shift_attn)
    first_low = first_out.astype(jnp.bfloat16)
    pre_act = project(first_low, dense_stack[4 * width :]) + bias_hidden
    act_low = activate(pre_act).astype(jnp.bfloat16)
    second_sum = first_out + project(act_low, dense_down) + bias_down
    final = layer_norm(second_sum, gain_ffn, shift_ffn)
    saved = (
        embedded,
        normed_low,
        qkv_low,
        lse,
        context_low,
        first_sum,
        first_low,
        pre_act,
        act_low,
        second_sum,
    )
    return (final, saved)


def layer_backward(grad_final, saved, live, dense_stack, dense_down, parts):
    (
        gain_embed,
        shift_embed,
        gain_attn,
        shift_attn,
        gain_ffn,
        shift_ffn,
        bias_query,
        bias_value,
        bias_out,
        bias_hidden,
        bias_down,
    ) = parts
    (
        embedded,
        normed_low,
        qkv_low,
        lse,
        context_low,
        first_sum,
        first_low,
        pre_act,
        act_low,
        second_sum,
    ) = saved
    seqs, seq_len, width = embedded.shape
    heads = width // HEAD_DIM
    grad_second, grad_gain_ffn, grad_shift_ffn = norm_back(
        second_sum, gain_ffn, shift_ffn, grad_final
    )
    grad_down_low = grad_second.astype(jnp.bfloat16)
    down_grad = weight_grad(grad_down_low, act_low)
    grad_act = project_back(grad_down_low, dense_down)
    unused, act_pull = jax.vjp(activate, pre_act)
    grad_pre_low = act_pull(grad_act)[0].astype(jnp.bfloat16)
    hidden_grad = weight_grad(grad_pre_low, first_low)
    grad_first = grad_second + project_back(grad_pre_low, dense_stack[4 * width :])
    grad_first_sum, grad_gain_attn, grad_shift_attn = norm_back(
        first_sum, gain_attn, shift_attn, grad_first
    )
    grad_out_low = grad_first_sum.astype(jnp.bfloat16)
    out_grad = weight_grad(grad_out_low, context_low)
    grad_context_low = project_back(grad_out_low, dense_stack[3 * width : 4 * width]).astype(
        jnp.bfloat16
    )
    split = qkv_low.reshape(seqs, seq_len, 3, heads, HEAD_DIM)
    grad_qkv = lax.map(
        attend_back,
        (
            split[:, :, 0],
            split[:, :, 1],
            split[:, :, 2],
            grad_context_low.reshape(seqs, seq_len, heads, HEAD_DIM),
            lse,
            live,
        ),
    )
    grad_qkv_low = grad_qkv.astype(jnp.bfloat16)
    qkv_grad = weight_grad(grad_qkv_low, normed_low)
    grad_normed = grad_first_sum + project_back(grad_qkv_low, dense_stack[: 3 * width])
    grad_embed, grad_gain_embed, grad_shift_embed = norm_back(
        embedded, gain_embed, shift_embed, grad_normed
    )
    stack_grad = jnp.concatenate([qkv_grad, out_grad, hidden_grad], 0)
    vectors_grad = jnp.concatenate(
        [
            grad_gain_embed,
            grad_shift_embed,
            grad_gain_attn,
            grad_shift_attn,
            grad_gain_ffn,
            grad_shift_ffn,
            column_sum(grad_qkv_low[:, :, :width]),
            column_sum(grad_qkv_low[:, :, 2 * width :]),
            column_sum(grad_out_low),
            column_sum(grad_pre_low),
            column_sum(grad_down_low),
        ]
    )
    return (grad_embed, stack_grad, down_grad, vectors_grad)


def combine_stats(first, second):
    s_top_one, s_total_one, t_top_one, t_total_one, cross_one = first
    s_top_two, s_total_two, t_top_two, t_total_two, cross_two = second
    s_top = jnp.maximum(s_top_one, s_top_two)
    t_top = jnp.maximum(t_top_one, t_top_two)
    s_total = s_total_one * jnp.exp(s_top_one - s_top) + s_total_two * jnp.exp(s_top_two - s_top)
    t_scale_one = jnp.exp(t_top_one - t_top)
    t_scale_two = jnp.exp(t_top_two - t_top)
    t_total = t_total_one * t_scale_one + t_total_two * t_scale_two
    cross = cross_one * t_scale_one + cross_two * t_scale_two
    return (s_top, s_total, t_top, t_total, cross)


def adam(weight_matrix, grad, first, second, rate):
    first = BETA_ONE * first + (1.0 - BETA_ONE) * grad
    second = BETA_TWO * second + (1.0 - BETA_TWO) * grad * grad
    first_hat = first / (1.0 - BETA_ONE**STEP)
    second_hat = second / (1.0 - BETA_TWO**STEP)
    new = weight_matrix - rate * (
        first_hat / (jnp.sqrt(second_hat) + ADAM_EPS) + WEIGHT_DECAY * weight_matrix
    )
    return (first, second, new)


def local(
    token_ids,
    lengths,
    masked_pos,
    teacher,
    stack_index,
    down_index,
    stack_next,
    down_next,
    word_table,
    table_first,
    table_second,
    pos_table,
    pos_first,
    pos_second,
    proj_stack,
    stack_first,
    stack_second,
    ffn_down,
    down_first,
    down_second,
    vectors,
    vectors_first,
    vectors_second,
    head_bias,
    bias_first,
    bias_second_moment,
):
    size = lax.axis_size("fsdp")
    devices = size * lax.axis_size("vocab")
    near = math.gcd(4, size)
    far = size // near
    width = proj_stack.shape[1]
    units = ffn_down.shape[1]
    pair_seqs, seq_len = token_ids.shape
    own_seqs = pair_seqs // 2
    own_rows = own_seqs * seq_len
    core = lax.axis_index("vocab")
    place = lax.axis_index("fsdp")
    p = place % near
    vocab_dev, columns = word_table.shape
    part = vocab_dev // near
    mask_slots = masked_pos.shape[1]
    near_bits = bits_of(near)
    far_bits = [near * bit for bit in bits_of(far)]

    stack_mask = kept(stack_index)
    down_mask = kept(down_index)
    stack_rows = proj_stack.shape[0]
    down_rows = ffn_down.shape[0]
    chunks = units // width
    own_stack = jnp.where(stack_mask, proj_stack, 0.0).astype(jnp.bfloat16)
    own_down = jnp.where(down_mask, ffn_down, 0.0).astype(jnp.bfloat16)
    own_small = jnp.concatenate(
        [pos_table.T.reshape(-1), vectors], 0
    ).astype(jnp.bfloat16)
    small_rows = -(-own_small.shape[0] // (16 * width)) * 16
    own_small = jnp.pad(own_small, (0, small_rows * width - own_small.shape[0]))
    everything = lax.all_gather(
        jnp.concatenate(
            [own_stack]
            + [own_down[:, j * width : (j + 1) * width] for j in range(chunks)]
            + [own_small.reshape(small_rows, width)],
            0,
        ),
        BOTH,
        axis=0,
    )
    dense_stack = everything[:, :stack_rows].reshape(-1, width)
    dense_down = jnp.concatenate(
        [
            everything[:, stack_rows + j * down_rows : stack_rows + (j + 1) * down_rows].reshape(
                -1, width
            )
            for j in range(chunks)
        ],
        1,
    )
    small = everything[:, stack_rows + chunks * down_rows :].reshape(devices, -1)
    pos_count = pos_table.size
    pos_all_t = small[:, :pos_count].reshape(width, seq_len)
    vectors_all = small[:, pos_count : pos_count + vectors.shape[0]].reshape(-1)
    parts = split_vectors(vectors_all.astype(jnp.float32), width)

    table_t = word_table.T
    all_ids = lax.all_to_all(
        jnp.broadcast_to(token_ids[None], (size, pair_seqs, seq_len)), "fsdp", 0, 0, tiled=True
    ).reshape(size, 2, own_seqs, seq_len)
    local_ids = (
        jnp.concatenate(
            [
                lax.dynamic_index_in_dim(all_ids, core, 1, False),
                lax.dynamic_index_in_dim(all_ids, 1 - core, 1, False),
            ],
            0,
        ).reshape(2 * size * own_seqs, 1, seq_len)
        - core * vocab_dev
    )
    half = size * own_seqs
    found = lookup(table_t, local_ids)
    own_found = found[:half] + swap(found[half:], "vocab", 1)
    own_found = own_found.reshape(size, own_seqs, columns, seq_len)
    tokens_t = lax.all_to_all(own_found, "fsdp", 0, 0, tiled=True)
    tokens_t = tokens_t.transpose(1, 0, 2, 3).reshape(own_seqs, width, seq_len)
    embedded = (tokens_t.astype(jnp.float32) + pos_all_t.astype(jnp.float32)[None]).transpose(
        0, 2, 1
    )

    table_low = table_t.astype(jnp.bfloat16)
    blocks = near_exchange(
        lambda q: lax.dynamic_slice_in_dim(table_low, q * part, part, 1), near
    )
    near_table = jnp.zeros((near * columns, part), jnp.bfloat16)
    for k, block in enumerate(blocks):
        near_table = lax.dynamic_update_slice_in_dim(near_table, block, (p ^ k) * columns, 0)
    table_part = far_gather(near_table, near)
    teach = jnp.concatenate(
        near_exchange(lambda q: lax.dynamic_slice_in_dim(teacher, q * part, part, 1), near), 0
    )

    seq_start = place * pair_seqs + core * own_seqs
    own_lengths = lax.dynamic_slice_in_dim(lengths, seq_start, own_seqs)
    live = jnp.arange(seq_len, dtype=jnp.int32)[None, :] < own_lengths[:, None]
    final, saved = layer_forward(embedded, live, dense_stack, dense_down, parts)
    own_pos = lax.dynamic_slice_in_dim(masked_pos, seq_start, own_seqs, 0)
    flat_rows = (jnp.arange(own_seqs, dtype=jnp.int32)[:, None] * seq_len + own_pos).reshape(-1)
    picked = jnp.take(final.reshape(own_rows, width), flat_rows, axis=0).astype(jnp.bfloat16)
    rows = join(picked, "vocab", 1).reshape(-1, width)
    for bit in near_bits:
        rows = jnp.concatenate([rows, swap(rows, "fsdp", bit)], 0)
    rows = rows.reshape(-1, width)

    bias_part = lax.dynamic_slice_in_dim(head_bias, p * part, part)
    output_logits = jnp.dot(rows, table_part, preferred_element_type=jnp.float32) + bias_part
    teach = teach.astype(jnp.float32)
    student_top = jnp.max(output_logits, axis=-1)
    student_total = jnp.sum(jnp.exp(output_logits - student_top[:, None]), axis=-1)
    teacher_top = jnp.max(teach, axis=-1)
    weighted = jnp.exp(teach - teacher_top[:, None])
    teacher_total = jnp.sum(weighted, axis=-1)
    cross = jnp.sum(weighted * (teach - output_logits), axis=-1)
    stats = jnp.stack([student_top, student_total, teacher_top, teacher_total, cross])
    stats = jnp.stack(combine_stats(stats, swap(stats, "vocab", 1)))
    for bit in near_bits:
        other = swap(stats, "fsdp", bit).reshape(5, near, -1)
        other = jnp.concatenate([other[:, k ^ bit] for k in range(near)], 1)
        stats = jnp.stack(combine_stats(stats, other))
    student_top, student_total, teacher_top, teacher_total, cross = stats
    student_lse = student_top + jnp.log(student_total)
    teacher_lse = teacher_top + jnp.log(teacher_total)
    divergence = cross / teacher_total - teacher_lse + student_lse
    group_pos = []
    group_lengths = []
    for k in range(near):
        start = (place ^ k) * pair_seqs
        group_pos.append(lax.dynamic_slice_in_dim(masked_pos, start, pair_seqs, 0))
        group_lengths.append(lax.dynamic_slice_in_dim(lengths, start, pair_seqs))
    group_valid = (
        (jnp.concatenate(group_pos, 0) < jnp.concatenate(group_lengths, 0)[:, None])
        .astype(jnp.float32)
        .reshape(-1)
    )
    count = jnp.sum((masked_pos < lengths[:, None]).astype(jnp.float32))
    group_loss = jnp.sum(divergence * group_valid) / (2 * near)
    scale_rows = (group_valid / count)[:, None]
    grad_logits = (
        (jnp.exp(output_logits - student_lse[:, None]) - jnp.exp(teach - teacher_lse[:, None]))
        * scale_rows
    ).astype(jnp.bfloat16)
    rows_grad = lax.dot_general(
        grad_logits, table_part, (((1,), (1,)), ((), ())), preferred_element_type=jnp.float32
    )
    rows_grad = rows_grad.reshape(near, 2, -1, width).transpose(1, 0, 2, 3)
    rows_grad = halve(rows_grad, "vocab", 1)
    for bit in near_bits[::-1]:
        rows_grad = rows_grad[:bit] + swap(rows_grad[bit:], "fsdp", bit)
    own_rows_grad = rows_grad[0]
    grad_final = (
        jnp.zeros((own_rows, width), jnp.float32)
        .at[flat_rows]
        .add(own_rows_grad)
        .reshape(own_seqs, seq_len, width)
    )

    bias_grad = sum_all(jnp.sum(grad_logits.astype(jnp.float32), axis=0), "fsdp", far_bits)
    for bit in near_bits:
        bias_grad = join(bias_grad, "fsdp", bit).reshape(-1)
    head_grad = lax.dot_general(
        rows, grad_logits, (((0,), (0,)), ((), ())), preferred_element_type=jnp.float32
    )
    head_grad = far_scatter(head_grad.reshape(far, near, columns, part), near)
    blocks = near_exchange(lambda q: lax.dynamic_index_in_dim(head_grad, q, 0, False), near)
    head_grad_t = jnp.zeros((columns, vocab_dev), jnp.float32)
    for k, block in enumerate(blocks):
        head_grad_t = lax.dynamic_update_slice_in_dim(head_grad_t, block, (p ^ k) * part, 1)

    grad_embed, stack_grad, down_grad, vectors_grad = layer_backward(
        grad_final, saved, live, dense_stack, dense_down, parts
    )
    stack_total = lax.psum_scatter(stack_grad, BOTH, scatter_dimension=0, tiled=True)
    down_total = lax.psum_scatter(down_grad, BOTH, scatter_dimension=0, tiled=True)

    embed_t = grad_embed.transpose(0, 2, 1).astype(jnp.bfloat16)
    embed_t = embed_t.reshape(own_seqs, size, columns, seq_len).transpose(1, 0, 2, 3)
    embed_t = lax.all_to_all(embed_t, "fsdp", 0, 0, tiled=True).reshape(half, columns, seq_len)
    embed_t = jnp.concatenate([embed_t, swap(embed_t, "vocab", 1)], 0)
    table_total = spread_add(head_grad_t, embed_t, local_ids)
    pos_total = jnp.sum(embed_t.astype(jnp.float32), axis=0)
    pos_total = lax.dynamic_slice_in_dim(pos_total, core * (columns // 2), columns // 2, 0)

    vectors_grad = sum_all(vectors_grad, "vocab", [1])
    vectors_grad = sum_all(vectors_grad, "fsdp", near_bits + far_bits)
    small_count = vectors.shape[0]
    vectors_total = lax.dynamic_slice_in_dim(
        vectors_grad, (2 * place + core) * small_count, small_count
    )

    stack_total = stack_total + jnp.where(stack_mask, 0.0, PRUNE_DECAY) * proj_stack
    down_total = down_total + jnp.where(down_mask, 0.0, PRUNE_DECAY) * ffn_down
    changes = jnp.sum((stack_mask != kept(stack_next)).astype(jnp.float32)) + jnp.sum(
        (down_mask != kept(down_next)).astype(jnp.float32)
    )
    squares = (
        jnp.sum(stack_total * stack_total)
        + jnp.sum(down_total * down_total)
        + jnp.sum(pos_total * pos_total)
        + jnp.sum(vectors_total * vectors_total)
        + jnp.sum(table_total * table_total)
        + jnp.sum(bias_grad * bias_grad) / size
    )
    scalars = jnp.stack([squares, group_loss, changes])
    scalars = sum_all(scalars, "vocab", [1])
    scalars = sum_all(scalars, "fsdp", near_bits + far_bits)
    total_squares, loss_sum, change_total = scalars[0], scalars[1], scalars[2]
    grad_norm = jnp.sqrt(total_squares)
    factor = jnp.minimum(1.0, CLIP / (grad_norm + 1e-06))
    table_out = adam(table_t, table_total * factor, table_first.T, table_second.T, RATE_MATRIX)
    pos_out = adam(pos_table.T, pos_total * factor, pos_first.T, pos_second.T, RATE_MATRIX)
    stack_out = adam(proj_stack, stack_total * factor, stack_first, stack_second, RATE_MATRIX)
    down_out = adam(ffn_down, down_total * factor, down_first, down_second, RATE_MATRIX)
    vectors_out = adam(vectors, vectors_total * factor, vectors_first, vectors_second, RATE_VECTOR)
    bias_out = adam(head_bias, bias_grad * factor, bias_first, bias_second_moment, RATE_VECTOR)
    return (
        table_out[0].T,
        table_out[1].T,
        table_out[2].T,
        pos_out[0].T,
        pos_out[1].T,
        pos_out[2].T,
        stack_out[0],
        stack_out[1],
        stack_out[2],
        down_out[0],
        down_out[1],
        down_out[2],
        vectors_out[0],
        vectors_out[1],
        vectors_out[2],
        bias_out[0],
        bias_out[1],
        bias_out[2],
        loss_sum,
        count,
        grad_norm,
        change_total.astype(jnp.int32),
    )


def solution(mesh):
    in_specs = (
        P("fsdp", None),
        P(),
        P(),
        P("fsdp", "vocab"),
        P(("fsdp", "vocab"), None),
        P(("fsdp", "vocab"), None),
        P(("fsdp", "vocab"), None),
        P(("fsdp", "vocab"), None),
        P("vocab", "fsdp"),
        P("vocab", "fsdp"),
        P("vocab", "fsdp"),
        P(None, ("fsdp", "vocab")),
        P(None, ("fsdp", "vocab")),
        P(None, ("fsdp", "vocab")),
        P(("fsdp", "vocab"), None),
        P(("fsdp", "vocab"), None),
        P(("fsdp", "vocab"), None),
        P(("fsdp", "vocab"), None),
        P(("fsdp", "vocab"), None),
        P(("fsdp", "vocab"), None),
        P(("fsdp", "vocab")),
        P(("fsdp", "vocab")),
        P(("fsdp", "vocab")),
        P("vocab"),
        P("vocab"),
        P("vocab"),
    )
    out_specs = (
        P("vocab", "fsdp"),
        P("vocab", "fsdp"),
        P("vocab", "fsdp"),
        P(None, ("fsdp", "vocab")),
        P(None, ("fsdp", "vocab")),
        P(None, ("fsdp", "vocab")),
        P(("fsdp", "vocab"), None),
        P(("fsdp", "vocab"), None),
        P(("fsdp", "vocab"), None),
        P(("fsdp", "vocab"), None),
        P(("fsdp", "vocab"), None),
        P(("fsdp", "vocab"), None),
        P(("fsdp", "vocab")),
        P(("fsdp", "vocab")),
        P(("fsdp", "vocab")),
        P("vocab"),
        P("vocab"),
        P("vocab"),
        P(),
        P(),
        P(),
        P(),
    )
    return jax.shard_map(local, mesh=mesh, in_specs=in_specs, out_specs=out_specs, check_vma=False)
```

```python
import functools
import math

import jax
import jax.numpy as jnp
from jax import lax
from jax.experimental import pallas as pl
from jax.experimental.pallas import tpu as pltpu
from jax.sharding import PartitionSpec as P

HEAD_DIM = 64
STEP = 10


NORM_EPS = 1e-05
CLIP = 0.005
PRUNE_DECAY = 0.0002
BETA_ONE = 0.9
BETA_TWO = 0.999
ADAM_EPS = 1e-08
WEIGHT_DECAY = 0.01
RATE_MATRIX = 0.1
RATE_VECTOR = 1.0
SCORE_SCALE = 0.125


HIGH_COUNT = 512
BOTH = ("fsdp", "vocab")


def kept(words):
    columns = words.shape[1] * 16
    place = lax.broadcasted_iota(jnp.int32, (2 * words.shape[1], columns), 0)
    column = lax.broadcasted_iota(jnp.int32, (2 * words.shape[1], columns), 1)
    spread = (place % words.shape[1] * 2 + place // words.shape[1] == column // 8).astype(
        jnp.bfloat16
    )
    bytes_low = jnp.concatenate([words & 255, words >> 8], 1).astype(jnp.bfloat16)
    byte = jnp.dot(bytes_low, spread, preferred_element_type=jnp.float32).astype(jnp.int32)
    spot = lax.broadcasted_iota(jnp.int32, byte.shape, 1)
    nibble = jnp.where(spot % 8 < 4, byte & 15, byte >> 4)
    spot = spot % 4
    return ((nibble & 3) == spot) | ((nibble >> 2) == spot)


def swap(x, axis, bit):
    size = lax.axis_size(axis)
    return lax.ppermute(x, axis, [(i, i ^ bit) for i in range(size)])


def my_bit(axis, bit):
    return lax.axis_index(axis) // bit % 2


def bits_of(size):
    return [1 << k for k in range(size.bit_length() - 1)]


def after(x, *needed):
    if not needed:
        return x
    return lax.optimization_barrier((x, needed))[0]


def tree_sum(parts):
    while len(parts) > 1:
        parts = [one + two for one, two in zip(parts[::2], parts[1::2])]
    return parts[0]


def sum_all(x, near):
    x = x + swap(x, "vocab", 1)
    x = tree_sum(near_exchange(lambda q: x, near))
    return sum_far(x, near)


def sum_far(x, near):
    far = lax.axis_size("fsdp") // near
    if far == 4:
        return tree_sum([x] + [swap(x, "fsdp", k * near) for k in range(1, far)])
    for bit in bits_of(far):
        x = x + swap(x, "fsdp", bit * near)
    return x


def join(x, axis, bit):
    other = swap(x, axis, bit)
    upper = my_bit(axis, bit) == 1
    return jnp.stack([jnp.where(upper, other, x), jnp.where(upper, x, other)])


def halve(x, axis, bit):
    mine = my_bit(axis, bit)
    return lax.dynamic_index_in_dim(x, mine, 0, False) + swap(
        lax.dynamic_index_in_dim(x, 1 - mine, 0, False), axis, bit
    )


def near_exchange(take, near):
    size = lax.axis_size("fsdp")
    p = lax.axis_index("fsdp") % near
    return [take(p)] + [
        lax.ppermute(take(p ^ k), "fsdp", [(i, i ^ k) for i in range(size)]) for k in range(1, near)
    ]


def far_groups(near):
    size = lax.axis_size("fsdp")
    return [list(range(q, size, near)) for q in range(near)]


def near_groups(near):
    size = lax.axis_size("fsdp")
    return [list(range(start, start + near)) for start in range(0, size, near)]


def exchange(x, groups):
    return lax.all_to_all(x, "fsdp", 0, 0, tiled=True, axis_index_groups=groups)


def in_rows(parts, near):
    p = lax.axis_index("fsdp") % near
    rows = parts[0].shape[0]
    stacked = jnp.zeros((near * rows,) + parts[0].shape[1:], parts[0].dtype)
    for k, part in enumerate(parts):
        stacked = lax.dynamic_update_slice_in_dim(stacked, part, (p ^ k) * rows, 0)
    return stacked


def far_gather(x, near):
    return lax.all_gather(x, "fsdp", axis=0, tiled=True, axis_index_groups=far_groups(near))


class FarLine:
    def __init__(self, x, near):
        self.x, self.near = x, near
        self.far = 4
        self.z = lax.axis_index("fsdp") // near
        self.k = 0
        self.up = self.down = None

    def entry(self, j):
        return lax.dynamic_index_in_dim(self.x, jnp.clip(j, 0, self.far - 1), 0, False)

    def step(self, *needed):
        self.k += 1
        k, near, size = self.k, self.near, self.far * self.near
        send_up = self.entry(self.far - k + self.z)
        send_down = self.entry(self.z - self.far + k)
        if k > 1:
            up, down = after([self.up, self.down], *needed)
            send_up, send_down = send_up + up, send_down + down
        sends = [send_up.astype(jnp.bfloat16), send_down.astype(jnp.bfloat16)]
        self.up = lax.ppermute(sends[0], "fsdp", [(i, i + near) for i in range(k * near)])
        self.down = lax.ppermute(
            sends[1], "fsdp", [(i, i - near) for i in range(size - k * near, size)]
        )
        return sends

    def total(self, *needed):
        up, down = after([self.up, self.down], *needed)
        return self.entry(self.z) + up + down


def far_sends(x, near):
    far = lax.axis_size("fsdp") // near
    z = lax.axis_index("fsdp") // near
    sends = [
        lax.dynamic_index_in_dim(x, z ^ k, 0, False).astype(jnp.bfloat16) for k in range(1, far)
    ]
    return lax.dynamic_index_in_dim(x, z, 0, False), sends


def far_arrive(sends, near):
    return [swap(send, "fsdp", k * near) for k, send in enumerate(sends, 1)]


def added(own, parts):
    for part in parts:
        own = own + part.astype(jnp.float32)
    return own


def far_reduce(x, near):
    return lax.psum_scatter(
        x, "fsdp", scatter_dimension=0, tiled=True, axis_index_groups=far_groups(near)
    )[0]


def begin_pair_sum(grad, rows, near):
    core = lax.axis_index("vocab")
    grad = grad.reshape(-1, near, 2, rows, grad.shape[-1])
    send = lax.dynamic_index_in_dim(grad, 1 - core, 2, False).astype(jnp.bfloat16)
    return (lax.dynamic_index_in_dim(grad, core, 2, False), [send])


def in_order(parts, near):
    p = lax.axis_index("fsdp") % near
    stacked = []
    for q in range(near):
        entry = parts[0]
        for k in range(1, near):
            entry = jnp.where(p ^ k == q, parts[k], entry)
        stacked.append(entry)
    return jnp.stack(stacked)


def place_kernel(spans, blocks, order_ref, *refs):
    count = len(refs) - len(spans) - 1
    pieces, outs, sems = refs[:count], refs[count:-1], refs[-1]
    for i, piece in enumerate(pieces):
        for kz in range(blocks):
            n = i * blocks + kz
            block = order_ref[n]
            for m, (first, last, start, rows) in enumerate(spans):

                def copy(m=m, kz=kz, n=n, first=first, start=start, rows=rows, piece=piece):
                    pltpu.make_async_copy(
                        piece.at[kz, pl.ds(start, rows)], outs[m].at[block - first], sems.at[n, m]
                    ).start()

                pl.when((block >= first) & (block < last))(copy)
    for i, piece in enumerate(pieces):
        for kz in range(blocks):
            n = i * blocks + kz
            block = order_ref[n]
            for m, (first, last, start, rows) in enumerate(spans):

                def wait(m=m, kz=kz, n=n, first=first, start=start, rows=rows, piece=piece):
                    pltpu.make_async_copy(
                        piece.at[kz, pl.ds(start, rows)], outs[m].at[block - first], sems.at[n, m]
                    ).wait()

                pl.when((block >= first) & (block < last))(wait)


def gather_pieces(line):
    half = line.shape[0] // 2
    one, two = line[:half], line[half:]
    one_x, two_y = swap(one, "fsdp", 1), swap(two, "fsdp", 2)
    one_y, two_x = swap(one, "fsdp", 2), swap(two, "fsdp", 1)
    one_xy, two_xy = swap(one_x, "fsdp", 2), swap(two_y, "fsdp", 1)
    return [[one, one_x, one_y, one_xy], [two, two_x, two_y, two_xy]]


def place_blocks(pieces, order, spans):
    total, width = len(order), pieces[0].shape[-1]
    return pl.pallas_call(
        functools.partial(place_kernel, spans, pieces[0].shape[0]),
        grid_spec=pltpu.PrefetchScalarGridSpec(
            num_scalar_prefetch=1,
            grid=(1,),
            in_specs=[pl.BlockSpec(memory_space=pltpu.VMEM)] * len(pieces),
            out_specs=[pl.BlockSpec(memory_space=pl.ANY)] * len(spans),
            scratch_shapes=[pltpu.SemaphoreType.DMA((total, len(spans)))],
        ),
        out_shape=[
            jax.ShapeDtypeStruct((last - first, rows, width), pieces[0].dtype)
            for first, last, _, rows in spans
        ],
        compiler_params=pltpu.CompilerParams(vmem_limit_bytes=40 * 1024 * 1024),
        name="place",
    )(jnp.stack(order).astype(jnp.int32), *pieces)


def lookup_kernel(low_count, ids_ref, table_ref, out_ref, spread):
    width = table_ref.shape[0]

    @pl.when(pl.program_id(0) == 0)
    def _():
        for low in range(low_count):
            spread[low * width : (low + 1) * width, :] = table_ref[
                :, low * HIGH_COUNT : (low + 1) * HIGH_COUNT
            ].astype(jnp.bfloat16)

    ids = ids_ref[0]
    low_ids = ids >> 9
    row = lax.broadcasted_iota(jnp.int32, (HIGH_COUNT, ids.shape[1]), 0)
    match = (row == (ids & (HIGH_COUNT - 1))).astype(jnp.bfloat16)
    found = jnp.dot(spread[...], match, preferred_element_type=jnp.float32)
    total = jnp.zeros((width, ids.shape[1]), jnp.float32)
    for low in range(low_count):
        total = jnp.where(low_ids == low, found[low * width : (low + 1) * width, :], total)
    out_ref[0] = total.astype(out_ref.dtype)


def lookup(table_t, ids):
    rows = table_t.shape[0]
    table_t = jnp.pad(table_t, ((0, -rows % 16), (0, 0)))
    width, vocab = table_t.shape
    blocks, _, length = ids.shape
    low_count = vocab // HIGH_COUNT
    found = pl.pallas_call(
        functools.partial(lookup_kernel, low_count),
        grid=(blocks,),
        in_specs=[
            pl.BlockSpec((1, 1, length), lambda i: (i, 0, 0)),
            pl.BlockSpec((width, vocab), lambda i: (0, 0)),
        ],
        out_specs=pl.BlockSpec((1, width, length), lambda i: (i, 0, 0)),
        out_shape=jax.ShapeDtypeStruct((blocks, width, length), jnp.bfloat16),
        scratch_shapes=[pltpu.VMEM((low_count * width, HIGH_COUNT), jnp.bfloat16)],
        compiler_params=pltpu.CompilerParams(vmem_limit_bytes=40 * 1024 * 1024),
        cost_estimate=pl.CostEstimate(
            flops=2 * blocks * length * width * vocab,
            bytes_accessed=4 * width * vocab + 2 * blocks * width * length,
            transcendentals=0,
        ),
        name="lookup",
    )(ids, table_t)
    return found[:, :rows]


def spread_kernel(low_count, ids_ref, grad_ref, out_ref, lhs, total):
    width = grad_ref.shape[1]
    step = pl.program_id(0)

    @pl.when(step == 0)
    def _():
        total[...] = jnp.zeros_like(total)

    ids = ids_ref[0]
    low_ids = ids >> 9
    grad = grad_ref[0].astype(jnp.float32)
    for low in range(low_count):
        lhs[low * width : (low + 1) * width, :] = jnp.where(low_ids == low, grad, 0.0).astype(
            jnp.bfloat16
        )
    row = lax.broadcasted_iota(jnp.int32, (HIGH_COUNT, ids.shape[1]), 0)
    match = (row == (ids & (HIGH_COUNT - 1))).astype(jnp.bfloat16)
    total[...] += lax.dot_general(
        lhs[...], match, (((1,), (1,)), ((), ())), preferred_element_type=jnp.float32
    )

    @pl.when(step == pl.num_programs(0) - 1)
    def _():
        for low in range(low_count):
            span = slice(low * HIGH_COUNT, (low + 1) * HIGH_COUNT)
            out_ref[:, span] = total[low * width : (low + 1) * width, :]


def spread_add(grads, ids, vocab):
    rows = grads.shape[1]
    grads = jnp.pad(grads, ((0, 0), (0, -rows % 16), (0, 0)))
    width = grads.shape[1]
    blocks, _, length = ids.shape
    low_count = vocab // HIGH_COUNT
    summed = pl.pallas_call(
        functools.partial(spread_kernel, low_count),
        grid=(blocks,),
        in_specs=[
            pl.BlockSpec((1, 1, length), lambda i: (i, 0, 0)),
            pl.BlockSpec((1, width, length), lambda i: (i, 0, 0)),
        ],
        out_specs=pl.BlockSpec((width, vocab), lambda i: (0, 0)),
        out_shape=jax.ShapeDtypeStruct((width, vocab), jnp.float32),
        scratch_shapes=[
            pltpu.VMEM((low_count * width, length), jnp.bfloat16),
            pltpu.VMEM((low_count * width, HIGH_COUNT), jnp.float32),
        ],
        compiler_params=pltpu.CompilerParams(vmem_limit_bytes=40 * 1024 * 1024),
        cost_estimate=pl.CostEstimate(
            flops=2 * blocks * length * width * vocab,
            bytes_accessed=4 * width * vocab + 2 * blocks * width * length,
            transcendentals=0,
        ),
        name="spread_add",
    )(ids, grads)
    return summed[:rows]


def split_vectors(vectors_all, width):
    hidden_units = vectors_all.shape[0] - 10 * width
    pieces = []
    offset = 0
    for piece_len in [width] * 9 + [hidden_units, width]:
        pieces.append(vectors_all[offset : offset + piece_len])
        offset = offset + piece_len
    return pieces


def layer_norm(input_batch, gain, shift):
    center = input_batch - jnp.mean(input_batch, axis=-1, keepdims=True)
    spread = jnp.mean(center * center, axis=-1, keepdims=True)
    return center * lax.rsqrt(spread + NORM_EPS) * gain + shift


def norm_back(input_batch, gain, shift, gradient_tree):
    unused, pull = jax.vjp(layer_norm, input_batch, gain, shift)
    return pull(gradient_tree)


def project(input_batch, weight_matrix):
    return jnp.einsum("mh,ph->mp", input_batch, weight_matrix, preferred_element_type=jnp.float32)


def project_back(gradient, weight_matrix):
    return jnp.einsum("az,zh->ah", gradient, weight_matrix, preferred_element_type=jnp.float32)


def weight_grad(gradient, input_batch):
    return jnp.einsum("bu,bw->uw", gradient, input_batch, preferred_element_type=jnp.float32)


def column_sum(gradient):
    return jnp.sum(gradient.astype(jnp.float32), axis=0)


def scores_of(query, key_rows, live):
    raw = lax.dot_general(
        query * SCORE_SCALE, key_rows, (((1,), (1,)), ((), ())), preferred_element_type=jnp.float32
    )
    scores = jnp.where(live, raw, -1e30)
    powers = jnp.exp(scores - jnp.max(scores, axis=-1, keepdims=True))
    return powers * (1.0 / jnp.sum(powers, axis=-1, keepdims=True))


def attend_kernel(lengths_ref, query_ref, key_ref, value_ref, out_ref):
    length = lengths_ref[pl.program_id(0)]
    live = lax.broadcasted_iota(jnp.int32, (1, key_ref.shape[0]), 1) < length
    for start in range(0, query_ref.shape[1], HEAD_DIM):
        span = slice(start, start + HEAD_DIM)
        prob = scores_of(query_ref[:, span], key_ref[:, span], live).astype(jnp.bfloat16)
        context = jnp.dot(prob, value_ref[:, span], preferred_element_type=jnp.float32)
        out_ref[:, span] = context.astype(out_ref.dtype)


def attend(qkv, lengths, seqs):
    rows, total = qkv.shape
    seq_len, width = rows // seqs, total // 3
    lanes = 2 * HEAD_DIM
    blocks = width // lanes

    def part(which):
        return pl.BlockSpec((seq_len, lanes), lambda s, j, _: (s, which * blocks + j))

    return pl.pallas_call(
        attend_kernel,
        grid_spec=pltpu.PrefetchScalarGridSpec(
            num_scalar_prefetch=1,
            grid=(seqs, blocks),
            in_specs=[part(0), part(1), part(2)],
            out_specs=pl.BlockSpec((seq_len, lanes), lambda s, j, _: (s, j)),
        ),
        out_shape=jax.ShapeDtypeStruct((rows, width), jnp.bfloat16),
        compiler_params=pltpu.CompilerParams(vmem_limit_bytes=40 * 1024 * 1024),
        cost_estimate=pl.CostEstimate(
            flops=4 * rows * seq_len * width,
            bytes_accessed=2 * rows * (total + width),
            transcendentals=rows * seq_len * width // HEAD_DIM,
        ),
        name="attend",
    )(lengths, qkv, qkv, qkv)


def attend_back_kernel(lengths_ref, query_ref, key_ref, value_ref, grad_ref, out_ref):
    length = lengths_ref[pl.program_id(0)]
    step = pl.program_id(1)
    width = out_ref.shape[1] // 3
    live = lax.broadcasted_iota(jnp.int32, (1, key_ref.shape[0]), 1) < length
    parts = [[], [], []]
    for start in range(0, query_ref.shape[1], HEAD_DIM):
        span = slice(start, start + HEAD_DIM)
        query, key_rows, value_rows = query_ref[:, span], key_ref[:, span], value_ref[:, span]
        grad_out = grad_ref[:, span]
        prob = scores_of(query, key_rows, live)
        grad_prob = lax.dot_general(
            grad_out, value_rows, (((1,), (1,)), ((), ())), preferred_element_type=jnp.float32
        )
        grad_value = lax.dot_general(
            prob.astype(jnp.bfloat16),
            grad_out,
            (((0,), (0,)), ((), ())),
            preferred_element_type=jnp.float32,
        )
        mean = jnp.sum(prob * grad_prob, axis=-1, keepdims=True)
        grad_score = (prob * (grad_prob - mean)).astype(jnp.bfloat16)
        grad_query = jnp.dot(grad_score, key_rows, preferred_element_type=jnp.float32)
        grad_key = lax.dot_general(
            grad_score, query, (((0,), (0,)), ((), ())), preferred_element_type=jnp.float32
        )
        parts[0].append(grad_query * SCORE_SCALE)
        parts[1].append(grad_key * SCORE_SCALE)
        parts[2].append(grad_value)
    lanes = query_ref.shape[1]
    for which, pieces in enumerate(parts):
        start = pl.multiple_of(which * width + step * lanes, lanes)
        out_ref[:, pl.ds(start, lanes)] = jnp.concatenate(pieces, 1).astype(out_ref.dtype)


def attend_back(qkv, grad_context, lengths, seqs):
    rows, total = qkv.shape
    seq_len, width = rows // seqs, total // 3
    lanes = 2 * HEAD_DIM
    blocks = width // lanes

    def part(which):
        return pl.BlockSpec((seq_len, lanes), lambda s, j, _: (s, which * blocks + j))

    return pl.pallas_call(
        attend_back_kernel,
        grid_spec=pltpu.PrefetchScalarGridSpec(
            num_scalar_prefetch=1,
            grid=(seqs, blocks),
            in_specs=[part(0), part(1), part(2), part(0)],
            out_specs=pl.BlockSpec((seq_len, total), lambda s, j, _: (s, 0)),
        ),
        out_shape=jax.ShapeDtypeStruct((rows, total), jnp.bfloat16),
        compiler_params=pltpu.CompilerParams(vmem_limit_bytes=40 * 1024 * 1024),
        cost_estimate=pl.CostEstimate(
            flops=10 * rows * seq_len * width,
            bytes_accessed=2 * rows * (2 * total + width),
            transcendentals=rows * seq_len * width // HEAD_DIM,
        ),
        name="attend_back",
    )(lengths, qkv, qkv, qkv, grad_context)


def head_kernel(rows_ref, table_ref, bias_ref, teach_ref, logits_ref, stats_ref):
    logits = (
        jnp.dot(rows_ref[...], table_ref[...], preferred_element_type=jnp.float32) + bias_ref[...]
    )
    logits_ref[...] = logits
    teach = teach_ref[...].astype(jnp.float32)
    student_top = jnp.max(logits, axis=-1, keepdims=True)
    student_total = jnp.sum(jnp.exp(logits - student_top), axis=-1, keepdims=True)
    teacher_top = jnp.max(teach, axis=-1, keepdims=True)
    weighted = jnp.exp(teach - teacher_top)
    teacher_total = jnp.sum(weighted, axis=-1, keepdims=True)
    cross = jnp.sum(weighted * (teach - logits), axis=-1, keepdims=True)
    lane = lax.broadcasted_iota(jnp.int32, (logits.shape[0], 128), 1)
    packed = jnp.zeros((logits.shape[0], 128), jnp.float32)
    for i, stat in enumerate((student_top, student_total, teacher_top, teacher_total, cross)):
        packed = jnp.where(lane == i, stat, packed)
    stats_ref[0] = packed.T[:8]


def head(rows, table_part, bias_part, teach, near):
    count, width = rows.shape
    vocab = table_part.shape[1]
    block = count // near
    return pl.pallas_call(
        head_kernel,
        grid=(near,),
        in_specs=[
            pl.BlockSpec((block, width), lambda i: (i, 0)),
            pl.BlockSpec((width, vocab), lambda i: (0, 0)),
            pl.BlockSpec((1, vocab), lambda i: (0, 0)),
            pl.BlockSpec((block, vocab), lambda i: (i, 0)),
        ],
        out_specs=[
            pl.BlockSpec((block, vocab), lambda i: (i, 0)),
            pl.BlockSpec((1, 8, block), lambda i: (i, 0, 0)),
        ],
        out_shape=[
            jax.ShapeDtypeStruct((count, vocab), jnp.float32),
            jax.ShapeDtypeStruct((near, 8, block), jnp.float32),
        ],
        compiler_params=pltpu.CompilerParams(vmem_limit_bytes=48 * 1024 * 1024),
        cost_estimate=pl.CostEstimate(
            flops=2 * count * width * vocab,
            bytes_accessed=count * vocab * 6 + 2 * width * vocab,
            transcendentals=2 * count * vocab,
        ),
        name="head",
    )(rows, table_part, bias_part, teach)


def head_back_kernel(
    logits_ref, teach_ref, stats_ref, scale_ref, table_ref, grad_ref, rows_ref, bias_ref, loss_ref
):
    step = pl.program_id(0)
    stats = stats_ref[:, 0]
    tops, totals, teacher_tops, teacher_totals, crosses = (stats[:, i] for i in range(5))
    top = jnp.max(tops, axis=0, keepdims=True)
    total = jnp.sum(totals * jnp.exp(tops - top), axis=0, keepdims=True)
    teacher_top = jnp.max(teacher_tops, axis=0, keepdims=True)
    teacher_scale = jnp.exp(teacher_tops - teacher_top)
    teacher_total = jnp.sum(teacher_totals * teacher_scale, axis=0, keepdims=True)
    cross = jnp.sum(crosses * teacher_scale, axis=0, keepdims=True)
    student_lse = top + jnp.log(total)
    teacher_lse = teacher_top + jnp.log(teacher_total)
    loss_ref[0] = cross / teacher_total - teacher_lse + student_lse
    packed = jnp.concatenate(
        [student_lse, teacher_lse, scale_ref[0], jnp.zeros((5, top.shape[1]), jnp.float32)], 0
    ).T
    grad = (
        (
            jnp.exp(logits_ref[...] - packed[:, 0:1])
            - jnp.exp(teach_ref[...].astype(jnp.float32) - packed[:, 1:2])
        )
        * packed[:, 2:3]
    ).astype(jnp.bfloat16)
    grad_ref[...] = grad
    rows_ref[...] = lax.dot_general(
        grad, table_ref[...], (((1,), (1,)), ((), ())), preferred_element_type=jnp.float32
    )

    @pl.when(step == 0)
    def _():
        bias_ref[...] = jnp.zeros_like(bias_ref)

    bias_ref[...] += jnp.sum(grad.astype(jnp.float32), axis=0, keepdims=True)


def head_back(logits, teach, stats, scale, table_part, near):
    count, vocab = logits.shape
    width = table_part.shape[0]
    block = count // near
    members = stats.shape[0]
    return pl.pallas_call(
        head_back_kernel,
        grid=(near,),
        in_specs=[
            pl.BlockSpec((block, vocab), lambda i: (i, 0)),
            pl.BlockSpec((block, vocab), lambda i: (i, 0)),
            pl.BlockSpec((members, 1, 8, block), lambda i: (0, i, 0, 0)),
            pl.BlockSpec((1, 1, block), lambda i: (i, 0, 0)),
            pl.BlockSpec((width, vocab), lambda i: (0, 0)),
        ],
        out_specs=[
            pl.BlockSpec((block, vocab), lambda i: (i, 0)),
            pl.BlockSpec((block, width), lambda i: (i, 0)),
            pl.BlockSpec((1, vocab), lambda i: (0, 0)),
            pl.BlockSpec((1, 1, block), lambda i: (i, 0, 0)),
        ],
        out_shape=[
            jax.ShapeDtypeStruct((count, vocab), jnp.bfloat16),
            jax.ShapeDtypeStruct((count, width), jnp.float32),
            jax.ShapeDtypeStruct((1, vocab), jnp.float32),
            jax.ShapeDtypeStruct((near, 1, block), jnp.float32),
        ],
        compiler_params=pltpu.CompilerParams(vmem_limit_bytes=48 * 1024 * 1024),
        cost_estimate=pl.CostEstimate(
            flops=2 * count * width * vocab,
            bytes_accessed=count * vocab * 8 + 2 * width * vocab,
            transcendentals=2 * count * vocab,
        ),
        name="head_back",
    )(logits, teach, stats, scale, table_part)


def layer_forward(
    embedded, lengths, seqs, weight_qkv, weight_out, weight_up, weight_down_after, parts
):
    (
        gain_embed,
        shift_embed,
        gain_attn,
        shift_attn,
        gain_ffn,
        shift_ffn,
        bias_query,
        bias_value,
        bias_out,
        bias_hidden,
        bias_down,
    ) = parts
    normed = layer_norm(embedded, gain_embed, shift_embed)
    normed_low = normed.astype(jnp.bfloat16)
    qkv_bias = jnp.concatenate([bias_query, jnp.zeros_like(bias_query), bias_value])
    qkv_low = (project(normed_low, weight_qkv) + qkv_bias).astype(jnp.bfloat16)
    context_low = attend(qkv_low, lengths, seqs)
    first_sum = normed + project(context_low, weight_out) + bias_out
    first_out = layer_norm(first_sum, gain_attn, shift_attn)
    first_low = first_out.astype(jnp.bfloat16)
    pre_act = project(first_low, weight_up) + bias_hidden
    share = 0.5 + 0.5 * lax.erf(pre_act * math.sqrt(0.5))
    act_low = (pre_act * share).astype(jnp.bfloat16)
    weight_down = weight_down_after(first_low)
    slope = share + pre_act * jnp.exp(-0.5 * pre_act * pre_act) * (1.0 / math.sqrt(2.0 * math.pi))
    second_sum = first_out + project(act_low, weight_down) + bias_down
    final = layer_norm(second_sum, gain_ffn, shift_ffn)
    saved = (
        embedded,
        normed_low,
        qkv_low,
        context_low,
        first_sum,
        first_low,
        slope,
        act_low,
        second_sum,
    )
    return (final, saved, weight_down)


def layer_backward(
    grad_final,
    saved,
    lengths,
    seqs,
    weight_qkv,
    weight_out,
    weight_up,
    weight_down,
    parts,
    sums,
    line,
    embed_columns,
    stack_rows,
    down_rows,
):
    (
        gain_embed,
        shift_embed,
        gain_attn,
        shift_attn,
        gain_ffn,
        shift_ffn,
        bias_query,
        bias_value,
        bias_out,
        bias_hidden,
        bias_down,
    ) = parts
    (
        embedded,
        normed_low,
        qkv_low,
        context_low,
        first_sum,
        first_low,
        slope,
        act_low,
        second_sum,
    ) = saved
    width = embedded.shape[1]
    grad_second, grad_gain_ffn, grad_shift_ffn = norm_back(
        second_sum, gain_ffn, shift_ffn, grad_final
    )
    grad_down_low = grad_second.astype(jnp.bfloat16)
    sums.begin("down", weight_grad(grad_down_low, act_low), down_rows)
    grad_pre_low = (
        project_back(after(grad_down_low, *sums.sent("down")), weight_down) * slope
    ).astype(jnp.bfloat16)
    grad_pre_low = lax.optimization_barrier(grad_pre_low)
    sums.begin("up", weight_grad(grad_pre_low, first_low), stack_rows)
    grad_first = grad_second + project_back(after(grad_pre_low, *sums.sent("up")), weight_up)
    grad_first_sum, grad_gain_attn, grad_shift_attn = norm_back(
        first_sum, gain_attn, shift_attn, grad_first
    )
    grad_out_low = grad_first_sum.astype(jnp.bfloat16)
    grad_context_low = project_back(grad_out_low, weight_out).astype(jnp.bfloat16)
    out_grad = weight_grad(grad_out_low, context_low)
    sums.in_plane(("down", "up"), grad_context_low)
    line_sends = line.step(grad_context_low) if line else []
    grad_qkv_low = attend_back(
        qkv_low, after(grad_context_low, *sums.sent("up"), *line_sends), lengths, seqs
    )
    grad_normed = grad_first_sum + project_back(grad_qkv_low, weight_qkv)
    grad_embed, grad_gain_embed, grad_shift_embed = norm_back(
        embedded, gain_embed, shift_embed, grad_normed
    )
    embed_t = embed_columns(grad_embed)
    line_sends = line.step(embed_t) if line else []
    qkv_grad = weight_grad(after(grad_qkv_low, embed_t, *line_sends), normed_low)
    sums.begin("attention", jnp.concatenate([qkv_grad, out_grad], 0), stack_rows)
    vectors_grad = jnp.concatenate(
        [
            grad_gain_embed,
            grad_shift_embed,
            grad_gain_attn,
            grad_shift_attn,
            grad_gain_ffn,
            grad_shift_ffn,
            column_sum(grad_qkv_low[:, :width]),
            column_sum(grad_qkv_low[:, 2 * width :]),
            column_sum(grad_out_low),
            column_sum(grad_pre_low),
            column_sum(grad_down_low),
        ]
    )
    return (embed_t, vectors_grad)


class WeightSums:
    def __init__(self, near, far, width):
        self.near, self.staged, self.width = near, far == 4, width
        self.state = {}

    def begin(self, name, grad, rows):
        self.state[name] = begin_pair_sum(grad, rows, self.near) if self.staged else (grad, [])

    def sent(self, name):
        return self.state[name][1] if self.staged else []

    def narrow(self, x):
        parts = [
            x[..., j : j + self.width] for j in range(0, x.shape[-1], self.width)
        ]
        return parts[0] if len(parts) == 1 else jnp.concatenate(parts, -2)

    def in_plane(self, names, *needed):
        if not self.staged:
            return
        p = lax.axis_index("fsdp") % self.near
        owns, sends = [], [[] for _ in range(1, self.near)]
        for name in names:
            keep, pair_sends = self.state[name]
            arrived = after(swap(pair_sends[0], "vocab", 1), *needed)
            keep = keep + arrived.astype(jnp.float32)
            owns.append(self.narrow(lax.dynamic_index_in_dim(keep, p, 1, False)))
            for k in range(1, self.near):
                send = lax.dynamic_index_in_dim(keep, p ^ k, 1, False).astype(jnp.bfloat16)
                sends[k - 1].append(self.narrow(send).reshape(-1, self.width))
        sends = [parts[0] if len(parts) == 1 else jnp.concatenate(parts, 0) for parts in sends]
        for name, own in zip(names, owns):
            self.state[name] = (own, sends)

    def plane_totals(self, names, *needed):
        sends = self.state[names[0]][1]
        arrived = after([swap(send, "fsdp", k) for k, send in enumerate(sends, 1)], *needed)
        totals, start = [], 0
        for name in names:
            own = self.state[name][0]
            count = own.shape[0] * own.shape[1]
            totals.append(
                added(own, [part[start : start + count].reshape(own.shape) for part in arrived])
            )
            start += count
        return totals


def adam(weight_matrix, grad, first, second, rate):
    first = BETA_ONE * first + (1.0 - BETA_ONE) * grad
    second = BETA_TWO * second + (1.0 - BETA_TWO) * grad * grad
    first_hat = first / (1.0 - BETA_ONE**STEP)
    second_hat = second / (1.0 - BETA_TWO**STEP)
    new = weight_matrix - rate * (
        first_hat / (jnp.sqrt(second_hat) + ADAM_EPS) + WEIGHT_DECAY * weight_matrix
    )
    return (first, second, new)


def local(
    token_ids,
    lengths,
    masked_pos,
    teacher,
    stack_index,
    down_index,
    stack_next,
    down_next,
    word_table,
    table_first,
    table_second,
    pos_table,
    pos_first,
    pos_second,
    proj_stack,
    stack_first,
    stack_second,
    ffn_down,
    down_first,
    down_second,
    vectors,
    vectors_first,
    vectors_second,
    head_bias,
    bias_first,
    bias_second_moment,
):
    size = lax.axis_size("fsdp")
    near = math.gcd(4, size)
    far = size // near
    width = proj_stack.shape[1]
    units = ffn_down.shape[1]
    pair_seqs, seq_len = token_ids.shape
    own_seqs = pair_seqs // 2
    own_rows = own_seqs * seq_len
    core = lax.axis_index("vocab")
    place = lax.axis_index("fsdp")
    p = place % near
    vocab_dev, columns = word_table.shape
    part = vocab_dev // near
    mask_slots = masked_pos.shape[1]

    table_t = word_table.T
    all_ids = lax.all_to_all(
        jnp.broadcast_to(token_ids[None], (size, pair_seqs, seq_len)), "fsdp", 0, 0, tiled=True
    ).reshape(size, 2, own_seqs, seq_len)
    local_ids = (
        jnp.concatenate(
            [
                lax.dynamic_index_in_dim(all_ids, core, 1, False),
                lax.dynamic_index_in_dim(all_ids, 1 - core, 1, False),
            ],
            0,
        ).reshape(2 * size * own_seqs, 1, seq_len)
        - core * vocab_dev
    )

    stack_mask = kept(stack_index)
    down_mask = kept(down_index)
    stack_rows = proj_stack.shape[0]
    down_rows = ffn_down.shape[0]
    small_count = vectors.shape[0]
    own_stack = jnp.where(stack_mask, proj_stack, 0.0).astype(jnp.bfloat16)
    own_down = jnp.where(down_mask, ffn_down, 0.0).astype(jnp.bfloat16)
    pos_rows = -(-(columns // 2) // 16) * 16
    own_stack = jnp.concatenate(
        [
            own_stack,
            jnp.pad(
                pos_table.T.astype(jnp.bfloat16),
                ((0, pos_rows - columns // 2), (0, width - seq_len)),
            ),
            jnp.pad(
                vectors.astype(jnp.bfloat16)[None], ((0, 15), (0, width - small_count))
            ),
        ],
        0,
    )
    table_low = table_t.astype(jnp.bfloat16)
    half = size * own_seqs
    table_blocks = table_low.reshape(columns, near, part).transpose(1, 0, 2)
    def teacher_parts(*needed):
        given = after(teacher, *needed)
        return near_exchange(lambda q: lax.dynamic_slice_in_dim(given, q * part, part, 1), near)

    if far == 4:
        own_stack = after(own_stack, all_ids)
        stack_line = [swap(own_stack, "fsdp", k * near) for k in range(1, far)]
        near_table = exchange(after(table_blocks, all_ids), near_groups(near))
        found = lookup(table_t, after(local_ids, own_stack))
        near_table = after(near_table, found).reshape(near * columns, part)
        own_found = found[:half] + swap(found[half:], "vocab", 1)
        stack_line = jnp.stack([own_stack] + after(stack_line, found))
        stack_pieces = gather_pieces(stack_line)
        own_found = after(own_found, stack_line, near_table)
        tokens_t = exchange(own_found.reshape(size, own_seqs, columns, seq_len), None)
        own_down = after(own_down, own_found)
        down_line = exchange(
            after(jnp.broadcast_to(own_down[None], (far,) + own_down.shape), tokens_t),
            far_groups(near),
        )
        stack_others = [[swap(piece, "vocab", 1) for piece in half] for half in stack_pieces]
        own_blocks = exchange(
            after(
                jnp.broadcast_to(down_line[None], (near,) + down_line.shape),
                stack_pieces[0][3],
                stack_pieces[1][3],
            ),
            near_groups(near),
        )
        other_blocks = swap(own_blocks, "vocab", 1)
        teach_parts = teacher_parts(stack_pieces[0][3], stack_pieces[1][3])
        qkv_blocks = 3 * width // stack_rows
        attention_blocks = 4 * width // stack_rows
        weight_qkv, weight_out, weight_up, small = place_blocks(
            [piece for group in (stack_pieces, stack_others) for half in group for piece in half],
            [
                (place ^ ((first + kz) * near + kp)) * 2 + (core ^ kc)
                for kc in range(2)
                for first in (0, far // 2)
                for kp in range(near)
                for kz in range(far // 2)
            ],
            (
                (0, qkv_blocks, 0, stack_rows),
                (qkv_blocks, attention_blocks, 0, stack_rows),
                (attention_blocks, 2 * size, 0, stack_rows),
                (0, 2 * size, stack_rows, pos_rows + 16),
            ),
        )
        weight_qkv = weight_qkv.reshape(-1, width)
        weight_out = weight_out.reshape(-1, width)
        weight_up = weight_up.reshape(-1, width)

        def weight_down_after(*needed):
            arrived = after([own_blocks, other_blocks], *needed)
            (weight_down,) = place_blocks(
                [blocks.reshape((size,) + own_down.shape) for blocks in arrived],
                [
                    (kz * near + kp) * 2 + (core ^ kc)
                    for kc in range(2)
                    for kp in range(near)
                    for kz in range(far)
                ],
                ((0, 2 * size, 0, down_rows),),
            )
            return weight_down.reshape(-1, units)

    else:
        teach_parts = teacher_parts()
        stack_all = lax.all_gather(own_stack, BOTH, axis=0)
        dense_stack = stack_all[:, :stack_rows].reshape(-1, width)
        small = stack_all[:, stack_rows:]
        weight_qkv = dense_stack[: 3 * width]
        weight_out = dense_stack[3 * width : 4 * width]
        weight_up = dense_stack[4 * width :]
        weight_down = lax.all_gather(own_down, BOTH, axis=0, tiled=True)

        def weight_down_after(*needed):
            return weight_down

        near_table = exchange(table_blocks, near_groups(near)).reshape(near * columns, part)
        found = lookup(table_t, local_ids)
        own_found = found[:half] + swap(found[half:], "vocab", 1)
        tokens_t = exchange(own_found.reshape(size, own_seqs, columns, seq_len), None)
    pos_all_t = small[:, : columns // 2, :seq_len].reshape(width, seq_len)
    vectors_all = small[:, pos_rows, :small_count].reshape(-1)
    parts = split_vectors(vectors_all.astype(jnp.float32), width)

    table_part = far_gather(near_table, near)
    tokens_t = tokens_t.transpose(1, 0, 2, 3).reshape(own_seqs, width, seq_len)
    embedded = (
        tokens_t.transpose(0, 2, 1).astype(jnp.float32)
        + pos_all_t.T.astype(jnp.float32)[None]
    ).reshape(own_rows, width)

    seq_start = place * pair_seqs + core * own_seqs
    own_lengths = lax.dynamic_slice_in_dim(lengths, seq_start, own_seqs)
    final, saved, weight_down = layer_forward(
        embedded, own_lengths, own_seqs, weight_qkv, weight_out, weight_up, weight_down_after, parts
    )
    teach = in_rows(teach_parts, near)
    own_pos = lax.dynamic_slice_in_dim(masked_pos, seq_start, own_seqs, 0)
    flat_rows = (jnp.arange(own_seqs, dtype=jnp.int32)[:, None] * seq_len + own_pos).reshape(-1)
    picked = jnp.take(final.reshape(own_rows, width), flat_rows, axis=0).astype(jnp.bfloat16)
    rows = join(picked, "vocab", 1).reshape(-1, width)
    rows = in_order(near_exchange(lambda q: rows, near), near).reshape(-1, width)

    bias_part = lax.dynamic_slice_in_dim(head_bias, p * part, part)
    output_logits, stats = head(rows, table_part, bias_part[None], teach, near)
    stats = jnp.stack(
        [stats]
        + [
            lax.ppermute(stats, BOTH, [(i, i ^ k) for i in range(2 * size)])
            for k in range(1, 2 * near)
        ]
    )
    group_start = (place - p) * pair_seqs
    group_pos = lax.dynamic_slice_in_dim(masked_pos, group_start, near * pair_seqs, 0)
    group_lengths = lax.dynamic_slice_in_dim(lengths, group_start, near * pair_seqs)
    group_valid = (group_pos < group_lengths[:, None]).astype(jnp.float32).reshape(near, 1, -1)
    count = jnp.sum((masked_pos < lengths[:, None]).astype(jnp.float32))
    grad_logits, rows_grad, bias_part_grad, divergence = head_back(
        output_logits, teach, stats, group_valid / count, table_part, near
    )
    group_loss = jnp.sum(divergence * group_valid) / (2 * near)
    rows_grad = halve(rows_grad.reshape(near, 2, -1, width).transpose(1, 0, 2, 3), "vocab", 1)
    rows_sends = [lax.dynamic_index_in_dim(rows_grad, p ^ k, 0, False) for k in range(near)]
    own_rows_grad = tree_sum(
        [rows_sends[0]] + [swap(send, "fsdp", k) for k, send in enumerate(rows_sends[1:], 1)]
    )
    grad_final = (
        jnp.zeros((own_rows, width), jnp.float32)
        .at[flat_rows]
        .add(own_rows_grad)
    )

    bias_part_grad = sum_far(after(bias_part_grad[0], *rows_sends), near)
    bias_grad = in_order(near_exchange(lambda q: bias_part_grad, near), near).reshape(-1)
    head_grad = lax.dot_general(
        rows,
        after(grad_logits, *rows_sends),
        (((0,), (0,)), ((), ())),
        preferred_element_type=jnp.float32,
    ).reshape(far, near, columns, part)
    if far == 4:
        line = FarLine(after(head_grad, bias_grad), near)
        grad_final = after(grad_final, *line.step())
    else:
        line = None

    def embed_columns(grad_embed):
        embed_t = grad_embed.reshape(own_seqs, seq_len, width).astype(jnp.bfloat16)
        embed_t = embed_t.transpose(0, 2, 1).reshape(own_seqs, size, columns, seq_len)
        return embed_t.transpose(1, 0, 2, 3)

    sums = WeightSums(near, far, width)
    embed_t, vectors_grad = layer_backward(
        grad_final,
        saved,
        own_lengths,
        own_seqs,
        weight_qkv,
        weight_out,
        weight_up,
        weight_down,
        parts,
        sums,
        line,
        embed_columns,
        stack_rows,
        down_rows,
    )

    embed_t = lax.all_to_all(embed_t, "fsdp", 0, 0, tiled=True).reshape(half, columns, seq_len)
    if far == 4:
        down_plane, up_plane = sums.plane_totals(("down", "up"), *sums.sent("attention"))
        sums.in_plane(("attention",), up_plane)
        attention_sends = sums.sent("attention")
        embed_t = after(embed_t, *attention_sends)
        other_t = swap(embed_t, "vocab", 1)
        vectors_grad = vectors_grad + swap(after(vectors_grad, *attention_sends), "vocab", 1)
        head_grad = line.total(*attention_sends)
        blocks = near_exchange(lambda q: lax.dynamic_index_in_dim(head_grad, q, 0, False), near)
        token_grad = spread_add(after(embed_t, head_grad, other_t), local_ids[:half], vocab_dev)
        (attention_plane,) = sums.plane_totals(("attention",), token_grad)
        own = jnp.concatenate(
            [jnp.concatenate([attention_plane, up_plane], 0), down_plane], 1
        )
        far_low = own.astype(jnp.bfloat16)
        arrived = exchange(far_low, far_groups(near))
        token_grad = token_grad + spread_add(
            after(other_t, far_low), local_ids[half:], vocab_dev
        )
        vectors_grad = tree_sum(near_exchange(lambda q: after(vectors_grad, far_low), near))
        vectors_far = [swap(vectors_grad, "fsdp", k * near) for k in range(1, far)]
        vectors_grad = tree_sum([vectors_grad] + after(vectors_far, token_grad))
        z = place // near
        other = lax.broadcasted_iota(jnp.int32, (far, 1, 1), 0) != z
        total = jnp.sum(jnp.where(other, arrived.astype(jnp.float32), own), axis=0)
        stack_total = total[:stack_rows]
        down_total = jnp.concatenate(
            jnp.split(total[stack_rows:], units // width, axis=0), 1
        )
        embed_t = jnp.concatenate([embed_t, other_t], 0)
    else:
        embed_t = jnp.concatenate([embed_t, swap(embed_t, "vocab", 1)], 0)
        token_grad = spread_add(embed_t, local_ids, vocab_dev)
        vectors_grad = sum_all(vectors_grad, near)
        head_grad = far_reduce(head_grad, near)
        blocks = near_exchange(lambda q: lax.dynamic_index_in_dim(head_grad, q, 0, False), near)
        stack_grad = [sums.state[name][0] for name in ("attention", "up")]
        stack_total = lax.psum_scatter(
            jnp.concatenate(stack_grad, 0), BOTH, scatter_dimension=0, tiled=True
        )
        down_total = lax.psum_scatter(
            sums.state["down"][0], BOTH, scatter_dimension=0, tiled=True
        )
    head_grad_t = jnp.concatenate(list(in_order(blocks, near)), 1).astype(jnp.float32)
    table_total = head_grad_t + token_grad
    pos_total = jnp.sum(embed_t.astype(jnp.float32), axis=0)
    pos_total = lax.dynamic_slice_in_dim(pos_total, core * (columns // 2), columns // 2, 0)
    vectors_total = lax.dynamic_slice_in_dim(
        vectors_grad, (2 * place + core) * small_count, small_count
    )

    stack_total = stack_total + jnp.where(stack_mask, 0.0, PRUNE_DECAY) * proj_stack
    down_total = down_total + jnp.where(down_mask, 0.0, PRUNE_DECAY) * ffn_down
    changes = jnp.sum((stack_mask != kept(stack_next)).astype(jnp.float32)) + jnp.sum(
        (down_mask != kept(down_next)).astype(jnp.float32)
    )
    squares = (
        jnp.sum(stack_total * stack_total)
        + jnp.sum(down_total * down_total)
        + jnp.sum(pos_total * pos_total)
        + jnp.sum(vectors_total * vectors_total)
        + jnp.sum(table_total * table_total)
        + jnp.sum(bias_grad * bias_grad) / size
    )
    scalars = jnp.stack([squares, group_loss, changes])
    scalars = sum_all(scalars, near)
    total_squares, loss_sum, change_total = scalars[0], scalars[1], scalars[2]
    grad_norm = jnp.sqrt(total_squares)
    factor = jnp.minimum(1.0, CLIP / (grad_norm + 1e-06))
    table_out = adam(table_t, table_total * factor, table_first.T, table_second.T, RATE_MATRIX)
    pos_out = adam(pos_table.T, pos_total * factor, pos_first.T, pos_second.T, RATE_MATRIX)
    stack_out = adam(proj_stack, stack_total * factor, stack_first, stack_second, RATE_MATRIX)
    down_out = adam(ffn_down, down_total * factor, down_first, down_second, RATE_MATRIX)
    vectors_out = adam(vectors, vectors_total * factor, vectors_first, vectors_second, RATE_VECTOR)
    bias_out = adam(head_bias, bias_grad * factor, bias_first, bias_second_moment, RATE_VECTOR)
    return (
        table_out[0].T,
        table_out[1].T,
        table_out[2].T,
        pos_out[0].T,
        pos_out[1].T,
        pos_out[2].T,
        stack_out[0],
        stack_out[1],
        stack_out[2],
        down_out[0],
        down_out[1],
        down_out[2],
        vectors_out[0],
        vectors_out[1],
        vectors_out[2],
        bias_out[0],
        bias_out[1],
        bias_out[2],
        loss_sum,
        count,
        grad_norm,
        change_total.astype(jnp.int32),
    )


def solution(mesh):
    in_specs = (
        P("fsdp", None),
        P(),
        P(),
        P("fsdp", "vocab"),
        P(("fsdp", "vocab"), None),
        P(("fsdp", "vocab"), None),
        P(("fsdp", "vocab"), None),
        P(("fsdp", "vocab"), None),
        P("vocab", "fsdp"),
        P("vocab", "fsdp"),
        P("vocab", "fsdp"),
        P(None, ("fsdp", "vocab")),
        P(None, ("fsdp", "vocab")),
        P(None, ("fsdp", "vocab")),
        P(("fsdp", "vocab"), None),
        P(("fsdp", "vocab"), None),
        P(("fsdp", "vocab"), None),
        P(("fsdp", "vocab"), None),
        P(("fsdp", "vocab"), None),
        P(("fsdp", "vocab"), None),
        P(("fsdp", "vocab")),
        P(("fsdp", "vocab")),
        P(("fsdp", "vocab")),
        P("vocab"),
        P("vocab"),
        P("vocab"),
    )
    out_specs = (
        P("vocab", "fsdp"),
        P("vocab", "fsdp"),
        P("vocab", "fsdp"),
        P(None, ("fsdp", "vocab")),
        P(None, ("fsdp", "vocab")),
        P(None, ("fsdp", "vocab")),
        P(("fsdp", "vocab"), None),
        P(("fsdp", "vocab"), None),
        P(("fsdp", "vocab"), None),
        P(("fsdp", "vocab"), None),
        P(("fsdp", "vocab"), None),
        P(("fsdp", "vocab"), None),
        P(("fsdp", "vocab")),
        P(("fsdp", "vocab")),
        P(("fsdp", "vocab")),
        P("vocab"),
        P("vocab"),
        P("vocab"),
        P(),
        P(),
        P(),
        P(),
    )
    return jax.shard_map(local, mesh=mesh, in_specs=in_specs, out_specs=out_specs, check_vma=False)
```

```python
import functools
import math

import jax
import jax.numpy as jnp
from jax import lax
from jax.experimental import pallas as pl
from jax.experimental.pallas import tpu as pltpu
from jax.sharding import PartitionSpec as P

HEAD_DIM = 64
STEP = 10


NORM_EPS = 1e-05
CLIP = 0.005
PRUNE_DECAY = 0.0002
BETA_ONE = 0.9
BETA_TWO = 0.999
ADAM_EPS = 1e-08
WEIGHT_DECAY = 0.01
RATE_MATRIX = 0.1
RATE_VECTOR = 1.0
SCORE_SCALE = 0.125


HIGH_COUNT = 512
COST = pl.CostEstimate(flops=1, bytes_accessed=1, transcendentals=0)
BOTH = ("fsdp", "vocab")


def kept(words):
    columns = words.shape[1] * 16
    place = lax.broadcasted_iota(jnp.int32, (2 * words.shape[1], columns), 0)
    column = lax.broadcasted_iota(jnp.int32, (2 * words.shape[1], columns), 1)
    spread = (place % words.shape[1] * 2 + place // words.shape[1] == column // 8).astype(
        jnp.bfloat16
    )
    bytes_low = jnp.concatenate([words & 255, words >> 8], 1).astype(jnp.bfloat16)
    byte = jnp.dot(bytes_low, spread, preferred_element_type=jnp.float32).astype(jnp.int32)
    spot = lax.broadcasted_iota(jnp.int32, byte.shape, 1)
    nibble = jnp.where(spot % 8 < 4, byte & 15, byte >> 4)
    spot = spot % 4
    return ((nibble & 3) == spot) | ((nibble >> 2) == spot)


def swap(x, axis, bit):
    size = lax.axis_size(axis)
    return lax.ppermute(x, axis, [(i, i ^ bit) for i in range(size)])


def my_bit(axis, bit):
    return lax.axis_index(axis) // bit % 2


def bits_of(size):
    return [1 << k for k in range(size.bit_length() - 1)]


def gate_kernel(*refs):
    pass


def after(x, *needed):
    if not needed:
        return x
    parts = x if isinstance(x, list) else [x]
    anywhere = pl.BlockSpec(memory_space=pl.ANY)
    outs = pl.pallas_call(
        gate_kernel,
        in_specs=[anywhere] * (len(parts) + len(needed)),
        out_specs=[anywhere] * len(parts),
        out_shape=[jax.ShapeDtypeStruct(part.shape, part.dtype) for part in parts],
        input_output_aliases={i: i for i in range(len(parts))},
        name="gate",
    )(*parts, *needed)
    return list(outs) if isinstance(x, list) else outs[0]


def tree_sum(parts):
    while len(parts) > 1:
        parts = [one + two for one, two in zip(parts[::2], parts[1::2])]
    return parts[0]


def sum_all(x, near):
    x = x + swap(x, "vocab", 1)
    x = tree_sum(near_exchange(lambda q: x, near))
    return sum_far(x, near)


def sum_far(x, near):
    far = lax.axis_size("fsdp") // near
    if far == 4:
        return tree_sum([x] + [swap(x, "fsdp", k * near) for k in range(1, far)])
    for bit in bits_of(far):
        x = x + swap(x, "fsdp", bit * near)
    return x


def join(x, axis, bit):
    other = swap(x, axis, bit)
    upper = my_bit(axis, bit) == 1
    return jnp.stack([jnp.where(upper, other, x), jnp.where(upper, x, other)])


def halve(x, axis, bit):
    mine = my_bit(axis, bit)
    return lax.dynamic_index_in_dim(x, mine, 0, False) + swap(
        lax.dynamic_index_in_dim(x, 1 - mine, 0, False), axis, bit
    )


def near_exchange(take, near):
    size = lax.axis_size("fsdp")
    p = lax.axis_index("fsdp") % near
    return [take(p)] + [
        lax.ppermute(take(p ^ k), "fsdp", [(i, i ^ k) for i in range(size)]) for k in range(1, near)
    ]


def far_groups(near):
    size = lax.axis_size("fsdp")
    return [list(range(q, size, near)) for q in range(near)]


def near_groups(near):
    size = lax.axis_size("fsdp")
    return [list(range(start, start + near)) for start in range(0, size, near)]


def exchange(x, groups):
    return lax.all_to_all(x, "fsdp", 0, 0, tiled=True, axis_index_groups=groups)


def far_gather(x, near):
    return lax.all_gather(x, "fsdp", axis=0, tiled=True, axis_index_groups=far_groups(near))


class FarLine:
    def __init__(self, x, near):
        self.x, self.near = x, near
        self.far = 4
        self.z = lax.axis_index("fsdp") // near
        self.k = 0
        self.up = self.down = None

    def entry(self, j):
        return lax.dynamic_index_in_dim(self.x, jnp.clip(j, 0, self.far - 1), 0, False)

    def arrived(self):
        return [self.up, self.down]

    def step(self, *needed):
        self.k += 1
        k, near, size = self.k, self.near, self.far * self.near
        send_up = self.entry(self.far - k + self.z)
        send_down = self.entry(self.z - self.far + k)
        if k > 1:
            up, down = after([self.up, self.down], *needed) if needed else (self.up, self.down)
            send_up, send_down = send_up + up, send_down + down
        sends = [send_up.astype(jnp.bfloat16), send_down.astype(jnp.bfloat16)]
        self.up = lax.ppermute(sends[0], "fsdp", [(i, i + near) for i in range(k * near)])
        self.down = lax.ppermute(
            sends[1], "fsdp", [(i, i - near) for i in range(size - k * near, size)]
        )
        return sends

    def total(self, *needed):
        up, down = after([self.up, self.down], *needed)
        return self.entry(self.z) + up + down


def far_sends(x, near):
    far = lax.axis_size("fsdp") // near
    z = lax.axis_index("fsdp") // near
    sends = [
        lax.dynamic_index_in_dim(x, z ^ k, 0, False).astype(jnp.bfloat16) for k in range(1, far)
    ]
    return lax.dynamic_index_in_dim(x, z, 0, False), sends


def far_arrive(sends, near):
    return [swap(send, "fsdp", k * near) for k, send in enumerate(sends, 1)]


def added(own, parts):
    for part in parts:
        own = own + part.astype(jnp.float32)
    return own


def far_reduce(x, near):
    return lax.psum_scatter(
        x, "fsdp", scatter_dimension=0, tiled=True, axis_index_groups=far_groups(near)
    )[0]


def begin_pair_sum(grad, rows, near):
    core = lax.axis_index("vocab")
    grad = grad.reshape(-1, near, 2, rows, grad.shape[-1])
    send = lax.dynamic_index_in_dim(grad, 1 - core, 2, False).astype(jnp.bfloat16)
    return (lax.dynamic_index_in_dim(grad, core, 2, False), [send])


def weight_kernel(counts, core_ref, *refs):
    keep_ref, send_ref = refs[-2:]
    step, first = pl.program_id(0), 0
    rows = keep_ref.shape[1]
    mine = core_ref[0] == 0
    for i, count in enumerate(counts):

        def put(grad_ref=refs[2 * i], input_ref=refs[2 * i + 1]):
            product = lax.dot_general(
                grad_ref[...],
                input_ref[...],
                (((0,), (0,)), ((), ())),
                preferred_element_type=jnp.float32,
            )
            one, two = product[:rows], product[rows:]
            keep_ref[0] = jnp.where(mine, one, two)
            send_ref[0] = jnp.where(mine, two, one).astype(send_ref.dtype)

        pl.when((step >= first) & (step < first + count))(put)
        first += count


def weight_sums(pairs, rows):
    width = pairs[0][1].shape[1]
    counts = [grad.shape[1] // (2 * rows) for grad, _ in pairs]
    total = sum(counts)
    specs, operands, first = [], [], 0
    for (grad, given), count in zip(pairs, counts):
        specs.append(
            pl.BlockSpec(
                (grad.shape[0], 2 * rows),
                lambda i, _, first=first, count=count: (0, jnp.clip(i - first, 0, count - 1)),
            )
        )
        specs.append(pl.BlockSpec(given.shape, lambda i, _: (0, 0)))
        operands += [grad, given]
        first += count
    return pl.pallas_call(
        functools.partial(weight_kernel, counts),
        grid_spec=pltpu.PrefetchScalarGridSpec(
            num_scalar_prefetch=1,
            grid=(total,),
            in_specs=specs,
            out_specs=[pl.BlockSpec((1, rows, width), lambda i, _: (i, 0, 0))] * 2,
        ),
        out_shape=[
            jax.ShapeDtypeStruct((total, rows, width), jnp.float32),
            jax.ShapeDtypeStruct((total, rows, width), jnp.bfloat16),
        ],
        compiler_params=pltpu.CompilerParams(vmem_limit_bytes=40 * 1024 * 1024),
        name="weight_sums",
    )(lax.axis_index("vocab").astype(jnp.int32).reshape(1), *operands)


def in_order(parts, near):
    p = lax.axis_index("fsdp") % near
    stacked = []
    for q in range(near):
        entry = parts[0]
        for k in range(1, near):
            entry = jnp.where(p ^ k == q, parts[k], entry)
        stacked.append(entry)
    return jnp.stack(stacked)


def place_kernel(spans, blocks, order_ref, *refs):
    pieces, outs = refs[: -len(spans)], refs[-len(spans) :]
    for i, piece in enumerate(pieces):
        for kz in range(blocks):
            block = order_ref[i * blocks + kz]
            for out, (first, last, start, rows) in zip(outs, spans):

                def put(piece=piece, kz=kz, block=block, out=out, first=first, start=start, rows=rows):
                    out[block - first] = piece[kz, start : start + rows]

                if first == 0 and last == len(pieces) * blocks:
                    put()
                else:
                    pl.when((block >= first) & (block < last))(put)


def gather_pieces(line):
    half = line.shape[0] // 2
    one, two = line[:half], line[half:]
    one_x, two_y = swap(one, "fsdp", 1), swap(two, "fsdp", 2)
    one_y, two_x = swap(one, "fsdp", 2), swap(two, "fsdp", 1)
    one_xy, two_xy = swap(one_x, "fsdp", 2), swap(two_y, "fsdp", 1)
    return [[one, one_x, one_y, one_xy], [two, two_x, two_y, two_xy]]


def place_blocks(pieces, order, spans):
    width = pieces[0].shape[-1]
    return pl.pallas_call(
        functools.partial(place_kernel, spans, pieces[0].shape[0]),
        grid_spec=pltpu.PrefetchScalarGridSpec(
            num_scalar_prefetch=1,
            grid=(1,),
            in_specs=[pl.BlockSpec(memory_space=pltpu.VMEM)] * len(pieces),
            out_specs=[pl.BlockSpec(memory_space=pltpu.VMEM)] * len(spans),
        ),
        out_shape=[
            jax.ShapeDtypeStruct((last - first, rows, width), pieces[0].dtype)
            for first, last, _, rows in spans
        ],
        compiler_params=pltpu.CompilerParams(vmem_limit_bytes=40 * 1024 * 1024),
        name="place",
    )(jnp.stack(order).astype(jnp.int32), *pieces)


def lookup_kernel(low_count, ids_ref, table_ref, *refs):
    out_ref, spread = refs[-2:]
    width = table_ref.shape[0]

    @pl.when(pl.program_id(0) == 0)
    def _():
        for low in range(low_count):
            spread[low * width : (low + 1) * width, :] = table_ref[
                :, low * HIGH_COUNT : (low + 1) * HIGH_COUNT
            ].astype(jnp.bfloat16)

    ids = ids_ref[0]
    low_ids = ids >> 9
    row = lax.broadcasted_iota(jnp.int32, (HIGH_COUNT, ids.shape[1]), 0)
    match = (row == (ids & (HIGH_COUNT - 1))).astype(jnp.bfloat16)
    found = jnp.dot(spread[...], match, preferred_element_type=jnp.float32)
    total = jnp.zeros((width, ids.shape[1]), jnp.float32)
    for low in range(low_count):
        total = jnp.where(low_ids == low, found[low * width : (low + 1) * width, :], total)
    out_ref[0] = total.astype(out_ref.dtype)


def lookup(table_t, ids, *needed):
    rows = table_t.shape[0]
    table_t = jnp.pad(table_t, ((0, -rows % 16), (0, 0)))
    width, vocab = table_t.shape
    blocks, _, length = ids.shape
    low_count = vocab // HIGH_COUNT
    found = pl.pallas_call(
        functools.partial(lookup_kernel, low_count),
        grid=(blocks,),
        in_specs=[
            pl.BlockSpec((1, 1, length), lambda i: (i, 0, 0)),
            pl.BlockSpec((width, vocab), lambda i: (0, 0)),
        ]
        + [pl.BlockSpec(memory_space=pl.ANY)] * len(needed),
        out_specs=pl.BlockSpec((1, width, length), lambda i: (i, 0, 0)),
        out_shape=jax.ShapeDtypeStruct((blocks, width, length), jnp.bfloat16),
        scratch_shapes=[pltpu.VMEM((low_count * width, HIGH_COUNT), jnp.bfloat16)],
        compiler_params=pltpu.CompilerParams(vmem_limit_bytes=40 * 1024 * 1024),
        cost_estimate=pl.CostEstimate(
            flops=2 * blocks * length * width * vocab,
            bytes_accessed=4 * width * vocab + 2 * blocks * width * length,
            transcendentals=0,
        ),
        name="lookup",
    )(ids, table_t, *needed)
    return found[:, :rows]


def spread_kernel(low_count, ids_ref, grad_ref, *refs):
    out_ref, lhs, total = refs[-3:]
    width = grad_ref.shape[1]
    step = pl.program_id(0)

    @pl.when(step == 0)
    def _():
        total[...] = jnp.zeros_like(total)

    ids = ids_ref[0]
    low_ids = ids >> 9
    grad = grad_ref[0].astype(jnp.float32)
    for low in range(low_count):
        lhs[low * width : (low + 1) * width, :] = jnp.where(low_ids == low, grad, 0.0).astype(
            jnp.bfloat16
        )
    row = lax.broadcasted_iota(jnp.int32, (HIGH_COUNT, ids.shape[1]), 0)
    match = (row == (ids & (HIGH_COUNT - 1))).astype(jnp.bfloat16)
    total[...] += lax.dot_general(
        lhs[...], match, (((1,), (1,)), ((), ())), preferred_element_type=jnp.float32
    )

    @pl.when(step == pl.num_programs(0) - 1)
    def _():
        for low in range(low_count):
            span = slice(low * HIGH_COUNT, (low + 1) * HIGH_COUNT)
            out_ref[:, span] = total[low * width : (low + 1) * width, :]


def spread_add(grads, ids, vocab, *needed):
    rows = grads.shape[1]
    grads = jnp.pad(grads, ((0, 0), (0, -rows % 16), (0, 0)))
    width = grads.shape[1]
    blocks, _, length = ids.shape
    low_count = vocab // HIGH_COUNT
    summed = pl.pallas_call(
        functools.partial(spread_kernel, low_count),
        grid=(blocks,),
        in_specs=[
            pl.BlockSpec((1, 1, length), lambda i: (i, 0, 0)),
            pl.BlockSpec((1, width, length), lambda i: (i, 0, 0)),
        ]
        + [pl.BlockSpec(memory_space=pl.ANY)] * len(needed),
        out_specs=pl.BlockSpec((width, vocab), lambda i: (0, 0)),
        out_shape=jax.ShapeDtypeStruct((width, vocab), jnp.float32),
        scratch_shapes=[
            pltpu.VMEM((low_count * width, length), jnp.bfloat16),
            pltpu.VMEM((low_count * width, HIGH_COUNT), jnp.float32),
        ],
        compiler_params=pltpu.CompilerParams(vmem_limit_bytes=40 * 1024 * 1024),
        cost_estimate=COST,
        name="spread_add",
    )(ids, grads, *needed)
    return summed[:rows]


def split_vectors(vectors_all, width):
    hidden_units = vectors_all.shape[0] - 10 * width
    pieces = []
    offset = 0
    for piece_len in [width] * 9 + [hidden_units, width]:
        pieces.append(vectors_all[offset : offset + piece_len])
        offset = offset + piece_len
    return pieces


def layer_norm(input_batch, gain, shift):
    center = input_batch - jnp.mean(input_batch, axis=-1, keepdims=True)
    spread = jnp.mean(center * center, axis=-1, keepdims=True)
    return center * lax.rsqrt(spread + NORM_EPS) * gain + shift


def norm_back(input_batch, gain, shift, gradient_tree):
    unused, pull = jax.vjp(layer_norm, input_batch, gain, shift)
    return pull(gradient_tree)


def project(input_batch, weight_matrix):
    return jnp.einsum("mh,ph->mp", input_batch, weight_matrix, preferred_element_type=jnp.float32)


def project_back(gradient, weight_matrix):
    return jnp.einsum("az,zh->ah", gradient, weight_matrix, preferred_element_type=jnp.float32)


def weight_grad(gradient, input_batch):
    return jnp.einsum("bu,bw->uw", gradient, input_batch, preferred_element_type=jnp.float32)


def column_sum(gradient):
    return jnp.sum(gradient.astype(jnp.float32), axis=0)


def scores_of(query, key_rows, live):
    raw = lax.dot_general(
        query * SCORE_SCALE, key_rows, (((1,), (1,)), ((), ())), preferred_element_type=jnp.float32
    )
    scores = jnp.where(live, raw, -1e30)
    powers = jnp.exp(scores - jnp.max(scores, axis=-1, keepdims=True))
    return powers * (1.0 / jnp.sum(powers, axis=-1, keepdims=True))


def attend_kernel(lengths_ref, query_ref, key_ref, value_ref, *refs):
    out_ref = refs[-1]
    length = lengths_ref[pl.program_id(0)]
    live = lax.broadcasted_iota(jnp.int32, (1, key_ref.shape[0]), 1) < length
    for start in range(0, query_ref.shape[1], HEAD_DIM):
        span = slice(start, start + HEAD_DIM)
        prob = scores_of(query_ref[:, span], key_ref[:, span], live).astype(jnp.bfloat16)
        context = jnp.dot(prob, value_ref[:, span], preferred_element_type=jnp.float32)
        out_ref[:, span] = context.astype(out_ref.dtype)


def attend(qkv, lengths, seqs, *needed):
    rows, total = qkv.shape
    seq_len, width = rows // seqs, total // 3
    lanes = 2 * HEAD_DIM
    blocks = width // lanes

    def part(which):
        return pl.BlockSpec((seq_len, lanes), lambda s, j, _: (s, which * blocks + j))

    return pl.pallas_call(
        attend_kernel,
        grid_spec=pltpu.PrefetchScalarGridSpec(
            num_scalar_prefetch=1,
            grid=(seqs, blocks),
            in_specs=[part(0), part(1), part(2)]
            + [pl.BlockSpec(memory_space=pl.ANY)] * len(needed),
            out_specs=pl.BlockSpec((seq_len, lanes), lambda s, j, _: (s, j)),
        ),
        out_shape=jax.ShapeDtypeStruct((rows, width), jnp.bfloat16),
        compiler_params=pltpu.CompilerParams(vmem_limit_bytes=40 * 1024 * 1024),
        cost_estimate=COST,
        name="attend",
    )(lengths, qkv, qkv, qkv, *needed)


def attend_back_kernel(lengths_ref, query_ref, key_ref, value_ref, grad_ref, *refs):
    out_ref = refs[-1]
    length = lengths_ref[pl.program_id(0)]
    step = pl.program_id(1)
    width = out_ref.shape[1] // 3
    live = lax.broadcasted_iota(jnp.int32, (1, key_ref.shape[0]), 1) < length
    parts = [[], [], []]
    for start in range(0, query_ref.shape[1], HEAD_DIM):
        span = slice(start, start + HEAD_DIM)
        query, key_rows, value_rows = query_ref[:, span], key_ref[:, span], value_ref[:, span]
        grad_out = grad_ref[:, span]
        prob = scores_of(query, key_rows, live)
        grad_prob = lax.dot_general(
            grad_out, value_rows, (((1,), (1,)), ((), ())), preferred_element_type=jnp.float32
        )
        grad_value = lax.dot_general(
            prob.astype(jnp.bfloat16),
            grad_out,
            (((0,), (0,)), ((), ())),
            preferred_element_type=jnp.float32,
        )
        mean = jnp.sum(prob * grad_prob, axis=-1, keepdims=True)
        grad_score = (prob * (grad_prob - mean)).astype(jnp.bfloat16)
        grad_query = jnp.dot(grad_score, key_rows, preferred_element_type=jnp.float32)
        grad_key = lax.dot_general(
            grad_score, query, (((0,), (0,)), ((), ())), preferred_element_type=jnp.float32
        )
        parts[0].append(grad_query * SCORE_SCALE)
        parts[1].append(grad_key * SCORE_SCALE)
        parts[2].append(grad_value)
    lanes = query_ref.shape[1]
    for which, pieces in enumerate(parts):
        start = pl.multiple_of(which * width + step * lanes, lanes)
        out_ref[:, pl.ds(start, lanes)] = jnp.concatenate(pieces, 1).astype(out_ref.dtype)


def attend_back(qkv, grad_context, lengths, seqs, *needed):
    rows, total = qkv.shape
    seq_len, width = rows // seqs, total // 3
    lanes = 2 * HEAD_DIM
    blocks = width // lanes

    def part(which):
        return pl.BlockSpec((seq_len, lanes), lambda s, j, _: (s, which * blocks + j))

    return pl.pallas_call(
        attend_back_kernel,
        grid_spec=pltpu.PrefetchScalarGridSpec(
            num_scalar_prefetch=1,
            grid=(seqs, blocks),
            in_specs=[part(0), part(1), part(2), part(0)]
            + [pl.BlockSpec(memory_space=pl.ANY)] * len(needed),
            out_specs=pl.BlockSpec((seq_len, total), lambda s, j, _: (s, 0)),
        ),
        out_shape=jax.ShapeDtypeStruct((rows, total), jnp.bfloat16),
        compiler_params=pltpu.CompilerParams(vmem_limit_bytes=40 * 1024 * 1024),
        cost_estimate=COST,
        name="attend_back",
    )(lengths, qkv, qkv, qkv, grad_context, *needed)


def teacher_rows(place_ref, parts, held):
    which = place_ref[0] ^ pl.program_id(0)
    for k, part_ref in enumerate(parts):

        def hold(part_ref=part_ref):
            held[...] = part_ref[...]

        pl.when(which == k)(hold)
    return held[...].astype(jnp.float32)


def head_kernel(place_ref, rows_ref, table_ref, bias_ref, *refs):
    parts, (logits_ref, stats_ref, held) = refs[:-3], refs[-3:]
    logits = (
        jnp.dot(rows_ref[...], table_ref[...], preferred_element_type=jnp.float32) + bias_ref[...]
    )
    logits_ref[...] = logits
    teach = teacher_rows(place_ref, parts, held)
    student_top = jnp.max(logits, axis=-1, keepdims=True)
    student_total = jnp.sum(jnp.exp(logits - student_top), axis=-1, keepdims=True)
    teacher_top = jnp.max(teach, axis=-1, keepdims=True)
    weighted = jnp.exp(teach - teacher_top)
    teacher_total = jnp.sum(weighted, axis=-1, keepdims=True)
    cross = jnp.sum(weighted * (teach - logits), axis=-1, keepdims=True)
    lane = lax.broadcasted_iota(jnp.int32, (logits.shape[0], 128), 1)
    packed = jnp.zeros((logits.shape[0], 128), jnp.float32)
    for i, stat in enumerate((student_top, student_total, teacher_top, teacher_total, cross)):
        packed = jnp.where(lane == i, stat, packed)
    stats_ref[0] = packed.T[:8]


def head(place, rows, table_part, bias_part, teach_parts, near):
    count, width = rows.shape
    vocab = table_part.shape[1]
    block = count // near
    whole = pl.BlockSpec((block, vocab), lambda i, _: (0, 0))
    return pl.pallas_call(
        head_kernel,
        grid_spec=pltpu.PrefetchScalarGridSpec(
            num_scalar_prefetch=1,
            grid=(near,),
            in_specs=[
                pl.BlockSpec((block, width), lambda i, _: (i, 0)),
                pl.BlockSpec((width, vocab), lambda i, _: (0, 0)),
                pl.BlockSpec((1, vocab), lambda i, _: (0, 0)),
            ]
            + [whole] * near,
            out_specs=[
                pl.BlockSpec((block, vocab), lambda i, _: (i, 0)),
                pl.BlockSpec((1, 8, block), lambda i, _: (i, 0, 0)),
            ],
            scratch_shapes=[pltpu.VMEM((block, vocab), jnp.bfloat16)],
        ),
        out_shape=[
            jax.ShapeDtypeStruct((count, vocab), jnp.float32),
            jax.ShapeDtypeStruct((near, 8, block), jnp.float32),
        ],
        compiler_params=pltpu.CompilerParams(vmem_limit_bytes=56 * 1024 * 1024),
        cost_estimate=COST,
        name="head",
    )(place, rows, table_part, bias_part, *teach_parts)


def head_back_kernel(place_ref, logits_ref, stats_ref, scale_ref, table_ref, *refs):
    parts, (grad_ref, rows_ref, bias_ref, loss_ref, held) = refs[:-5], refs[-5:]
    teach = teacher_rows(place_ref, parts, held)
    step = pl.program_id(0)
    stats = stats_ref[:, 0]
    tops, totals, teacher_tops, teacher_totals, crosses = (stats[:, i] for i in range(5))
    top = jnp.max(tops, axis=0, keepdims=True)
    total = jnp.sum(totals * jnp.exp(tops - top), axis=0, keepdims=True)
    teacher_top = jnp.max(teacher_tops, axis=0, keepdims=True)
    teacher_scale = jnp.exp(teacher_tops - teacher_top)
    teacher_total = jnp.sum(teacher_totals * teacher_scale, axis=0, keepdims=True)
    cross = jnp.sum(crosses * teacher_scale, axis=0, keepdims=True)
    student_lse = top + jnp.log(total)
    teacher_lse = teacher_top + jnp.log(teacher_total)
    loss_ref[0] = cross / teacher_total - teacher_lse + student_lse
    packed = jnp.concatenate(
        [student_lse, teacher_lse, scale_ref[0], jnp.zeros((5, top.shape[1]), jnp.float32)], 0
    ).T
    grad = (
        (
            jnp.exp(logits_ref[...] - packed[:, 0:1])
            - jnp.exp(teach - packed[:, 1:2])
        )
        * packed[:, 2:3]
    ).astype(jnp.bfloat16)
    grad_ref[...] = grad
    rows_ref[...] = lax.dot_general(
        grad, table_ref[...], (((1,), (1,)), ((), ())), preferred_element_type=jnp.float32
    )

    @pl.when(step == 0)
    def _():
        bias_ref[...] = jnp.zeros_like(bias_ref)

    bias_ref[...] += jnp.sum(grad.astype(jnp.float32), axis=0, keepdims=True)


def head_back(place, logits, stats, scale, table_part, teach_parts, near):
    count, vocab = logits.shape
    width = table_part.shape[0]
    block = count // near
    members = stats.shape[0]
    whole = pl.BlockSpec((block, vocab), lambda i, _: (0, 0))
    return pl.pallas_call(
        head_back_kernel,
        grid_spec=pltpu.PrefetchScalarGridSpec(
            num_scalar_prefetch=1,
            grid=(near,),
            in_specs=[
                pl.BlockSpec((block, vocab), lambda i, _: (i, 0)),
                pl.BlockSpec((members, 1, 8, block), lambda i, _: (0, i, 0, 0)),
                pl.BlockSpec((1, 1, block), lambda i, _: (i, 0, 0)),
                pl.BlockSpec((width, vocab), lambda i, _: (0, 0)),
            ]
            + [whole] * near,
            out_specs=[
                pl.BlockSpec((block, vocab), lambda i, _: (i, 0)),
                pl.BlockSpec((block, width), lambda i, _: (i, 0)),
                pl.BlockSpec((1, vocab), lambda i, _: (0, 0)),
                pl.BlockSpec((1, 1, block), lambda i, _: (i, 0, 0)),
            ],
            scratch_shapes=[pltpu.VMEM((block, vocab), jnp.bfloat16)],
        ),
        out_shape=[
            jax.ShapeDtypeStruct((count, vocab), jnp.bfloat16),
            jax.ShapeDtypeStruct((count, width), jnp.float32),
            jax.ShapeDtypeStruct((1, vocab), jnp.float32),
            jax.ShapeDtypeStruct((near, 1, block), jnp.float32),
        ],
        compiler_params=pltpu.CompilerParams(vmem_limit_bytes=56 * 1024 * 1024),
        cost_estimate=COST,
        name="head_back",
    )(place, logits, stats, scale, table_part, *teach_parts)


def layer_forward(
    embedded,
    lengths,
    seqs,
    weight_qkv,
    weight_out,
    weight_up,
    weight_down_after,
    parts,
    before_attention,
):
    (
        gain_embed,
        shift_embed,
        gain_attn,
        shift_attn,
        gain_ffn,
        shift_ffn,
        bias_query,
        bias_value,
        bias_out,
        bias_hidden,
        bias_down,
    ) = parts
    normed = layer_norm(embedded, gain_embed, shift_embed)
    normed_low = normed.astype(jnp.bfloat16)
    qkv_bias = jnp.concatenate([bias_query, jnp.zeros_like(bias_query), bias_value])
    qkv_low = (project(normed_low, weight_qkv) + qkv_bias).astype(jnp.bfloat16)
    context_low = attend(qkv_low, lengths, seqs, *before_attention)
    first_sum = normed + project(context_low, weight_out) + bias_out
    first_out = layer_norm(first_sum, gain_attn, shift_attn)
    first_low = first_out.astype(jnp.bfloat16)
    pre_act = project(first_low, weight_up) + bias_hidden
    share = 0.5 + 0.5 * lax.erf(pre_act * math.sqrt(0.5))
    act_low = (pre_act * share).astype(jnp.bfloat16)
    weight_down = weight_down_after()
    slope = share + pre_act * jnp.exp(-0.5 * pre_act * pre_act) * (1.0 / math.sqrt(2.0 * math.pi))
    second_sum = first_out + project(act_low, weight_down) + bias_down
    final = layer_norm(second_sum, gain_ffn, shift_ffn)
    saved = (
        embedded,
        normed_low,
        qkv_low,
        context_low,
        first_sum,
        first_low,
        slope,
        act_low,
        second_sum,
    )
    return (final, saved, weight_down)


def layer_backward(
    grad_final,
    saved,
    lengths,
    seqs,
    weight_qkv,
    weight_out,
    weight_up,
    weight_down,
    parts,
    sums,
    line,
    embed_columns,
    stack_rows,
    down_rows,
):
    (
        gain_embed,
        shift_embed,
        gain_attn,
        shift_attn,
        gain_ffn,
        shift_ffn,
        bias_query,
        bias_value,
        bias_out,
        bias_hidden,
        bias_down,
    ) = parts
    (
        embedded,
        normed_low,
        qkv_low,
        context_low,
        first_sum,
        first_low,
        slope,
        act_low,
        second_sum,
    ) = saved
    width = embedded.shape[1]
    grad_second, grad_gain_ffn, grad_shift_ffn = norm_back(
        second_sum, gain_ffn, shift_ffn, grad_final
    )
    grad_down_low = grad_second.astype(jnp.bfloat16)
    sums.begin("down", [(grad_down_low, act_low)], down_rows)
    grad_pre_low = (
        project_back(grad_down_low, weight_down) * slope
    ).astype(jnp.bfloat16)
    grad_pre_low = lax.optimization_barrier(grad_pre_low)
    sums.begin("up", [(grad_pre_low, first_low)], stack_rows)
    grad_first = grad_second + project_back(grad_pre_low, weight_up)
    grad_first_sum, grad_gain_attn, grad_shift_attn = norm_back(
        first_sum, gain_attn, shift_attn, grad_first
    )
    grad_out_low = grad_first_sum.astype(jnp.bfloat16)
    grad_context_low = project_back(grad_out_low, weight_out).astype(jnp.bfloat16)
    sums.in_plane(("down", "up"))
    line_sends = line.step(grad_context_low) if line else []
    grad_qkv_low = attend_back(
        qkv_low, grad_context_low, lengths, seqs, *sums.sent("up"), *line_sends
    )
    grad_normed = grad_first_sum + project_back(grad_qkv_low, weight_qkv)
    grad_embed, grad_gain_embed, grad_shift_embed = norm_back(
        embedded, gain_embed, shift_embed, grad_normed
    )
    embed_t = embed_columns(grad_embed)
    sums.begin(
        "attention",
        [(grad_qkv_low, normed_low), (grad_out_low, context_low)],
        stack_rows,
    )
    sums.hold("attention", *(line.arrived() if line else []))
    sums.arrive(("down", "up"))
    if line:
        line.step(*sums.sent("attention"))
    vectors_grad = jnp.concatenate(
        [
            grad_gain_embed,
            grad_shift_embed,
            grad_gain_attn,
            grad_shift_attn,
            grad_gain_ffn,
            grad_shift_ffn,
            column_sum(grad_qkv_low[:, :width]),
            column_sum(grad_qkv_low[:, 2 * width :]),
            column_sum(grad_out_low),
            column_sum(grad_pre_low),
            column_sum(grad_down_low),
        ]
    )
    return (embed_t, vectors_grad)


class WeightSums:
    def __init__(self, near, far, width):
        self.near, self.staged, self.width = near, far == 4, width
        self.state = {}

    def begin(self, name, pairs, rows):
        if not self.staged:
            grads = [weight_grad(grad, given) for grad, given in pairs]
            self.state[name] = (jnp.concatenate(grads, 0), [])
        elif pairs[0][0].shape[1] % (2 * rows) or 2 * rows % 128:
            grads = [weight_grad(grad, given) for grad, given in pairs]
            self.state[name] = begin_pair_sum(jnp.concatenate(grads, 0), rows, self.near)
        else:
            keep, send = weight_sums(pairs, rows)
            shape = (-1, self.near) + keep.shape[1:]
            self.state[name] = (keep.reshape(shape), [send.reshape(shape)])

    def sent(self, name):
        return self.state[name][1] if self.staged else []

    def narrow(self, x):
        parts = [
            x[..., j : j + self.width] for j in range(0, x.shape[-1], self.width)
        ]
        return parts[0] if len(parts) == 1 else jnp.concatenate(parts, -2)

    def in_plane(self, names):
        if not self.staged:
            return
        p = lax.axis_index("fsdp") % self.near
        sends = [[] for _ in range(self.near)]
        for name in names:
            keep, pair_sends = self.state[name]
            arrived = swap(pair_sends[0], "vocab", 1)
            for k in range(self.near):
                part = lax.dynamic_index_in_dim(keep, p ^ k, 1, False)
                part = part + lax.dynamic_index_in_dim(arrived, p ^ k, 1, False).astype(jnp.float32)
                part = part.astype(jnp.bfloat16) if k else part
                sends[k].append(self.narrow(part).reshape(-1, self.width))
        own, *sends = [
            parts[0] if len(parts) == 1 else jnp.concatenate(parts, 0) for parts in sends
        ]
        for name in names:
            self.state[name] = (own, sends)

    def hold(self, name, *needed):
        if self.staged:
            keep, sends = self.state[name]
            self.state[name] = (keep, after(sends, *needed))

    def arrive(self, names):
        if not self.staged:
            return []
        sends = self.state[names[0]][1]
        self.arrived = [swap(send, "fsdp", k) for k, send in enumerate(sends, 1)]
        return self.arrived

    def plane_total(self, name, arrived):
        return added(self.state[name][0], arrived)


def adam(weight_matrix, grad, first, second, rate):
    first = BETA_ONE * first + (1.0 - BETA_ONE) * grad
    second = BETA_TWO * second + (1.0 - BETA_TWO) * grad * grad
    first_hat = first / (1.0 - BETA_ONE**STEP)
    second_hat = second / (1.0 - BETA_TWO**STEP)
    new = weight_matrix - rate * (
        first_hat / (jnp.sqrt(second_hat) + ADAM_EPS) + WEIGHT_DECAY * weight_matrix
    )
    return (first, second, new)


def local(
    token_ids,
    lengths,
    masked_pos,
    teacher,
    stack_index,
    down_index,
    stack_next,
    down_next,
    word_table,
    table_first,
    table_second,
    pos_table,
    pos_first,
    pos_second,
    proj_stack,
    stack_first,
    stack_second,
    ffn_down,
    down_first,
    down_second,
    vectors,
    vectors_first,
    vectors_second,
    head_bias,
    bias_first,
    bias_second_moment,
):
    size = lax.axis_size("fsdp")
    near = math.gcd(4, size)
    far = size // near
    width = proj_stack.shape[1]
    units = ffn_down.shape[1]
    pair_seqs, seq_len = token_ids.shape
    own_seqs = pair_seqs // 2
    own_rows = own_seqs * seq_len
    core = lax.axis_index("vocab")
    place = lax.axis_index("fsdp")
    p = place % near
    vocab_dev, columns = word_table.shape
    part = vocab_dev // near
    mask_slots = masked_pos.shape[1]

    table_t = word_table.T
    all_ids = lax.all_to_all(
        jnp.broadcast_to(token_ids[None], (size, pair_seqs, seq_len)), "fsdp", 0, 0, tiled=True
    ).reshape(size, 2, own_seqs, seq_len)
    local_ids = (
        jnp.concatenate(
            [
                lax.dynamic_index_in_dim(all_ids, core, 1, False),
                lax.dynamic_index_in_dim(all_ids, 1 - core, 1, False),
            ],
            0,
        ).reshape(2 * size * own_seqs, 1, seq_len)
        - core * vocab_dev
    )

    stack_mask = kept(stack_index)
    down_mask = kept(down_index)
    stack_rows = proj_stack.shape[0]
    down_rows = ffn_down.shape[0]
    small_count = vectors.shape[0]
    own_stack = jnp.where(stack_mask, proj_stack, 0.0).astype(jnp.bfloat16)
    own_down = jnp.where(down_mask, ffn_down, 0.0).astype(jnp.bfloat16)
    pos_rows = -(-(columns // 2) // 16) * 16
    own_stack = jnp.concatenate(
        [
            own_stack,
            jnp.pad(
                pos_table.T.astype(jnp.bfloat16),
                ((0, pos_rows - columns // 2), (0, width - seq_len)),
            ),
            jnp.pad(
                vectors.astype(jnp.bfloat16)[None], ((0, 15), (0, width - small_count))
            ),
        ],
        0,
    )
    table_low = table_t.astype(jnp.bfloat16)
    half = size * own_seqs
    table_blocks = table_low.reshape(columns, near, part).transpose(1, 0, 2)
    teacher_blocks = [
        lax.dynamic_slice_in_dim(teacher, (p ^ k) * part, part, 1) for k in range(near)
    ]
    teach_parts = teacher_blocks[:1] + [
        swap(block, "fsdp", k) for k, block in enumerate(teacher_blocks[1:], 1)
    ]
    if far == 4:
        own_stack = after(own_stack, all_ids)
        stack_line = [swap(own_stack, "fsdp", k * near) for k in range(1, far)]
        near_table = exchange(table_blocks, near_groups(near)).reshape(near * columns, part)
        other_found = lookup(table_t, local_ids[half:], own_stack)
        swapped = swap(other_found, "vocab", 1)
        own_found = lookup(table_t, local_ids[:half], other_found, near_table)
        stack_line = jnp.stack([own_stack] + after(stack_line, own_found))
        own_found = own_found + swapped
        stack_pieces = gather_pieces(stack_line)
        tokens_t = exchange(own_found.reshape(size, own_seqs, columns, seq_len), None)
        down_line = exchange(
            after(jnp.broadcast_to(own_down[None], (far,) + own_down.shape), tokens_t),
            far_groups(near),
        )
        own_blocks = exchange(
            jnp.broadcast_to(down_line[None], (near,) + down_line.shape), near_groups(near)
        )
        stack_others = [[swap(piece, "vocab", 1) for piece in half] for half in stack_pieces]
        own_blocks = exchange(
            after(
                jnp.broadcast_to(down_line[None], (near,) + down_line.shape),
                stack_pieces[0][3],
                stack_pieces[1][3],
            ),
            near_groups(near),
        )
        other_blocks = swap(own_blocks, "vocab", 1)
        before_attention = [own_blocks]
        qkv_blocks = 3 * width // stack_rows
        attention_blocks = 4 * width // stack_rows
        weight_qkv, weight_out, weight_up, small = place_blocks(
            [piece for group in (stack_pieces, stack_others) for half in group for piece in half],
            [
                (place ^ ((first + kz) * near + kp)) * 2 + (core ^ kc)
                for kc in range(2)
                for first in (0, far // 2)
                for kp in range(near)
                for kz in range(far // 2)
            ],
            (
                (0, qkv_blocks, 0, stack_rows),
                (qkv_blocks, attention_blocks, 0, stack_rows),
                (attention_blocks, 2 * size, 0, stack_rows),
                (0, 2 * size, stack_rows, pos_rows + 16),
            ),
        )
        weight_qkv = weight_qkv.reshape(-1, width)
        weight_out = weight_out.reshape(-1, width)
        weight_up = weight_up.reshape(-1, width)

        def weight_down_after():
            arrived = [own_blocks, other_blocks]
            (weight_down,) = place_blocks(
                [blocks.reshape((size,) + own_down.shape) for blocks in arrived],
                [
                    (kz * near + kp) * 2 + (core ^ kc)
                    for kc in range(2)
                    for kp in range(near)
                    for kz in range(far)
                ],
                ((0, 2 * size, 0, down_rows),),
            )
            return weight_down.reshape(-1, units)

    else:
        before_attention = []
        stack_all = lax.all_gather(own_stack, BOTH, axis=0)
        dense_stack = stack_all[:, :stack_rows].reshape(-1, width)
        small = stack_all[:, stack_rows:]
        weight_qkv = dense_stack[: 3 * width]
        weight_out = dense_stack[3 * width : 4 * width]
        weight_up = dense_stack[4 * width :]
        weight_down = lax.all_gather(own_down, BOTH, axis=0, tiled=True)

        def weight_down_after():
            return weight_down

        near_table = exchange(table_blocks, near_groups(near)).reshape(near * columns, part)
        found = lookup(table_t, local_ids)
        own_found = found[:half] + swap(found[half:], "vocab", 1)
        tokens_t = exchange(own_found.reshape(size, own_seqs, columns, seq_len), None)
    pos_all_t = small[:, : columns // 2, :seq_len].reshape(width, seq_len)
    vectors_all = small[:, pos_rows, :small_count].reshape(-1)
    parts = split_vectors(vectors_all.astype(jnp.float32), width)

    table_part = far_gather(near_table, near)
    tokens_t = tokens_t.transpose(1, 0, 2, 3).reshape(own_seqs, width, seq_len)
    embedded = (
        tokens_t.transpose(0, 2, 1).astype(jnp.float32)
        + pos_all_t.T.astype(jnp.float32)[None]
    ).reshape(own_rows, width)

    seq_start = place * pair_seqs + core * own_seqs
    own_lengths = lax.dynamic_slice_in_dim(lengths, seq_start, own_seqs)
    final, saved, weight_down = layer_forward(
        embedded,
        own_lengths,
        own_seqs,
        weight_qkv,
        weight_out,
        weight_up,
        weight_down_after,
        parts,
        before_attention,
    )
    own_pos = lax.dynamic_slice_in_dim(masked_pos, seq_start, own_seqs, 0)
    flat_rows = (jnp.arange(own_seqs, dtype=jnp.int32)[:, None] * seq_len + own_pos).reshape(-1)
    picked = jnp.take(final.reshape(own_rows, width), flat_rows, axis=0).astype(jnp.bfloat16)
    rows = join(picked, "vocab", 1).reshape(-1, width)
    rows = in_order(near_exchange(lambda q: rows, near), near).reshape(-1, width)

    bias_part = lax.dynamic_slice_in_dim(head_bias, p * part, part)
    own_place = p.astype(jnp.int32).reshape(1)
    output_logits, stats = head(
        own_place, rows, table_part, bias_part[None], teach_parts, near
    )
    stats = jnp.stack([stats, swap(stats, "vocab", 1)])
    stats = jnp.concatenate(near_exchange(lambda q: stats, near), 0)
    group_start = (place - p) * pair_seqs
    group_pos = lax.dynamic_slice_in_dim(masked_pos, group_start, near * pair_seqs, 0)
    group_lengths = lax.dynamic_slice_in_dim(lengths, group_start, near * pair_seqs)
    group_valid = (group_pos < group_lengths[:, None]).astype(jnp.float32).reshape(near, 1, -1)
    count = jnp.sum((masked_pos < lengths[:, None]).astype(jnp.float32))
    grad_logits, rows_grad, bias_part_grad, divergence = head_back(
        own_place, output_logits, stats, group_valid / count, table_part, teach_parts, near
    )
    group_loss = jnp.sum(divergence * group_valid) / (2 * near)
    rows_grad = halve(rows_grad.reshape(near, 2, -1, width).transpose(1, 0, 2, 3), "vocab", 1)
    rows_sends = [lax.dynamic_index_in_dim(rows_grad, p ^ k, 0, False) for k in range(near)]
    own_rows_grad = tree_sum(
        [rows_sends[0]] + [swap(send, "fsdp", k) for k, send in enumerate(rows_sends[1:], 1)]
    )
    grad_final = (
        jnp.zeros((own_rows, width), jnp.float32)
        .at[flat_rows]
        .add(own_rows_grad)
    )

    bias_full = lax.dynamic_update_slice_in_dim(
        jnp.zeros((vocab_dev,), jnp.float32), bias_part_grad[0], p * part, 0
    )
    head_grad = lax.dot_general(
        rows,
        grad_logits,
        (((0,), (0,)), ((), ())),
        preferred_element_type=jnp.float32,
    ).reshape(far, near, columns, part)
    if far == 4:
        line = FarLine(head_grad, near)
        line_sends = line.step()
        grad_final = after(grad_final, *line_sends)
    else:
        line = None

    def embed_columns(grad_embed):
        embed_t = grad_embed.reshape(own_seqs, seq_len, width).astype(jnp.bfloat16)
        embed_t = embed_t.transpose(0, 2, 1).reshape(own_seqs, size, columns, seq_len)
        return embed_t.transpose(1, 0, 2, 3)

    sums = WeightSums(near, far, width)
    embed_t, vectors_grad = layer_backward(
        grad_final,
        saved,
        own_lengths,
        own_seqs,
        weight_qkv,
        weight_out,
        weight_up,
        weight_down,
        parts,
        sums,
        line,
        embed_columns,
        stack_rows,
        down_rows,
    )

    embed_t = lax.all_to_all(embed_t, "fsdp", 0, 0, tiled=True).reshape(half, columns, seq_len)
    if far == 4:
        first_plane = sums.plane_total("up", sums.arrived)
        down_plane = first_plane[: far * (units // width) * down_rows].reshape(far, -1, width)
        up_plane = first_plane[far * (units // width) * down_rows :].reshape(-1, stack_rows, width)
        sums.in_plane(("attention",))
        attention_sends = sums.sent("attention")
        other_t = swap(embed_t, "vocab", 1)
        token_grad = spread_add(embed_t, local_ids[:half], vocab_dev, other_t, *attention_sends)
        head_grad = line.total(token_grad)
        blocks_sent = [
            lax.dynamic_index_in_dim(head_grad, p ^ k, 0, False) for k in range(near)
        ]
        blocks = [swap(block, "fsdp", k) for k, block in enumerate(blocks_sent[1:], 1)]
        attention_plane = sums.plane_total(
            "attention", after(sums.arrive(("attention",)), token_grad)
        ).reshape(-1, stack_rows, width)
        own = jnp.concatenate(
            [jnp.concatenate([attention_plane, up_plane], 0), down_plane], 1
        )
        far_low = own.astype(jnp.bfloat16)
        arrived = exchange(far_low, far_groups(near))
        last_grad = spread_add(
            other_t, local_ids[half:], vocab_dev, far_low, *blocks_sent
        )
        blocks = blocks_sent[:1] + after(blocks, last_grad)
        token_grad = token_grad + last_grad
        vectors_grad = after(vectors_grad, far_low)
        vectors_grad = vectors_grad + swap(vectors_grad, "vocab", 1)
        small_sums = jnp.concatenate([bias_full, vectors_grad])
        small_sums = tree_sum(near_exchange(lambda q: small_sums, near))
        small_sums = sum_far(small_sums, near)
        z = place // near
        other = lax.broadcasted_iota(jnp.int32, (far, 1, 1), 0) != z
        total = jnp.sum(jnp.where(other, arrived.astype(jnp.float32), own), axis=0)
        stack_total = total[:stack_rows]
        down_total = jnp.concatenate(
            jnp.split(total[stack_rows:], units // width, axis=0), 1
        )
        embed_t = jnp.concatenate([embed_t, other_t], 0)
    else:
        embed_t = jnp.concatenate([embed_t, swap(embed_t, "vocab", 1)], 0)
        token_grad = spread_add(embed_t, local_ids, vocab_dev)
        vectors_grad = vectors_grad + swap(vectors_grad, "vocab", 1)
        small_sums = jnp.concatenate([bias_full, vectors_grad])
        small_sums = tree_sum(near_exchange(lambda q: small_sums, near))
        small_sums = sum_far(small_sums, near)
        head_grad = far_reduce(head_grad, near)
        blocks = near_exchange(lambda q: lax.dynamic_index_in_dim(head_grad, q, 0, False), near)
        stack_grad = [sums.state[name][0] for name in ("attention", "up")]
        stack_total = lax.psum_scatter(
            jnp.concatenate(stack_grad, 0), BOTH, scatter_dimension=0, tiled=True
        )
        down_total = lax.psum_scatter(
            sums.state["down"][0], BOTH, scatter_dimension=0, tiled=True
        )
    bias_grad, vectors_grad = small_sums[:vocab_dev], small_sums[vocab_dev:]
    head_grad_t = jnp.concatenate(list(in_order(blocks, near)), 1).astype(jnp.float32)
    table_total = head_grad_t + token_grad
    pos_total = jnp.sum(embed_t.astype(jnp.float32), axis=0)
    pos_total = lax.dynamic_slice_in_dim(pos_total, core * (columns // 2), columns // 2, 0)
    vectors_total = lax.dynamic_slice_in_dim(
        vectors_grad, (2 * place + core) * small_count, small_count
    )

    stack_total = stack_total + jnp.where(stack_mask, 0.0, PRUNE_DECAY) * proj_stack
    down_total = down_total + jnp.where(down_mask, 0.0, PRUNE_DECAY) * ffn_down
    changes = jnp.sum((stack_mask != kept(stack_next)).astype(jnp.float32)) + jnp.sum(
        (down_mask != kept(down_next)).astype(jnp.float32)
    )
    squares = (
        jnp.sum(stack_total * stack_total)
        + jnp.sum(down_total * down_total)
        + jnp.sum(pos_total * pos_total)
        + jnp.sum(vectors_total * vectors_total)
        + jnp.sum(table_total * table_total)
        + jnp.sum(bias_grad * bias_grad) / size
    )
    scalars = jnp.stack([squares, group_loss, changes])
    scalars = sum_all(scalars, near)
    total_squares, loss_sum, change_total = scalars[0], scalars[1], scalars[2]
    grad_norm = jnp.sqrt(total_squares)
    factor = jnp.minimum(1.0, CLIP / (grad_norm + 1e-06))
    table_out = adam(table_t, table_total * factor, table_first.T, table_second.T, RATE_MATRIX)
    pos_out = adam(pos_table.T, pos_total * factor, pos_first.T, pos_second.T, RATE_MATRIX)
    stack_out = adam(proj_stack, stack_total * factor, stack_first, stack_second, RATE_MATRIX)
    down_out = adam(ffn_down, down_total * factor, down_first, down_second, RATE_MATRIX)
    vectors_out = adam(vectors, vectors_total * factor, vectors_first, vectors_second, RATE_VECTOR)
    bias_out = adam(head_bias, bias_grad * factor, bias_first, bias_second_moment, RATE_VECTOR)
    return (
        table_out[0].T,
        table_out[1].T,
        table_out[2].T,
        pos_out[0].T,
        pos_out[1].T,
        pos_out[2].T,
        stack_out[0],
        stack_out[1],
        stack_out[2],
        down_out[0],
        down_out[1],
        down_out[2],
        vectors_out[0],
        vectors_out[1],
        vectors_out[2],
        bias_out[0],
        bias_out[1],
        bias_out[2],
        loss_sum,
        count,
        grad_norm,
        change_total.astype(jnp.int32),
    )


def solution(mesh):
    in_specs = (
        P("fsdp", None),
        P(),
        P(),
        P("fsdp", "vocab"),
        P(("fsdp", "vocab"), None),
        P(("fsdp", "vocab"), None),
        P(("fsdp", "vocab"), None),
        P(("fsdp", "vocab"), None),
        P("vocab", "fsdp"),
        P("vocab", "fsdp"),
        P("vocab", "fsdp"),
        P(None, ("fsdp", "vocab")),
        P(None, ("fsdp", "vocab")),
        P(None, ("fsdp", "vocab")),
        P(("fsdp", "vocab"), None),
        P(("fsdp", "vocab"), None),
        P(("fsdp", "vocab"), None),
        P(("fsdp", "vocab"), None),
        P(("fsdp", "vocab"), None),
        P(("fsdp", "vocab"), None),
        P(("fsdp", "vocab")),
        P(("fsdp", "vocab")),
        P(("fsdp", "vocab")),
        P("vocab"),
        P("vocab"),
        P("vocab"),
    )
    out_specs = (
        P("vocab", "fsdp"),
        P("vocab", "fsdp"),
        P("vocab", "fsdp"),
        P(None, ("fsdp", "vocab")),
        P(None, ("fsdp", "vocab")),
        P(None, ("fsdp", "vocab")),
        P(("fsdp", "vocab"), None),
        P(("fsdp", "vocab"), None),
        P(("fsdp", "vocab"), None),
        P(("fsdp", "vocab"), None),
        P(("fsdp", "vocab"), None),
        P(("fsdp", "vocab"), None),
        P(("fsdp", "vocab")),
        P(("fsdp", "vocab")),
        P(("fsdp", "vocab")),
        P("vocab"),
        P("vocab"),
        P("vocab"),
        P(),
        P(),
        P(),
        P(),
    )
    return jax.shard_map(local, mesh=mesh, in_specs=in_specs, out_specs=out_specs, check_vma=False)
```

```python
import functools
import math

import jax
import jax.numpy as jnp
from jax import lax
from jax.experimental import pallas as pl
from jax.experimental.pallas import tpu as pltpu
from jax.sharding import PartitionSpec as P

HEAD_DIM = 64
STEP = 10


NORM_EPS = 1e-05
CLIP = 0.005
PRUNE_DECAY = 0.0002
BETA_ONE = 0.9
BETA_TWO = 0.999
ADAM_EPS = 1e-08
WEIGHT_DECAY = 0.01
RATE_MATRIX = 0.1
RATE_VECTOR = 1.0
SCORE_SCALE = 0.125


HIGH_COUNT = 512
COST = pl.CostEstimate(flops=1, bytes_accessed=1, transcendentals=0)
BOTH = ("fsdp", "vocab")


def kept(words):
    columns = words.shape[1] * 16
    place = lax.broadcasted_iota(jnp.int32, (2 * words.shape[1], columns), 0)
    column = lax.broadcasted_iota(jnp.int32, (2 * words.shape[1], columns), 1)
    spread = (place % words.shape[1] * 2 + place // words.shape[1] == column // 8).astype(
        jnp.bfloat16
    )
    bytes_low = jnp.concatenate([words & 255, words >> 8], 1).astype(jnp.bfloat16)
    byte = jnp.dot(bytes_low, spread, preferred_element_type=jnp.float32).astype(jnp.int32)
    spot = lax.broadcasted_iota(jnp.int32, byte.shape, 1)
    nibble = jnp.where(spot % 8 < 4, byte & 15, byte >> 4)
    spot = spot % 4
    return ((nibble & 3) == spot) | ((nibble >> 2) == spot)


def swap(x, axis, bit):
    size = lax.axis_size(axis)
    return lax.ppermute(x, axis, [(i, i ^ bit) for i in range(size)])


def my_bit(axis, bit):
    return lax.axis_index(axis) // bit % 2


def bits_of(size):
    return [1 << k for k in range(size.bit_length() - 1)]


def gate_kernel(*refs):
    pass


def after(x, *needed):
    if not needed:
        return x
    parts = x if isinstance(x, list) else [x]
    anywhere = pl.BlockSpec(memory_space=pl.ANY)
    outs = pl.pallas_call(
        gate_kernel,
        in_specs=[anywhere] * (len(parts) + len(needed)),
        out_specs=[anywhere] * len(parts),
        out_shape=[jax.ShapeDtypeStruct(part.shape, part.dtype) for part in parts],
        input_output_aliases={i: i for i in range(len(parts))},
        name="gate",
    )(*parts, *needed)
    return list(outs) if isinstance(x, list) else outs[0]


def tree_sum(parts):
    while len(parts) > 1:
        parts = [one + two for one, two in zip(parts[::2], parts[1::2])]
    return parts[0]


def sum_all(x, near):
    x = x + swap(x, "vocab", 1)
    x = tree_sum(near_exchange(lambda q: x, near))
    return sum_far(x, near)


def sum_far(x, near):
    far = lax.axis_size("fsdp") // near
    if far == 4:
        return tree_sum([x] + [swap(x, "fsdp", k * near) for k in range(1, far)])
    for bit in bits_of(far):
        x = x + swap(x, "fsdp", bit * near)
    return x


def join(x, axis, bit):
    other = swap(x, axis, bit)
    upper = my_bit(axis, bit) == 1
    return jnp.stack([jnp.where(upper, other, x), jnp.where(upper, x, other)])


def halve(x, axis, bit):
    mine = my_bit(axis, bit)
    return lax.dynamic_index_in_dim(x, mine, 0, False) + swap(
        lax.dynamic_index_in_dim(x, 1 - mine, 0, False), axis, bit
    )


def near_exchange(take, near):
    size = lax.axis_size("fsdp")
    p = lax.axis_index("fsdp") % near
    return [take(p)] + [
        lax.ppermute(take(p ^ k), "fsdp", [(i, i ^ k) for i in range(size)]) for k in range(1, near)
    ]


def far_groups(near):
    size = lax.axis_size("fsdp")
    return [list(range(q, size, near)) for q in range(near)]


def near_groups(near):
    size = lax.axis_size("fsdp")
    return [list(range(start, start + near)) for start in range(0, size, near)]


def exchange(x, groups):
    return lax.all_to_all(x, "fsdp", 0, 0, tiled=True, axis_index_groups=groups)


def far_gather(x, near):
    return lax.all_gather(x, "fsdp", axis=0, tiled=True, axis_index_groups=far_groups(near))


class FarLine:
    def __init__(self, x, near):
        self.x, self.near = x, near
        self.far = 4
        self.z = lax.axis_index("fsdp") // near
        self.k = 0
        self.up = self.down = None

    def entry(self, j):
        return lax.dynamic_index_in_dim(self.x, jnp.clip(j, 0, self.far - 1), 0, False)

    def arrived(self):
        return [self.up, self.down]

    def step(self, *needed):
        self.k += 1
        k, near, size = self.k, self.near, self.far * self.near
        send_up = self.entry(self.far - k + self.z)
        send_down = self.entry(self.z - self.far + k)
        if k > 1:
            up, down = after([self.up, self.down], *needed) if needed else (self.up, self.down)
            send_up, send_down = send_up + up, send_down + down
        sends = [send_up.astype(jnp.bfloat16), send_down.astype(jnp.bfloat16)]
        self.up = lax.ppermute(sends[0], "fsdp", [(i, i + near) for i in range(k * near)])
        self.down = lax.ppermute(
            sends[1], "fsdp", [(i, i - near) for i in range(size - k * near, size)]
        )
        return sends

    def total(self, *needed):
        up, down = after([self.up, self.down], *needed)
        return self.entry(self.z) + up + down


def far_sends(x, near):
    far = lax.axis_size("fsdp") // near
    z = lax.axis_index("fsdp") // near
    sends = [
        lax.dynamic_index_in_dim(x, z ^ k, 0, False).astype(jnp.bfloat16) for k in range(1, far)
    ]
    return lax.dynamic_index_in_dim(x, z, 0, False), sends


def far_arrive(sends, near):
    return [swap(send, "fsdp", k * near) for k, send in enumerate(sends, 1)]


def added(own, parts):
    for part in parts:
        own = own + part.astype(jnp.float32)
    return own


def far_reduce(x, near):
    return lax.psum_scatter(
        x, "fsdp", scatter_dimension=0, tiled=True, axis_index_groups=far_groups(near)
    )[0]


def begin_pair_sum(grad, rows, near):
    core = lax.axis_index("vocab")
    grad = grad.reshape(-1, near, 2, rows, grad.shape[-1])
    send = lax.dynamic_index_in_dim(grad, 1 - core, 2, False).astype(jnp.bfloat16)
    return (lax.dynamic_index_in_dim(grad, core, 2, False), [send])


def weight_kernel(counts, core_ref, *refs):
    keep_ref, send_ref = refs[-2:]
    step, first = pl.program_id(0), 0
    rows = keep_ref.shape[1]
    mine = core_ref[0] == 0
    for i, count in enumerate(counts):

        def put(grad_ref=refs[2 * i], input_ref=refs[2 * i + 1]):
            product = lax.dot_general(
                grad_ref[...],
                input_ref[...],
                (((0,), (0,)), ((), ())),
                preferred_element_type=jnp.float32,
            )
            one, two = product[:rows], product[rows:]
            keep_ref[0] = jnp.where(mine, one, two)
            send_ref[0] = jnp.where(mine, two, one).astype(send_ref.dtype)

        pl.when((step >= first) & (step < first + count))(put)
        first += count


def weight_sums(pairs, rows):
    width = pairs[0][1].shape[1]
    counts = [grad.shape[1] // (2 * rows) for grad, _ in pairs]
    total = sum(counts)
    specs, operands, first = [], [], 0
    for (grad, given), count in zip(pairs, counts):
        specs.append(
            pl.BlockSpec(
                (grad.shape[0], 2 * rows),
                lambda i, _, first=first, count=count: (0, jnp.clip(i - first, 0, count - 1)),
            )
        )
        specs.append(pl.BlockSpec(given.shape, lambda i, _: (0, 0)))
        operands += [grad, given]
        first += count
    return pl.pallas_call(
        functools.partial(weight_kernel, counts),
        grid_spec=pltpu.PrefetchScalarGridSpec(
            num_scalar_prefetch=1,
            grid=(total,),
            in_specs=specs,
            out_specs=[pl.BlockSpec((1, rows, width), lambda i, _: (i, 0, 0))] * 2,
        ),
        out_shape=[
            jax.ShapeDtypeStruct((total, rows, width), jnp.float32),
            jax.ShapeDtypeStruct((total, rows, width), jnp.bfloat16),
        ],
        compiler_params=pltpu.CompilerParams(vmem_limit_bytes=40 * 1024 * 1024),
        name="weight_sums",
    )(lax.axis_index("vocab").astype(jnp.int32).reshape(1), *operands)


def in_order(parts, near):
    p = lax.axis_index("fsdp") % near
    stacked = []
    for q in range(near):
        entry = parts[0]
        for k in range(1, near):
            entry = jnp.where(p ^ k == q, parts[k], entry)
        stacked.append(entry)
    return jnp.stack(stacked)


def place_kernel(spans, blocks, order_ref, *refs):
    pieces, outs = refs[: -len(spans)], refs[-len(spans) :]
    for i, piece in enumerate(pieces):
        for kz in range(blocks):
            block = order_ref[i * blocks + kz]
            for out, (first, last, start, rows) in zip(outs, spans):

                def put(piece=piece, kz=kz, block=block, out=out, first=first, start=start, rows=rows):
                    out[block - first] = piece[kz, start : start + rows]

                if first == 0 and last == len(pieces) * blocks:
                    put()
                else:
                    pl.when((block >= first) & (block < last))(put)


def gather_pieces(line):
    half = line.shape[0] // 2
    one, two = line[:half], line[half:]
    one_x, two_y = swap(one, "fsdp", 1), swap(two, "fsdp", 2)
    one_y, two_x = swap(one, "fsdp", 2), swap(two, "fsdp", 1)
    one_xy, two_xy = swap(one_x, "fsdp", 2), swap(two_y, "fsdp", 1)
    return [[one, one_x, one_y, one_xy], [two, two_x, two_y, two_xy]]


def place_blocks(pieces, order, spans):
    width = pieces[0].shape[-1]
    return pl.pallas_call(
        functools.partial(place_kernel, spans, pieces[0].shape[0]),
        grid_spec=pltpu.PrefetchScalarGridSpec(
            num_scalar_prefetch=1,
            grid=(1,),
            in_specs=[pl.BlockSpec(memory_space=pltpu.VMEM)] * len(pieces),
            out_specs=[pl.BlockSpec(memory_space=pltpu.VMEM)] * len(spans),
        ),
        out_shape=[
            jax.ShapeDtypeStruct((last - first, rows, width), pieces[0].dtype)
            for first, last, _, rows in spans
        ],
        compiler_params=pltpu.CompilerParams(vmem_limit_bytes=40 * 1024 * 1024),
        name="place",
    )(jnp.stack(order).astype(jnp.int32), *pieces)


def lookup_kernel(low_count, ids_ref, table_ref, *refs):
    out_ref, spread = refs[-2:]
    width = table_ref.shape[0]

    @pl.when(pl.program_id(0) == 0)
    def _():
        for low in range(low_count):
            spread[low * width : (low + 1) * width, :] = table_ref[
                :, low * HIGH_COUNT : (low + 1) * HIGH_COUNT
            ].astype(jnp.bfloat16)

    ids = ids_ref[0]
    low_ids = ids >> 9
    row = lax.broadcasted_iota(jnp.int32, (HIGH_COUNT, ids.shape[1]), 0)
    match = (row == (ids & (HIGH_COUNT - 1))).astype(jnp.bfloat16)
    found = jnp.dot(spread[...], match, preferred_element_type=jnp.float32)
    total = jnp.zeros((width, ids.shape[1]), jnp.float32)
    for low in range(low_count):
        total = jnp.where(low_ids == low, found[low * width : (low + 1) * width, :], total)
    out_ref[0] = total.astype(out_ref.dtype)


def lookup(table_t, ids, *needed):
    rows = table_t.shape[0]
    table_t = jnp.pad(table_t, ((0, -rows % 16), (0, 0)))
    width, vocab = table_t.shape
    blocks, _, length = ids.shape
    low_count = vocab // HIGH_COUNT
    found = pl.pallas_call(
        functools.partial(lookup_kernel, low_count),
        grid=(blocks,),
        in_specs=[
            pl.BlockSpec((1, 1, length), lambda i: (i, 0, 0)),
            pl.BlockSpec((width, vocab), lambda i: (0, 0)),
        ]
        + [pl.BlockSpec(memory_space=pl.ANY)] * len(needed),
        out_specs=pl.BlockSpec((1, width, length), lambda i: (i, 0, 0)),
        out_shape=jax.ShapeDtypeStruct((blocks, width, length), jnp.bfloat16),
        scratch_shapes=[pltpu.VMEM((low_count * width, HIGH_COUNT), jnp.bfloat16)],
        compiler_params=pltpu.CompilerParams(vmem_limit_bytes=40 * 1024 * 1024),
        cost_estimate=pl.CostEstimate(
            flops=2 * blocks * length * width * vocab,
            bytes_accessed=4 * width * vocab + 2 * blocks * width * length,
            transcendentals=0,
        ),
        name="lookup",
    )(ids, table_t, *needed)
    return found[:, :rows]


def spread_kernel(low_count, ids_ref, grad_ref, *refs):
    out_ref, lhs, total = refs[-3:]
    width = grad_ref.shape[1]
    step = pl.program_id(0)

    @pl.when(step == 0)
    def _():
        total[...] = jnp.zeros_like(total)

    ids = ids_ref[0]
    low_ids = ids >> 9
    grad = grad_ref[0].astype(jnp.float32)
    for low in range(low_count):
        lhs[low * width : (low + 1) * width, :] = jnp.where(low_ids == low, grad, 0.0).astype(
            jnp.bfloat16
        )
    row = lax.broadcasted_iota(jnp.int32, (HIGH_COUNT, ids.shape[1]), 0)
    match = (row == (ids & (HIGH_COUNT - 1))).astype(jnp.bfloat16)
    total[...] += lax.dot_general(
        lhs[...], match, (((1,), (1,)), ((), ())), preferred_element_type=jnp.float32
    )

    @pl.when(step == pl.num_programs(0) - 1)
    def _():
        for low in range(low_count):
            span = slice(low * HIGH_COUNT, (low + 1) * HIGH_COUNT)
            out_ref[:, span] = total[low * width : (low + 1) * width, :]


def spread_add(grads, ids, vocab, *needed):
    rows = grads.shape[1]
    grads = jnp.pad(grads, ((0, 0), (0, -rows % 16), (0, 0)))
    width = grads.shape[1]
    blocks, _, length = ids.shape
    low_count = vocab // HIGH_COUNT
    summed = pl.pallas_call(
        functools.partial(spread_kernel, low_count),
        grid=(blocks,),
        in_specs=[
            pl.BlockSpec((1, 1, length), lambda i: (i, 0, 0)),
            pl.BlockSpec((1, width, length), lambda i: (i, 0, 0)),
        ]
        + [pl.BlockSpec(memory_space=pl.ANY)] * len(needed),
        out_specs=pl.BlockSpec((width, vocab), lambda i: (0, 0)),
        out_shape=jax.ShapeDtypeStruct((width, vocab), jnp.float32),
        scratch_shapes=[
            pltpu.VMEM((low_count * width, length), jnp.bfloat16),
            pltpu.VMEM((low_count * width, HIGH_COUNT), jnp.float32),
        ],
        compiler_params=pltpu.CompilerParams(vmem_limit_bytes=40 * 1024 * 1024),
        cost_estimate=COST,
        name="spread_add",
    )(ids, grads, *needed)
    return summed[:rows]


def split_vectors(vectors_all, width):
    hidden_units = vectors_all.shape[0] - 10 * width
    pieces = []
    offset = 0
    for piece_len in [width] * 9 + [hidden_units, width]:
        pieces.append(vectors_all[offset : offset + piece_len])
        offset = offset + piece_len
    return pieces


def layer_norm(input_batch, gain, shift):
    center = input_batch - jnp.mean(input_batch, axis=-1, keepdims=True)
    spread = jnp.mean(center * center, axis=-1, keepdims=True)
    return center * lax.rsqrt(spread + NORM_EPS) * gain + shift


def norm_back(input_batch, gain, shift, gradient_tree):
    unused, pull = jax.vjp(layer_norm, input_batch, gain, shift)
    return pull(gradient_tree)


def project(input_batch, weight_matrix):
    return jnp.einsum("mh,ph->mp", input_batch, weight_matrix, preferred_element_type=jnp.float32)


def project_back(gradient, weight_matrix):
    return jnp.einsum("az,zh->ah", gradient, weight_matrix, preferred_element_type=jnp.float32)


def weight_grad(gradient, input_batch):
    return jnp.einsum("bu,bw->uw", gradient, input_batch, preferred_element_type=jnp.float32)


def column_sum(gradient):
    return jnp.sum(gradient.astype(jnp.float32), axis=0)


STRIP = 128
HEADS_STEP = 6
HELD = 3


def across(one, two):
    return lax.dot_general(one, two, (((1,), (1,)), ((), ())), preferred_element_type=jnp.float32)


def down(one, two):
    return lax.dot_general(one, two, (((0,), (0,)), ((), ())), preferred_element_type=jnp.float32)


def soften(raw, live):
    scores = jnp.where(live, raw, -1e30)
    powers = jnp.exp(scores - jnp.max(scores, axis=0, keepdims=True))
    return powers * (1.0 / jnp.sum(powers, axis=0, keepdims=True))


def attend_kernel(lengths_ref, query_ref, key_ref, value_ref, *refs):
    out_ref, scores, probs = refs[-3:]
    length = lengths_ref[pl.program_id(0)]
    rows = query_ref.shape[0]
    live = lax.broadcasted_iota(jnp.int32, (rows, 1), 0) < length
    contexts = []
    for head in range(query_ref.shape[1] // HEAD_DIM):
        span = slice(head * HEAD_DIM, (head + 1) * HEAD_DIM)
        scores[head % HELD] = across(key_ref[:, span], query_ref[:, span] * SCORE_SCALE)
        for start in range(0, rows, STRIP):
            part = slice(start, start + STRIP)
            probs[head % HELD, :, part] = soften(scores[head % HELD, :, part], live).astype(jnp.bfloat16)
        contexts.append(down(value_ref[:, span], probs[head % HELD]))
    out_ref[...] = jnp.concatenate(contexts, 0).T.astype(out_ref.dtype)


def attend(qkv, lengths, seqs, *needed):
    rows, total = qkv.shape
    seq_len, width = rows // seqs, total // 3
    lanes = HEADS_STEP * HEAD_DIM
    blocks = width // lanes

    def part(which):
        return pl.BlockSpec((seq_len, lanes), lambda s, j, _: (s, which * blocks + j))

    return pl.pallas_call(
        attend_kernel,
        grid_spec=pltpu.PrefetchScalarGridSpec(
            num_scalar_prefetch=1,
            grid=(seqs, blocks),
            in_specs=[part(0), part(1), part(2)]
            + [pl.BlockSpec(memory_space=pl.ANY)] * len(needed),
            out_specs=pl.BlockSpec((seq_len, lanes), lambda s, j, _: (s, j)),
            scratch_shapes=[
                pltpu.VMEM((HELD, seq_len, seq_len), jnp.float32),
                pltpu.VMEM((HELD, seq_len, seq_len), jnp.bfloat16),
            ],
        ),
        out_shape=jax.ShapeDtypeStruct((rows, width), jnp.bfloat16),
        compiler_params=pltpu.CompilerParams(vmem_limit_bytes=40 * 1024 * 1024),
        cost_estimate=COST,
        name="attend",
    )(lengths, qkv, qkv, qkv, *needed)


def attend_back_kernel(lengths_ref, query_ref, key_ref, value_ref, grad_ref, *refs):
    out_ref, scores, grad_probs, probs, grads = refs[-5:]
    length = lengths_ref[pl.program_id(0)]
    step = pl.program_id(1)
    width = out_ref.shape[1] // 3
    rows, lanes = query_ref.shape
    live = lax.broadcasted_iota(jnp.int32, (rows, 1), 0) < length
    parts = [[], [], []]
    for head in range(lanes // HEAD_DIM):
        span = slice(head * HEAD_DIM, (head + 1) * HEAD_DIM)
        query, key_rows, grad_out = query_ref[:, span], key_ref[:, span], grad_ref[:, span]
        scores[head % HELD] = across(key_rows, query * SCORE_SCALE)
        grad_probs[head % HELD] = across(value_ref[:, span], grad_out)
        for start in range(0, rows, STRIP):
            part = slice(start, start + STRIP)
            prob = soften(scores[head % HELD, :, part], live)
            grad_prob = grad_probs[head % HELD, :, part]
            mean = jnp.sum(prob * grad_prob, axis=0, keepdims=True)
            probs[head % HELD, :, part] = prob.astype(jnp.bfloat16)
            grads[head % HELD, :, part] = (prob * (grad_prob - mean)).astype(jnp.bfloat16)
        parts[0].append(down(key_rows, grads[head % HELD]) * SCORE_SCALE)
        parts[1].append(
            jnp.dot(grads[head % HELD], query, preferred_element_type=jnp.float32) * SCORE_SCALE
        )
        parts[2].append(jnp.dot(probs[head % HELD], grad_out, preferred_element_type=jnp.float32))
    merged = [jnp.concatenate(parts[0], 0).T] + [jnp.concatenate(part, 1) for part in parts[1:]]
    for which, gradient in enumerate(merged):
        start = pl.multiple_of(which * width + step * lanes, lanes)
        out_ref[:, pl.ds(start, lanes)] = gradient.astype(out_ref.dtype)


def attend_back(qkv, grad_context, lengths, seqs, *needed):
    rows, total = qkv.shape
    seq_len, width = rows // seqs, total // 3
    lanes = HEADS_STEP * HEAD_DIM
    blocks = width // lanes

    def part(which):
        return pl.BlockSpec((seq_len, lanes), lambda s, j, _: (s, which * blocks + j))

    return pl.pallas_call(
        attend_back_kernel,
        grid_spec=pltpu.PrefetchScalarGridSpec(
            num_scalar_prefetch=1,
            grid=(seqs, blocks),
            in_specs=[part(0), part(1), part(2), part(0)]
            + [pl.BlockSpec(memory_space=pl.ANY)] * len(needed),
            out_specs=pl.BlockSpec((seq_len, total), lambda s, j, _: (s, 0)),
            scratch_shapes=[
                pltpu.VMEM((HELD, seq_len, seq_len), kind)
                for kind in (jnp.float32, jnp.float32, jnp.bfloat16, jnp.bfloat16)
            ],
        ),
        out_shape=jax.ShapeDtypeStruct((rows, total), jnp.bfloat16),
        compiler_params=pltpu.CompilerParams(vmem_limit_bytes=40 * 1024 * 1024),
        cost_estimate=COST,
        name="attend_back",
    )(lengths, qkv, qkv, qkv, grad_context, *needed)


def teacher_rows(place_ref, parts, held):
    which = place_ref[0] ^ pl.program_id(0)
    for k, part_ref in enumerate(parts):

        def hold(part_ref=part_ref):
            held[...] = part_ref[...]

        pl.when(which == k)(hold)


HEAD_STRIP = 16


def head_kernel(place_ref, rows_ref, table_ref, bias_ref, *refs):
    parts, (logits_ref, stats_ref, held, packed) = refs[:-4], refs[-4:]
    teacher_rows(place_ref, parts, held)
    logits_ref[...] = (
        jnp.dot(rows_ref[...], table_ref[...], preferred_element_type=jnp.float32) + bias_ref[...]
    )
    lane = lax.broadcasted_iota(jnp.int32, (HEAD_STRIP, 128), 1)
    for row in range(0, held.shape[0], HEAD_STRIP):
        part = slice(row, row + HEAD_STRIP)
        logits = logits_ref[part, :]
        student_top = jnp.max(logits, axis=-1, keepdims=True)
        student_total = jnp.sum(jnp.exp(logits - student_top), axis=-1, keepdims=True)
        teach = held[part, :].astype(jnp.float32)
        teacher_top = jnp.max(teach, axis=-1, keepdims=True)
        weighted = jnp.exp(teach - teacher_top)
        teacher_total = jnp.sum(weighted, axis=-1, keepdims=True)
        cross = jnp.sum(weighted * (teach - logits), axis=-1, keepdims=True)
        stats = jnp.zeros((HEAD_STRIP, 128), jnp.float32)
        for i, stat in enumerate((student_top, student_total, teacher_top, teacher_total, cross)):
            stats = jnp.where(lane == i, stat, stats)
        packed[part, :] = stats
    stats_ref[0] = packed[...].T[:8]


def head(place, rows, table_part, bias_part, teach_parts, near):
    count, width = rows.shape
    vocab = table_part.shape[1]
    block = count // near
    whole = pl.BlockSpec((block, vocab), lambda i, _: (0, 0))
    return pl.pallas_call(
        head_kernel,
        grid_spec=pltpu.PrefetchScalarGridSpec(
            num_scalar_prefetch=1,
            grid=(near,),
            in_specs=[
                pl.BlockSpec((block, width), lambda i, _: (i, 0)),
                pl.BlockSpec((width, vocab), lambda i, _: (0, 0)),
                pl.BlockSpec((1, vocab), lambda i, _: (0, 0)),
            ]
            + [whole] * near,
            out_specs=[
                pl.BlockSpec((block, vocab), lambda i, _: (i, 0)),
                pl.BlockSpec((1, 8, block), lambda i, _: (i, 0, 0)),
            ],
            scratch_shapes=[
                pltpu.VMEM((block, vocab), jnp.bfloat16),
                pltpu.VMEM((block, 128), jnp.float32),
            ],
        ),
        out_shape=[
            jax.ShapeDtypeStruct((count, vocab), jnp.float32),
            jax.ShapeDtypeStruct((near, 8, block), jnp.float32),
        ],
        compiler_params=pltpu.CompilerParams(vmem_limit_bytes=56 * 1024 * 1024),
        cost_estimate=COST,
        name="head",
    )(place, rows, table_part, bias_part, *teach_parts)


def head_back_kernel(place_ref, logits_ref, stats_ref, scale_ref, table_ref, *refs):
    parts, (grad_ref, rows_ref, bias_ref, loss_ref, held) = refs[:-5], refs[-5:]
    teacher_rows(place_ref, parts, held)
    step = pl.program_id(0)
    stats = stats_ref[:, 0]
    tops, totals, teacher_tops, teacher_totals, crosses = (stats[:, i] for i in range(5))
    top = jnp.max(tops, axis=0, keepdims=True)
    total = jnp.sum(totals * jnp.exp(tops - top), axis=0, keepdims=True)
    teacher_top = jnp.max(teacher_tops, axis=0, keepdims=True)
    teacher_scale = jnp.exp(teacher_tops - teacher_top)
    teacher_total = jnp.sum(teacher_totals * teacher_scale, axis=0, keepdims=True)
    cross = jnp.sum(crosses * teacher_scale, axis=0, keepdims=True)
    student_lse = top + jnp.log(total)
    teacher_lse = teacher_top + jnp.log(teacher_total)
    loss_ref[0] = cross / teacher_total - teacher_lse + student_lse
    packed = jnp.concatenate(
        [student_lse, teacher_lse, scale_ref[0], jnp.zeros((5, top.shape[1]), jnp.float32)], 0
    ).T

    @pl.when(step == 0)
    def _():
        bias_ref[...] = jnp.zeros_like(bias_ref)

    for row in range(0, held.shape[0], HEAD_STRIP):
        part = slice(row, row + HEAD_STRIP)
        student = jnp.exp(logits_ref[part, :] - packed[part, 0:1])
        teach = jnp.exp(held[part, :].astype(jnp.float32) - packed[part, 1:2])
        grad = ((student - teach) * packed[part, 2:3]).astype(jnp.bfloat16)
        grad_ref[part, :] = grad
        bias_ref[...] += jnp.sum(grad.astype(jnp.float32), axis=0, keepdims=True)
    rows_ref[...] = lax.dot_general(
        grad_ref[...], table_ref[...], (((1,), (1,)), ((), ())), preferred_element_type=jnp.float32
    )


def head_back(place, logits, stats, scale, table_part, teach_parts, near):
    count, vocab = logits.shape
    width = table_part.shape[0]
    block = count // near
    members = stats.shape[0]
    whole = pl.BlockSpec((block, vocab), lambda i, _: (0, 0))
    return pl.pallas_call(
        head_back_kernel,
        grid_spec=pltpu.PrefetchScalarGridSpec(
            num_scalar_prefetch=1,
            grid=(near,),
            in_specs=[
                pl.BlockSpec((block, vocab), lambda i, _: (i, 0)),
                pl.BlockSpec((members, 1, 8, block), lambda i, _: (0, i, 0, 0)),
                pl.BlockSpec((1, 1, block), lambda i, _: (i, 0, 0)),
                pl.BlockSpec((width, vocab), lambda i, _: (0, 0)),
            ]
            + [whole] * near,
            out_specs=[
                pl.BlockSpec((block, vocab), lambda i, _: (i, 0)),
                pl.BlockSpec((block, width), lambda i, _: (i, 0)),
                pl.BlockSpec((1, vocab), lambda i, _: (0, 0)),
                pl.BlockSpec((1, 1, block), lambda i, _: (i, 0, 0)),
            ],
            scratch_shapes=[pltpu.VMEM((block, vocab), jnp.bfloat16)],
        ),
        out_shape=[
            jax.ShapeDtypeStruct((count, vocab), jnp.bfloat16),
            jax.ShapeDtypeStruct((count, width), jnp.float32),
            jax.ShapeDtypeStruct((1, vocab), jnp.float32),
            jax.ShapeDtypeStruct((near, 1, block), jnp.float32),
        ],
        compiler_params=pltpu.CompilerParams(vmem_limit_bytes=56 * 1024 * 1024),
        cost_estimate=COST,
        name="head_back",
    )(place, logits, stats, scale, table_part, *teach_parts)


def layer_forward(
    embedded,
    lengths,
    seqs,
    weight_qkv,
    weight_out,
    weight_up,
    weight_down_after,
    parts,
    before_attention,
):
    (
        gain_embed,
        shift_embed,
        gain_attn,
        shift_attn,
        gain_ffn,
        shift_ffn,
        bias_query,
        bias_value,
        bias_out,
        bias_hidden,
        bias_down,
    ) = parts
    normed = layer_norm(embedded, gain_embed, shift_embed)
    normed_low = normed.astype(jnp.bfloat16)
    qkv_bias = jnp.concatenate([bias_query, jnp.zeros_like(bias_query), bias_value])
    qkv_low = (project(normed_low, weight_qkv) + qkv_bias).astype(jnp.bfloat16)
    context_low = attend(qkv_low, lengths, seqs, *before_attention)
    first_sum = normed + project(context_low, weight_out) + bias_out
    first_out = layer_norm(first_sum, gain_attn, shift_attn)
    first_low = first_out.astype(jnp.bfloat16)
    pre_act = project(first_low, weight_up) + bias_hidden
    share = 0.5 + 0.5 * lax.erf(pre_act * math.sqrt(0.5))
    act_low = (pre_act * share).astype(jnp.bfloat16)
    weight_down = weight_down_after()
    slope = share + pre_act * jnp.exp(-0.5 * pre_act * pre_act) * (1.0 / math.sqrt(2.0 * math.pi))
    second_sum = first_out + project(act_low, weight_down) + bias_down
    final = layer_norm(second_sum, gain_ffn, shift_ffn)
    saved = (
        embedded,
        normed_low,
        qkv_low,
        context_low,
        first_sum,
        first_low,
        slope,
        act_low,
        second_sum,
    )
    return (final, saved, weight_down)


def layer_backward(
    grad_final,
    saved,
    lengths,
    seqs,
    weight_qkv,
    weight_out,
    weight_up,
    weight_down,
    parts,
    sums,
    line,
    embed_columns,
    stack_rows,
    down_rows,
):
    (
        gain_embed,
        shift_embed,
        gain_attn,
        shift_attn,
        gain_ffn,
        shift_ffn,
        bias_query,
        bias_value,
        bias_out,
        bias_hidden,
        bias_down,
    ) = parts
    (
        embedded,
        normed_low,
        qkv_low,
        context_low,
        first_sum,
        first_low,
        slope,
        act_low,
        second_sum,
    ) = saved
    width = embedded.shape[1]
    grad_second, grad_gain_ffn, grad_shift_ffn = norm_back(
        second_sum, gain_ffn, shift_ffn, grad_final
    )
    grad_down_low = grad_second.astype(jnp.bfloat16)
    sums.begin("down", [(grad_down_low, act_low)], down_rows)
    grad_pre_low = (
        project_back(grad_down_low, weight_down) * slope
    ).astype(jnp.bfloat16)
    grad_pre_low = lax.optimization_barrier(grad_pre_low)
    sums.begin("up", [(grad_pre_low, first_low)], stack_rows)
    grad_first = grad_second + project_back(grad_pre_low, weight_up)
    grad_first_sum, grad_gain_attn, grad_shift_attn = norm_back(
        first_sum, gain_attn, shift_attn, grad_first
    )
    grad_out_low = grad_first_sum.astype(jnp.bfloat16)
    grad_context_low = project_back(grad_out_low, weight_out).astype(jnp.bfloat16)
    sums.in_plane(("down", "up"))
    line_sends = line.step(grad_context_low) if line else []
    grad_qkv_low = attend_back(
        qkv_low, grad_context_low, lengths, seqs, *sums.sent("up"), *line_sends
    )
    grad_normed = grad_first_sum + project_back(grad_qkv_low, weight_qkv)
    grad_embed, grad_gain_embed, grad_shift_embed = norm_back(
        embedded, gain_embed, shift_embed, grad_normed
    )
    embed_t = embed_columns(grad_embed)
    sums.begin(
        "attention",
        [(grad_qkv_low, normed_low), (grad_out_low, context_low)],
        stack_rows,
    )
    sums.hold("attention", *(line.arrived() if line else []))
    sums.arrive(("down", "up"))
    if line:
        line.step(*sums.sent("attention"))
    vectors_grad = jnp.concatenate(
        [
            grad_gain_embed,
            grad_shift_embed,
            grad_gain_attn,
            grad_shift_attn,
            grad_gain_ffn,
            grad_shift_ffn,
            column_sum(grad_qkv_low[:, :width]),
            column_sum(grad_qkv_low[:, 2 * width :]),
            column_sum(grad_out_low),
            column_sum(grad_pre_low),
            column_sum(grad_down_low),
        ]
    )
    return (embed_t, vectors_grad)


class WeightSums:
    def __init__(self, near, far, width):
        self.near, self.staged, self.width = near, far == 4, width
        self.state = {}

    def begin(self, name, pairs, rows):
        if not self.staged:
            grads = [weight_grad(grad, given) for grad, given in pairs]
            self.state[name] = (jnp.concatenate(grads, 0), [])
        elif pairs[0][0].shape[1] % (2 * rows) or 2 * rows % 128:
            grads = [weight_grad(grad, given) for grad, given in pairs]
            self.state[name] = begin_pair_sum(jnp.concatenate(grads, 0), rows, self.near)
        else:
            keep, send = weight_sums(pairs, rows)
            shape = (-1, self.near) + keep.shape[1:]
            self.state[name] = (keep.reshape(shape), [send.reshape(shape)])

    def sent(self, name):
        return self.state[name][1] if self.staged else []

    def narrow(self, x):
        parts = [
            x[..., j : j + self.width] for j in range(0, x.shape[-1], self.width)
        ]
        return parts[0] if len(parts) == 1 else jnp.concatenate(parts, -2)

    def in_plane(self, names):
        if not self.staged:
            return
        p = lax.axis_index("fsdp") % self.near
        sends = [[] for _ in range(self.near)]
        for name in names:
            keep, pair_sends = self.state[name]
            arrived = swap(pair_sends[0], "vocab", 1)
            for k in range(self.near):
                part = lax.dynamic_index_in_dim(keep, p ^ k, 1, False)
                part = part + lax.dynamic_index_in_dim(arrived, p ^ k, 1, False).astype(jnp.float32)
                part = part.astype(jnp.bfloat16) if k else part
                sends[k].append(self.narrow(part).reshape(-1, self.width))
        own, *sends = [
            parts[0] if len(parts) == 1 else jnp.concatenate(parts, 0) for parts in sends
        ]
        for name in names:
            self.state[name] = (own, sends)

    def hold(self, name, *needed):
        if self.staged:
            keep, sends = self.state[name]
            self.state[name] = (keep, after(sends, *needed))

    def arrive(self, names):
        if not self.staged:
            return []
        sends = self.state[names[0]][1]
        self.arrived = [swap(send, "fsdp", k) for k, send in enumerate(sends, 1)]
        return self.arrived

    def plane_total(self, name, arrived):
        return added(self.state[name][0], arrived)


def adam(weight_matrix, grad, first, second, rate):
    first = BETA_ONE * first + (1.0 - BETA_ONE) * grad
    second = BETA_TWO * second + (1.0 - BETA_TWO) * grad * grad
    first_hat = first / (1.0 - BETA_ONE**STEP)
    second_hat = second / (1.0 - BETA_TWO**STEP)
    new = weight_matrix - rate * (
        first_hat / (jnp.sqrt(second_hat) + ADAM_EPS) + WEIGHT_DECAY * weight_matrix
    )
    return (first, second, new)


def local(
    token_ids,
    lengths,
    masked_pos,
    teacher,
    stack_index,
    down_index,
    stack_next,
    down_next,
    word_table,
    table_first,
    table_second,
    pos_table,
    pos_first,
    pos_second,
    proj_stack,
    stack_first,
    stack_second,
    ffn_down,
    down_first,
    down_second,
    vectors,
    vectors_first,
    vectors_second,
    head_bias,
    bias_first,
    bias_second_moment,
):
    size = lax.axis_size("fsdp")
    near = math.gcd(4, size)
    far = size // near
    width = proj_stack.shape[1]
    units = ffn_down.shape[1]
    pair_seqs, seq_len = token_ids.shape
    own_seqs = pair_seqs // 2
    own_rows = own_seqs * seq_len
    core = lax.axis_index("vocab")
    place = lax.axis_index("fsdp")
    p = place % near
    vocab_dev, columns = word_table.shape
    part = vocab_dev // near
    mask_slots = masked_pos.shape[1]

    table_t = word_table.T
    all_ids = lax.all_to_all(
        jnp.broadcast_to(token_ids[None], (size, pair_seqs, seq_len)), "fsdp", 0, 0, tiled=True
    ).reshape(size, 2, own_seqs, seq_len)
    local_ids = (
        jnp.concatenate(
            [
                lax.dynamic_index_in_dim(all_ids, core, 1, False),
                lax.dynamic_index_in_dim(all_ids, 1 - core, 1, False),
            ],
            0,
        ).reshape(2 * size * own_seqs, 1, seq_len)
        - core * vocab_dev
    )

    stack_mask = kept(stack_index)
    down_mask = kept(down_index)
    stack_rows = proj_stack.shape[0]
    down_rows = ffn_down.shape[0]
    small_count = vectors.shape[0]
    own_stack = jnp.where(stack_mask, proj_stack, 0.0).astype(jnp.bfloat16)
    own_down = jnp.where(down_mask, ffn_down, 0.0).astype(jnp.bfloat16)
    pos_rows = -(-(columns // 2) // 16) * 16
    own_stack = jnp.concatenate(
        [
            own_stack,
            jnp.pad(
                pos_table.T.astype(jnp.bfloat16),
                ((0, pos_rows - columns // 2), (0, width - seq_len)),
            ),
            jnp.pad(
                vectors.astype(jnp.bfloat16)[None], ((0, 15), (0, width - small_count))
            ),
        ],
        0,
    )
    table_low = table_t.astype(jnp.bfloat16)
    half = size * own_seqs
    table_blocks = table_low.reshape(columns, near, part).transpose(1, 0, 2)
    teacher_blocks = [
        lax.dynamic_slice_in_dim(teacher, (p ^ k) * part, part, 1) for k in range(near)
    ]
    teach_parts = teacher_blocks[:1] + [
        swap(block, "fsdp", k) for k, block in enumerate(teacher_blocks[1:], 1)
    ]
    if far == 4:
        own_stack = after(own_stack, all_ids)
        stack_line = [swap(own_stack, "fsdp", k * near) for k in range(1, far)]
        near_table = exchange(table_blocks, near_groups(near)).reshape(near * columns, part)
        other_found = lookup(table_t, local_ids[half:], own_stack)
        swapped = swap(other_found, "vocab", 1)
        own_found = lookup(table_t, local_ids[:half], other_found, near_table)
        stack_line = jnp.stack([own_stack] + after(stack_line, own_found))
        own_found = own_found + swapped
        stack_pieces = gather_pieces(stack_line)
        tokens_t = exchange(own_found.reshape(size, own_seqs, columns, seq_len), None)
        down_line = exchange(
            after(jnp.broadcast_to(own_down[None], (far,) + own_down.shape), tokens_t),
            far_groups(near),
        )
        own_blocks = exchange(
            jnp.broadcast_to(down_line[None], (near,) + down_line.shape), near_groups(near)
        )
        stack_others = [[swap(piece, "vocab", 1) for piece in half] for half in stack_pieces]
        own_blocks = exchange(
            after(
                jnp.broadcast_to(down_line[None], (near,) + down_line.shape),
                stack_pieces[0][3],
                stack_pieces[1][3],
            ),
            near_groups(near),
        )
        other_blocks = swap(own_blocks, "vocab", 1)
        before_attention = [own_blocks]
        qkv_blocks = 3 * width // stack_rows
        attention_blocks = 4 * width // stack_rows
        weight_qkv, weight_out, weight_up, small = place_blocks(
            [piece for group in (stack_pieces, stack_others) for half in group for piece in half],
            [
                (place ^ ((first + kz) * near + kp)) * 2 + (core ^ kc)
                for kc in range(2)
                for first in (0, far // 2)
                for kp in range(near)
                for kz in range(far // 2)
            ],
            (
                (0, qkv_blocks, 0, stack_rows),
                (qkv_blocks, attention_blocks, 0, stack_rows),
                (attention_blocks, 2 * size, 0, stack_rows),
                (0, 2 * size, stack_rows, pos_rows + 16),
            ),
        )
        weight_qkv = weight_qkv.reshape(-1, width)
        weight_out = weight_out.reshape(-1, width)
        weight_up = weight_up.reshape(-1, width)

        def weight_down_after():
            arrived = [own_blocks, other_blocks]
            (weight_down,) = place_blocks(
                [blocks.reshape((size,) + own_down.shape) for blocks in arrived],
                [
                    (kz * near + kp) * 2 + (core ^ kc)
                    for kc in range(2)
                    for kp in range(near)
                    for kz in range(far)
                ],
                ((0, 2 * size, 0, down_rows),),
            )
            return weight_down.reshape(-1, units)

    else:
        before_attention = []
        stack_all = lax.all_gather(own_stack, BOTH, axis=0)
        dense_stack = stack_all[:, :stack_rows].reshape(-1, width)
        small = stack_all[:, stack_rows:]
        weight_qkv = dense_stack[: 3 * width]
        weight_out = dense_stack[3 * width : 4 * width]
        weight_up = dense_stack[4 * width :]
        weight_down = lax.all_gather(own_down, BOTH, axis=0, tiled=True)

        def weight_down_after():
            return weight_down

        near_table = exchange(table_blocks, near_groups(near)).reshape(near * columns, part)
        found = lookup(table_t, local_ids)
        own_found = found[:half] + swap(found[half:], "vocab", 1)
        tokens_t = exchange(own_found.reshape(size, own_seqs, columns, seq_len), None)
    pos_all_t = small[:, : columns // 2, :seq_len].reshape(width, seq_len)
    vectors_all = small[:, pos_rows, :small_count].reshape(-1)
    parts = split_vectors(vectors_all.astype(jnp.float32), width)

    table_part = far_gather(near_table, near)
    tokens_t = tokens_t.transpose(1, 0, 2, 3).reshape(own_seqs, width, seq_len)
    embedded = (
        tokens_t.transpose(0, 2, 1).astype(jnp.float32)
        + pos_all_t.T.astype(jnp.float32)[None]
    ).reshape(own_rows, width)

    seq_start = place * pair_seqs + core * own_seqs
    own_lengths = lax.dynamic_slice_in_dim(lengths, seq_start, own_seqs)
    final, saved, weight_down = layer_forward(
        embedded,
        own_lengths,
        own_seqs,
        weight_qkv,
        weight_out,
        weight_up,
        weight_down_after,
        parts,
        before_attention,
    )
    own_pos = lax.dynamic_slice_in_dim(masked_pos, seq_start, own_seqs, 0)
    flat_rows = (jnp.arange(own_seqs, dtype=jnp.int32)[:, None] * seq_len + own_pos).reshape(-1)
    picked = jnp.take(final.reshape(own_rows, width), flat_rows, axis=0).astype(jnp.bfloat16)
    rows = join(picked, "vocab", 1).reshape(-1, width)
    rows = in_order(near_exchange(lambda q: rows, near), near).reshape(-1, width)

    bias_part = lax.dynamic_slice_in_dim(head_bias, p * part, part)
    own_place = p.astype(jnp.int32).reshape(1)
    output_logits, stats = head(
        own_place, rows, table_part, bias_part[None], teach_parts, near
    )
    stats = jnp.stack([stats, swap(stats, "vocab", 1)])
    stats = jnp.concatenate(near_exchange(lambda q: stats, near), 0)
    group_start = (place - p) * pair_seqs
    group_pos = lax.dynamic_slice_in_dim(masked_pos, group_start, near * pair_seqs, 0)
    group_lengths = lax.dynamic_slice_in_dim(lengths, group_start, near * pair_seqs)
    group_valid = (group_pos < group_lengths[:, None]).astype(jnp.float32).reshape(near, 1, -1)
    count = jnp.sum((masked_pos < lengths[:, None]).astype(jnp.float32))
    grad_logits, rows_grad, bias_part_grad, divergence = head_back(
        own_place, output_logits, stats, group_valid / count, table_part, teach_parts, near
    )
    group_loss = jnp.sum(divergence * group_valid) / (2 * near)
    rows_grad = halve(rows_grad.reshape(near, 2, -1, width).transpose(1, 0, 2, 3), "vocab", 1)
    rows_sends = [lax.dynamic_index_in_dim(rows_grad, p ^ k, 0, False) for k in range(near)]
    own_rows_grad = tree_sum(
        [rows_sends[0]] + [swap(send, "fsdp", k) for k, send in enumerate(rows_sends[1:], 1)]
    )
    grad_final = (
        jnp.zeros((own_rows, width), jnp.float32)
        .at[flat_rows]
        .add(own_rows_grad)
    )

    bias_full = lax.dynamic_update_slice_in_dim(
        jnp.zeros((vocab_dev,), jnp.float32), bias_part_grad[0], p * part, 0
    )
    head_grad = lax.dot_general(
        rows,
        grad_logits,
        (((0,), (0,)), ((), ())),
        preferred_element_type=jnp.float32,
    ).reshape(far, near, columns, part)
    if far == 4:
        line = FarLine(head_grad, near)
        line_sends = line.step()
        grad_final = after(grad_final, *line_sends)
    else:
        line = None

    def embed_columns(grad_embed):
        embed_t = grad_embed.reshape(own_seqs, seq_len, width).astype(jnp.bfloat16)
        embed_t = embed_t.transpose(0, 2, 1).reshape(own_seqs, size, columns, seq_len)
        return embed_t.transpose(1, 0, 2, 3)

    sums = WeightSums(near, far, width)
    embed_t, vectors_grad = layer_backward(
        grad_final,
        saved,
        own_lengths,
        own_seqs,
        weight_qkv,
        weight_out,
        weight_up,
        weight_down,
        parts,
        sums,
        line,
        embed_columns,
        stack_rows,
        down_rows,
    )

    embed_t = lax.all_to_all(embed_t, "fsdp", 0, 0, tiled=True).reshape(half, columns, seq_len)
    if far == 4:
        first_plane = sums.plane_total("up", sums.arrived)
        down_plane = first_plane[: far * (units // width) * down_rows].reshape(far, -1, width)
        up_plane = first_plane[far * (units // width) * down_rows :].reshape(-1, stack_rows, width)
        sums.in_plane(("attention",))
        attention_sends = sums.sent("attention")
        other_t = swap(embed_t, "vocab", 1)
        token_grad = spread_add(embed_t, local_ids[:half], vocab_dev, other_t, *attention_sends)
        head_grad = line.total(token_grad)
        blocks_sent = [
            lax.dynamic_index_in_dim(head_grad, p ^ k, 0, False) for k in range(near)
        ]
        blocks = [swap(block, "fsdp", k) for k, block in enumerate(blocks_sent[1:], 1)]
        attention_plane = sums.plane_total(
            "attention", after(sums.arrive(("attention",)), token_grad)
        ).reshape(-1, stack_rows, width)
        own = jnp.concatenate(
            [jnp.concatenate([attention_plane, up_plane], 0), down_plane], 1
        )
        far_low = own.astype(jnp.bfloat16)
        arrived = exchange(far_low, far_groups(near))
        last_grad = spread_add(
            other_t, local_ids[half:], vocab_dev, far_low, *blocks_sent
        )
        blocks = blocks_sent[:1] + after(blocks, last_grad)
        token_grad = token_grad + last_grad
        vectors_grad = after(vectors_grad, far_low)
        vectors_grad = vectors_grad + swap(vectors_grad, "vocab", 1)
        small_sums = jnp.concatenate([bias_full, vectors_grad])
        small_sums = tree_sum(near_exchange(lambda q: small_sums, near))
        small_sums = sum_far(small_sums, near)
        z = place // near
        other = lax.broadcasted_iota(jnp.int32, (far, 1, 1), 0) != z
        total = jnp.sum(jnp.where(other, arrived.astype(jnp.float32), own), axis=0)
        stack_total = total[:stack_rows]
        down_total = jnp.concatenate(
            jnp.split(total[stack_rows:], units // width, axis=0), 1
        )
        embed_t = jnp.concatenate([embed_t, other_t], 0)
    else:
        embed_t = jnp.concatenate([embed_t, swap(embed_t, "vocab", 1)], 0)
        token_grad = spread_add(embed_t, local_ids, vocab_dev)
        vectors_grad = vectors_grad + swap(vectors_grad, "vocab", 1)
        small_sums = jnp.concatenate([bias_full, vectors_grad])
        small_sums = tree_sum(near_exchange(lambda q: small_sums, near))
        small_sums = sum_far(small_sums, near)
        head_grad = far_reduce(head_grad, near)
        blocks = near_exchange(lambda q: lax.dynamic_index_in_dim(head_grad, q, 0, False), near)
        stack_grad = [sums.state[name][0] for name in ("attention", "up")]
        stack_total = lax.psum_scatter(
            jnp.concatenate(stack_grad, 0), BOTH, scatter_dimension=0, tiled=True
        )
        down_total = lax.psum_scatter(
            sums.state["down"][0], BOTH, scatter_dimension=0, tiled=True
        )
    bias_grad, vectors_grad = small_sums[:vocab_dev], small_sums[vocab_dev:]
    head_grad_t = jnp.concatenate(list(in_order(blocks, near)), 1).astype(jnp.float32)
    table_total = head_grad_t + token_grad
    pos_total = jnp.sum(embed_t.astype(jnp.float32), axis=0)
    pos_total = lax.dynamic_slice_in_dim(pos_total, core * (columns // 2), columns // 2, 0)
    vectors_total = lax.dynamic_slice_in_dim(
        vectors_grad, (2 * place + core) * small_count, small_count
    )

    stack_total = stack_total + jnp.where(stack_mask, 0.0, PRUNE_DECAY) * proj_stack
    down_total = down_total + jnp.where(down_mask, 0.0, PRUNE_DECAY) * ffn_down
    changes = jnp.sum((stack_mask != kept(stack_next)).astype(jnp.float32)) + jnp.sum(
        (down_mask != kept(down_next)).astype(jnp.float32)
    )
    squares = (
        jnp.sum(stack_total * stack_total)
        + jnp.sum(down_total * down_total)
        + jnp.sum(pos_total * pos_total)
        + jnp.sum(vectors_total * vectors_total)
        + jnp.sum(table_total * table_total)
        + jnp.sum(bias_grad * bias_grad) / size
    )
    scalars = jnp.stack([squares, group_loss, changes])
    scalars = sum_all(scalars, near)
    total_squares, loss_sum, change_total = scalars[0], scalars[1], scalars[2]
    grad_norm = jnp.sqrt(total_squares)
    factor = jnp.minimum(1.0, CLIP / (grad_norm + 1e-06))
    table_out = adam(table_t, table_total * factor, table_first.T, table_second.T, RATE_MATRIX)
    pos_out = adam(pos_table.T, pos_total * factor, pos_first.T, pos_second.T, RATE_MATRIX)
    stack_out = adam(proj_stack, stack_total * factor, stack_first, stack_second, RATE_MATRIX)
    down_out = adam(ffn_down, down_total * factor, down_first, down_second, RATE_MATRIX)
    vectors_out = adam(vectors, vectors_total * factor, vectors_first, vectors_second, RATE_VECTOR)
    bias_out = adam(head_bias, bias_grad * factor, bias_first, bias_second_moment, RATE_VECTOR)
    return (
        table_out[0].T,
        table_out[1].T,
        table_out[2].T,
        pos_out[0].T,
        pos_out[1].T,
        pos_out[2].T,
        stack_out[0],
        stack_out[1],
        stack_out[2],
        down_out[0],
        down_out[1],
        down_out[2],
        vectors_out[0],
        vectors_out[1],
        vectors_out[2],
        bias_out[0],
        bias_out[1],
        bias_out[2],
        loss_sum,
        count,
        grad_norm,
        change_total.astype(jnp.int32),
    )


def solution(mesh):
    in_specs = (
        P("fsdp", None),
        P(),
        P(),
        P("fsdp", "vocab"),
        P(("fsdp", "vocab"), None),
        P(("fsdp", "vocab"), None),
        P(("fsdp", "vocab"), None),
        P(("fsdp", "vocab"), None),
        P("vocab", "fsdp"),
        P("vocab", "fsdp"),
        P("vocab", "fsdp"),
        P(None, ("fsdp", "vocab")),
        P(None, ("fsdp", "vocab")),
        P(None, ("fsdp", "vocab")),
        P(("fsdp", "vocab"), None),
        P(("fsdp", "vocab"), None),
        P(("fsdp", "vocab"), None),
        P(("fsdp", "vocab"), None),
        P(("fsdp", "vocab"), None),
        P(("fsdp", "vocab"), None),
        P(("fsdp", "vocab")),
        P(("fsdp", "vocab")),
        P(("fsdp", "vocab")),
        P("vocab"),
        P("vocab"),
        P("vocab"),
    )
    out_specs = (
        P("vocab", "fsdp"),
        P("vocab", "fsdp"),
        P("vocab", "fsdp"),
        P(None, ("fsdp", "vocab")),
        P(None, ("fsdp", "vocab")),
        P(None, ("fsdp", "vocab")),
        P(("fsdp", "vocab"), None),
        P(("fsdp", "vocab"), None),
        P(("fsdp", "vocab"), None),
        P(("fsdp", "vocab"), None),
        P(("fsdp", "vocab"), None),
        P(("fsdp", "vocab"), None),
        P(("fsdp", "vocab")),
        P(("fsdp", "vocab")),
        P(("fsdp", "vocab")),
        P("vocab"),
        P("vocab"),
        P("vocab"),
        P(),
        P(),
        P(),
        P(),
    )
    return jax.shard_map(local, mesh=mesh, in_specs=in_specs, out_specs=out_specs, check_vma=False)
```

```python
import functools
import math

import jax
import jax.numpy as jnp
from jax import lax
from jax.experimental import pallas as pl
from jax.experimental.pallas import tpu as pltpu
from jax.sharding import PartitionSpec as P

HEAD_DIM = 64
STEP = 10


NORM_EPS = 1e-05
CLIP = 0.005
PRUNE_DECAY = 0.0002
BETA_ONE = 0.9
BETA_TWO = 0.999
ADAM_EPS = 1e-08
WEIGHT_DECAY = 0.01
RATE_MATRIX = 0.1
RATE_VECTOR = 1.0
SCORE_SCALE = 0.125


HIGH_COUNT = 512
COST = pl.CostEstimate(flops=1, bytes_accessed=1, transcendentals=0)
BOTH = ("fsdp", "vocab")


def kept(words):
    columns = words.shape[1] * 16
    place = lax.broadcasted_iota(jnp.int32, (2 * words.shape[1], columns), 0)
    column = lax.broadcasted_iota(jnp.int32, (2 * words.shape[1], columns), 1)
    spread = (place % words.shape[1] * 2 + place // words.shape[1] == column // 8).astype(
        jnp.bfloat16
    )
    bytes_low = jnp.concatenate([words & 255, words >> 8], 1).astype(jnp.bfloat16)
    byte = jnp.dot(bytes_low, spread, preferred_element_type=jnp.float32).astype(jnp.int32)
    spot = lax.broadcasted_iota(jnp.int32, byte.shape, 1)
    nibble = jnp.where(spot % 8 < 4, byte & 15, byte >> 4)
    spot = spot % 4
    return ((nibble & 3) == spot) | ((nibble >> 2) == spot)


def swap(x, axis, bit):
    size = lax.axis_size(axis)
    return lax.ppermute(x, axis, [(i, i ^ bit) for i in range(size)])


def my_bit(axis, bit):
    return lax.axis_index(axis) // bit % 2


def bits_of(size):
    return [1 << k for k in range(size.bit_length() - 1)]


def gate_kernel(*refs):
    pass


def after(x, *needed):
    if not needed:
        return x
    parts = x if isinstance(x, list) else [x]
    anywhere = pl.BlockSpec(memory_space=pl.ANY)
    outs = pl.pallas_call(
        gate_kernel,
        in_specs=[anywhere] * (len(parts) + len(needed)),
        out_specs=[anywhere] * len(parts),
        out_shape=[jax.ShapeDtypeStruct(part.shape, part.dtype) for part in parts],
        input_output_aliases={i: i for i in range(len(parts))},
        name="gate",
    )(*parts, *needed)
    return list(outs) if isinstance(x, list) else outs[0]


def tree_sum(parts):
    while len(parts) > 1:
        parts = [one + two for one, two in zip(parts[::2], parts[1::2])]
    return parts[0]


def sum_all(x, near):
    x = x + swap(x, "vocab", 1)
    x = tree_sum(near_exchange(lambda q: x, near))
    return sum_far(x, near)


def sum_far(x, near):
    far = lax.axis_size("fsdp") // near
    if far == 4:
        return tree_sum([x] + [swap(x, "fsdp", k * near) for k in range(1, far)])
    for bit in bits_of(far):
        x = x + swap(x, "fsdp", bit * near)
    return x


def join(x, axis, bit):
    other = swap(x, axis, bit)
    upper = my_bit(axis, bit) == 1
    return jnp.stack([jnp.where(upper, other, x), jnp.where(upper, x, other)])


def halve(x, axis, bit):
    mine = my_bit(axis, bit)
    return lax.dynamic_index_in_dim(x, mine, 0, False) + swap(
        lax.dynamic_index_in_dim(x, 1 - mine, 0, False), axis, bit
    )


def near_exchange(take, near):
    size = lax.axis_size("fsdp")
    p = lax.axis_index("fsdp") % near
    return [take(p)] + [
        lax.ppermute(take(p ^ k), "fsdp", [(i, i ^ k) for i in range(size)]) for k in range(1, near)
    ]


def far_groups(near):
    size = lax.axis_size("fsdp")
    return [list(range(q, size, near)) for q in range(near)]


def near_groups(near):
    size = lax.axis_size("fsdp")
    return [list(range(start, start + near)) for start in range(0, size, near)]


def exchange(x, groups):
    return lax.all_to_all(x, "fsdp", 0, 0, tiled=True, axis_index_groups=groups)


def far_gather(x, near):
    return lax.all_gather(x, "fsdp", axis=0, tiled=True, axis_index_groups=far_groups(near))


class FarLine:
    def __init__(self, x, near):
        self.x, self.near = x, near
        self.far = 4
        self.z = lax.axis_index("fsdp") // near
        self.k = 0
        self.up = self.down = None

    def entry(self, j):
        return lax.dynamic_index_in_dim(self.x, jnp.clip(j, 0, self.far - 1), 0, False)

    def arrived(self):
        return [self.up, self.down]

    def step(self, *needed):
        self.k += 1
        k, near, size = self.k, self.near, self.far * self.near
        send_up = self.entry(self.far - k + self.z)
        send_down = self.entry(self.z - self.far + k)
        if k > 1:
            up, down = after([self.up, self.down], *needed) if needed else (self.up, self.down)
            send_up, send_down = send_up + up, send_down + down
        sends = [send_up.astype(jnp.bfloat16), send_down.astype(jnp.bfloat16)]
        self.up = lax.ppermute(sends[0], "fsdp", [(i, i + near) for i in range(k * near)])
        self.down = lax.ppermute(
            sends[1], "fsdp", [(i, i - near) for i in range(size - k * near, size)]
        )
        return sends

    def total(self, *needed):
        up, down = after([self.up, self.down], *needed)
        return self.entry(self.z) + up + down


def far_sends(x, near):
    far = lax.axis_size("fsdp") // near
    z = lax.axis_index("fsdp") // near
    sends = [
        lax.dynamic_index_in_dim(x, z ^ k, 0, False).astype(jnp.bfloat16) for k in range(1, far)
    ]
    return lax.dynamic_index_in_dim(x, z, 0, False), sends


def far_arrive(sends, near):
    return [swap(send, "fsdp", k * near) for k, send in enumerate(sends, 1)]


def added(own, parts):
    for part in parts:
        own = own + part.astype(jnp.float32)
    return own


def far_reduce(x, near):
    return lax.psum_scatter(
        x, "fsdp", scatter_dimension=0, tiled=True, axis_index_groups=far_groups(near)
    )[0]


def begin_pair_sum(grad, rows, near):
    core = lax.axis_index("vocab")
    grad = grad.reshape(-1, near, 2, rows, grad.shape[-1])
    send = lax.dynamic_index_in_dim(grad, 1 - core, 2, False).astype(jnp.bfloat16)
    return (lax.dynamic_index_in_dim(grad, core, 2, False), [send])


def weight_kernel(counts, core_ref, *refs):
    keep_ref, send_ref = refs[-2:]
    step, first = pl.program_id(0), 0
    rows = keep_ref.shape[1]
    mine = core_ref[0] == 0
    for i, count in enumerate(counts):

        def put(grad_ref=refs[2 * i], input_ref=refs[2 * i + 1]):
            product = lax.dot_general(
                grad_ref[...],
                input_ref[...],
                (((0,), (0,)), ((), ())),
                preferred_element_type=jnp.float32,
            )
            one, two = product[:rows], product[rows:]
            keep_ref[0] = jnp.where(mine, one, two)
            send_ref[0] = jnp.where(mine, two, one).astype(send_ref.dtype)

        pl.when((step >= first) & (step < first + count))(put)
        first += count


def weight_sums(pairs, rows):
    width = pairs[0][1].shape[1]
    counts = [grad.shape[1] // (2 * rows) for grad, _ in pairs]
    total = sum(counts)
    specs, operands, first = [], [], 0
    for (grad, given), count in zip(pairs, counts):
        specs.append(
            pl.BlockSpec(
                (grad.shape[0], 2 * rows),
                lambda i, _, first=first, count=count: (0, jnp.clip(i - first, 0, count - 1)),
            )
        )
        specs.append(pl.BlockSpec(given.shape, lambda i, _: (0, 0)))
        operands += [grad, given]
        first += count
    return pl.pallas_call(
        functools.partial(weight_kernel, counts),
        grid_spec=pltpu.PrefetchScalarGridSpec(
            num_scalar_prefetch=1,
            grid=(total,),
            in_specs=specs,
            out_specs=[pl.BlockSpec((1, rows, width), lambda i, _: (i, 0, 0))] * 2,
        ),
        out_shape=[
            jax.ShapeDtypeStruct((total, rows, width), jnp.float32),
            jax.ShapeDtypeStruct((total, rows, width), jnp.bfloat16),
        ],
        compiler_params=pltpu.CompilerParams(vmem_limit_bytes=40 * 1024 * 1024),
        name="weight_sums",
    )(lax.axis_index("vocab").astype(jnp.int32).reshape(1), *operands)


def in_order(parts, near):
    p = lax.axis_index("fsdp") % near
    stacked = []
    for q in range(near):
        entry = parts[0]
        for k in range(1, near):
            entry = jnp.where(p ^ k == q, parts[k], entry)
        stacked.append(entry)
    return jnp.stack(stacked)


def place_kernel(spans, blocks, order_ref, *refs):
    pieces, outs = refs[: -len(spans)], refs[-len(spans) :]
    for i, piece in enumerate(pieces):
        for kz in range(blocks):
            block = order_ref[i * blocks + kz]
            for out, (first, last, start, rows) in zip(outs, spans):

                def put(piece=piece, kz=kz, block=block, out=out, first=first, start=start, rows=rows):
                    out[block - first] = piece[kz, start : start + rows]

                if first == 0 and last == len(pieces) * blocks:
                    put()
                else:
                    pl.when((block >= first) & (block < last))(put)


def gather_pieces(line):
    half = line.shape[0] // 2
    one, two = line[:half], line[half:]
    one_x, two_y = swap(one, "fsdp", 1), swap(two, "fsdp", 2)
    one_y, two_x = swap(one, "fsdp", 2), swap(two, "fsdp", 1)
    one_xy, two_xy = swap(one_x, "fsdp", 2), swap(two_y, "fsdp", 1)
    return [[one, one_x, one_y, one_xy], [two, two_x, two_y, two_xy]]


def place_blocks(pieces, order, spans):
    width = pieces[0].shape[-1]
    return pl.pallas_call(
        functools.partial(place_kernel, spans, pieces[0].shape[0]),
        grid_spec=pltpu.PrefetchScalarGridSpec(
            num_scalar_prefetch=1,
            grid=(1,),
            in_specs=[pl.BlockSpec(memory_space=pltpu.VMEM)] * len(pieces),
            out_specs=[pl.BlockSpec(memory_space=pltpu.VMEM)] * len(spans),
        ),
        out_shape=[
            jax.ShapeDtypeStruct((last - first, rows, width), pieces[0].dtype)
            for first, last, _, rows in spans
        ],
        compiler_params=pltpu.CompilerParams(vmem_limit_bytes=40 * 1024 * 1024),
        name="place",
    )(jnp.stack(order).astype(jnp.int32), *pieces)


def lookup_kernel(low_count, ids_ref, table_ref, *refs):
    out_ref, spread = refs[-2:]
    width = table_ref.shape[0]

    @pl.when(pl.program_id(0) == 0)
    def _():
        for low in range(low_count):
            spread[low * width : (low + 1) * width, :] = table_ref[
                :, low * HIGH_COUNT : (low + 1) * HIGH_COUNT
            ].astype(jnp.bfloat16)

    for block in range(ids_ref.shape[0]):
        ids = ids_ref[block]
        low_ids = ids >> 9
        row = lax.broadcasted_iota(jnp.int32, (HIGH_COUNT, ids.shape[1]), 0)
        match = (row == (ids & (HIGH_COUNT - 1))).astype(jnp.bfloat16)
        found = jnp.dot(spread[...], match, preferred_element_type=jnp.float32)
        total = jnp.zeros((width, ids.shape[1]), jnp.float32)
        for low in range(low_count):
            total = jnp.where(low_ids == low, found[low * width : (low + 1) * width, :], total)
        out_ref[block] = total.astype(out_ref.dtype)


def lookup(table_t, ids, *needed):
    rows = table_t.shape[0]
    table_t = jnp.pad(table_t, ((0, -rows % 16), (0, 0)))
    width, vocab = table_t.shape
    blocks, _, length = ids.shape
    low_count = vocab // HIGH_COUNT
    group = math.gcd(2, blocks)
    found = pl.pallas_call(
        functools.partial(lookup_kernel, low_count),
        grid=(blocks // group,),
        in_specs=[
            pl.BlockSpec((group, 1, length), lambda i: (i, 0, 0)),
            pl.BlockSpec((width, vocab), lambda i: (0, 0)),
        ]
        + [pl.BlockSpec(memory_space=pl.ANY)] * len(needed),
        out_specs=pl.BlockSpec((group, width, length), lambda i: (i, 0, 0)),
        out_shape=jax.ShapeDtypeStruct((blocks, width, length), jnp.bfloat16),
        scratch_shapes=[pltpu.VMEM((low_count * width, HIGH_COUNT), jnp.bfloat16)],
        compiler_params=pltpu.CompilerParams(vmem_limit_bytes=40 * 1024 * 1024),
        cost_estimate=pl.CostEstimate(
            flops=2 * blocks * length * width * vocab,
            bytes_accessed=4 * width * vocab + 2 * blocks * width * length,
            transcendentals=0,
        ),
        name="lookup",
    )(ids, table_t, *needed)
    return found[:, :rows]


def spread_kernel(low_count, ids_ref, grad_ref, *refs):
    out_ref, lhs, total = refs[-3:]
    width = grad_ref.shape[1]
    step = pl.program_id(0)

    @pl.when(step == 0)
    def _():
        total[...] = jnp.zeros_like(total)

    length = ids_ref.shape[2]
    matches = []
    for block in range(ids_ref.shape[0]):
        ids = ids_ref[block]
        low_ids = ids >> 9
        grad = grad_ref[block].astype(jnp.float32)
        part = slice(block * length, (block + 1) * length)
        for low in range(low_count):
            lhs[low * width : (low + 1) * width, part] = jnp.where(low_ids == low, grad, 0.0).astype(
                jnp.bfloat16
            )
        row = lax.broadcasted_iota(jnp.int32, (HIGH_COUNT, length), 0)
        matches.append((row == (ids & (HIGH_COUNT - 1))).astype(jnp.bfloat16))
    match = jnp.concatenate(matches, 1)
    total[...] += lax.dot_general(
        lhs[...], match, (((1,), (1,)), ((), ())), preferred_element_type=jnp.float32
    )

    @pl.when(step == pl.num_programs(0) - 1)
    def _():
        for low in range(low_count):
            span = slice(low * HIGH_COUNT, (low + 1) * HIGH_COUNT)
            out_ref[:, span] = total[low * width : (low + 1) * width, :]


def spread_add(grads, ids, vocab, *needed):
    rows = grads.shape[1]
    grads = jnp.pad(grads, ((0, 0), (0, -rows % 16), (0, 0)))
    width = grads.shape[1]
    blocks, _, length = ids.shape
    low_count = vocab // HIGH_COUNT
    group = math.gcd(2, blocks)
    summed = pl.pallas_call(
        functools.partial(spread_kernel, low_count),
        grid=(blocks // group,),
        in_specs=[
            pl.BlockSpec((group, 1, length), lambda i: (i, 0, 0)),
            pl.BlockSpec((group, width, length), lambda i: (i, 0, 0)),
        ]
        + [pl.BlockSpec(memory_space=pl.ANY)] * len(needed),
        out_specs=pl.BlockSpec((width, vocab), lambda i: (0, 0)),
        out_shape=jax.ShapeDtypeStruct((width, vocab), jnp.float32),
        scratch_shapes=[
            pltpu.VMEM((low_count * width, group * length), jnp.bfloat16),
            pltpu.VMEM((low_count * width, HIGH_COUNT), jnp.float32),
        ],
        compiler_params=pltpu.CompilerParams(vmem_limit_bytes=40 * 1024 * 1024),
        cost_estimate=COST,
        name="spread_add",
    )(ids, grads, *needed)
    return summed[:rows]


def split_vectors(vectors_all, width):
    hidden_units = vectors_all.shape[0] - 10 * width
    pieces = []
    offset = 0
    for piece_len in [width] * 9 + [hidden_units, width]:
        pieces.append(vectors_all[offset : offset + piece_len])
        offset = offset + piece_len
    return pieces


def layer_norm(input_batch, gain, shift):
    center = input_batch - jnp.mean(input_batch, axis=-1, keepdims=True)
    spread = jnp.mean(center * center, axis=-1, keepdims=True)
    return center * lax.rsqrt(spread + NORM_EPS) * gain + shift


def norm_back(input_batch, gain, shift, gradient_tree):
    unused, pull = jax.vjp(layer_norm, input_batch, gain, shift)
    return pull(gradient_tree)


def project(input_batch, weight_matrix):
    return jnp.einsum("mh,ph->mp", input_batch, weight_matrix, preferred_element_type=jnp.float32)


def project_back(gradient, weight_matrix):
    return jnp.einsum("az,zh->ah", gradient, weight_matrix, preferred_element_type=jnp.float32)


def weight_grad(gradient, input_batch):
    return jnp.einsum("bu,bw->uw", gradient, input_batch, preferred_element_type=jnp.float32)


def column_sum(gradient):
    return jnp.sum(gradient.astype(jnp.float32), axis=0)


STRIP = 128
HEADS_STEP = 6
HELD = 3


def across(one, two):
    return lax.dot_general(one, two, (((1,), (1,)), ((), ())), preferred_element_type=jnp.float32)


def down(one, two):
    return lax.dot_general(one, two, (((0,), (0,)), ((), ())), preferred_element_type=jnp.float32)


def soften(raw, live):
    scores = jnp.where(live, raw, -1e30)
    powers = jnp.exp(scores - jnp.max(scores, axis=0, keepdims=True))
    return powers * (1.0 / jnp.sum(powers, axis=0, keepdims=True))


def attend_kernel(lengths_ref, query_ref, key_ref, value_ref, *refs):
    out_ref, scores, probs = refs[-3:]
    length = lengths_ref[pl.program_id(0)]
    rows = query_ref.shape[0]
    live = lax.broadcasted_iota(jnp.int32, (rows, 1), 0) < length
    contexts = []
    for head in range(query_ref.shape[1] // HEAD_DIM):
        span = slice(head * HEAD_DIM, (head + 1) * HEAD_DIM)
        scores[head % HELD] = across(key_ref[:, span], query_ref[:, span] * SCORE_SCALE)
        for start in range(0, rows, STRIP):
            part = slice(start, start + STRIP)
            probs[head % HELD, :, part] = soften(scores[head % HELD, :, part], live).astype(jnp.bfloat16)
        contexts.append(down(value_ref[:, span], probs[head % HELD]))
    out_ref[...] = jnp.concatenate(contexts, 0).T.astype(out_ref.dtype)


def attend(qkv, lengths, seqs, *needed):
    rows, total = qkv.shape
    seq_len, width = rows // seqs, total // 3
    lanes = HEADS_STEP * HEAD_DIM
    blocks = width // lanes

    def part(which):
        return pl.BlockSpec((seq_len, lanes), lambda s, j, _: (s, which * blocks + j))

    return pl.pallas_call(
        attend_kernel,
        grid_spec=pltpu.PrefetchScalarGridSpec(
            num_scalar_prefetch=1,
            grid=(seqs, blocks),
            in_specs=[part(0), part(1), part(2)]
            + [pl.BlockSpec(memory_space=pl.ANY)] * len(needed),
            out_specs=pl.BlockSpec((seq_len, lanes), lambda s, j, _: (s, j)),
            scratch_shapes=[
                pltpu.VMEM((HELD, seq_len, seq_len), jnp.float32),
                pltpu.VMEM((HELD, seq_len, seq_len), jnp.bfloat16),
            ],
        ),
        out_shape=jax.ShapeDtypeStruct((rows, width), jnp.bfloat16),
        compiler_params=pltpu.CompilerParams(vmem_limit_bytes=40 * 1024 * 1024),
        cost_estimate=COST,
        name="attend",
    )(lengths, qkv, qkv, qkv, *needed)


def attend_back_kernel(lengths_ref, query_ref, key_ref, value_ref, grad_ref, *refs):
    out_ref, scores, grad_probs, probs, grads = refs[-5:]
    length = lengths_ref[pl.program_id(0)]
    step = pl.program_id(1)
    width = out_ref.shape[1] // 3
    rows, lanes = query_ref.shape
    live = lax.broadcasted_iota(jnp.int32, (rows, 1), 0) < length
    parts = [[], [], []]
    for head in range(lanes // HEAD_DIM):
        span = slice(head * HEAD_DIM, (head + 1) * HEAD_DIM)
        query, key_rows, grad_out = query_ref[:, span], key_ref[:, span], grad_ref[:, span]
        scores[head % HELD] = across(key_rows, query * SCORE_SCALE)
        grad_probs[head % HELD] = across(value_ref[:, span], grad_out)
        for start in range(0, rows, STRIP):
            part = slice(start, start + STRIP)
            prob = soften(scores[head % HELD, :, part], live)
            grad_prob = grad_probs[head % HELD, :, part]
            mean = jnp.sum(prob * grad_prob, axis=0, keepdims=True)
            probs[head % HELD, :, part] = prob.astype(jnp.bfloat16)
            grads[head % HELD, :, part] = (prob * (grad_prob - mean)).astype(jnp.bfloat16)
        parts[0].append(down(key_rows, grads[head % HELD]) * SCORE_SCALE)
        parts[1].append(
            jnp.dot(grads[head % HELD], query, preferred_element_type=jnp.float32) * SCORE_SCALE
        )
        parts[2].append(jnp.dot(probs[head % HELD], grad_out, preferred_element_type=jnp.float32))
    merged = [jnp.concatenate(parts[0], 0).T] + [jnp.concatenate(part, 1) for part in parts[1:]]
    for which, gradient in enumerate(merged):
        start = pl.multiple_of(which * width + step * lanes, lanes)
        out_ref[:, pl.ds(start, lanes)] = gradient.astype(out_ref.dtype)


def attend_back(qkv, grad_context, lengths, seqs, *needed):
    rows, total = qkv.shape
    seq_len, width = rows // seqs, total // 3
    lanes = HEADS_STEP * HEAD_DIM
    blocks = width // lanes

    def part(which):
        return pl.BlockSpec((seq_len, lanes), lambda s, j, _: (s, which * blocks + j))

    return pl.pallas_call(
        attend_back_kernel,
        grid_spec=pltpu.PrefetchScalarGridSpec(
            num_scalar_prefetch=1,
            grid=(seqs, blocks),
            in_specs=[part(0), part(1), part(2), part(0)]
            + [pl.BlockSpec(memory_space=pl.ANY)] * len(needed),
            out_specs=pl.BlockSpec((seq_len, total), lambda s, j, _: (s, 0)),
            scratch_shapes=[
                pltpu.VMEM((HELD, seq_len, seq_len), kind)
                for kind in (jnp.float32, jnp.float32, jnp.bfloat16, jnp.bfloat16)
            ],
        ),
        out_shape=jax.ShapeDtypeStruct((rows, total), jnp.bfloat16),
        compiler_params=pltpu.CompilerParams(vmem_limit_bytes=40 * 1024 * 1024),
        cost_estimate=COST,
        name="attend_back",
    )(lengths, qkv, qkv, qkv, grad_context, *needed)


def teacher_rows(place_ref, parts, held):
    which = place_ref[0] ^ pl.program_id(0)
    for k, part_ref in enumerate(parts):

        def hold(part_ref=part_ref):
            held[...] = part_ref[...]

        pl.when(which == k)(hold)


HEAD_STRIP = 16


def head_kernel(place_ref, rows_ref, table_ref, bias_ref, *refs):
    parts, (logits_ref, stats_ref, held, packed) = refs[:-4], refs[-4:]
    teacher_rows(place_ref, parts, held)
    logits_ref[...] = (
        jnp.dot(rows_ref[...], table_ref[...], preferred_element_type=jnp.float32) + bias_ref[...]
    )
    lane = lax.broadcasted_iota(jnp.int32, (HEAD_STRIP, 128), 1)
    for row in range(0, held.shape[0], HEAD_STRIP):
        part = slice(row, row + HEAD_STRIP)
        logits = logits_ref[part, :]
        student_top = jnp.max(logits, axis=-1, keepdims=True)
        student_total = jnp.sum(jnp.exp(logits - student_top), axis=-1, keepdims=True)
        teach = held[part, :].astype(jnp.float32)
        teacher_top = jnp.max(teach, axis=-1, keepdims=True)
        weighted = jnp.exp(teach - teacher_top)
        teacher_total = jnp.sum(weighted, axis=-1, keepdims=True)
        cross = jnp.sum(weighted * (teach - logits), axis=-1, keepdims=True)
        stats = jnp.zeros((HEAD_STRIP, 128), jnp.float32)
        for i, stat in enumerate((student_top, student_total, teacher_top, teacher_total, cross)):
            stats = jnp.where(lane == i, stat, stats)
        packed[part, :] = stats
    stats_ref[0] = packed[...].T[:8]


def head(place, rows, table_part, bias_part, teach_parts, near):
    count, width = rows.shape
    vocab = table_part.shape[1]
    block = count // near
    whole = pl.BlockSpec((block, vocab), lambda i, _: (0, 0))
    return pl.pallas_call(
        head_kernel,
        grid_spec=pltpu.PrefetchScalarGridSpec(
            num_scalar_prefetch=1,
            grid=(near,),
            in_specs=[
                pl.BlockSpec((block, width), lambda i, _: (i, 0)),
                pl.BlockSpec((width, vocab), lambda i, _: (0, 0)),
                pl.BlockSpec((1, vocab), lambda i, _: (0, 0)),
            ]
            + [whole] * near,
            out_specs=[
                pl.BlockSpec((block, vocab), lambda i, _: (i, 0)),
                pl.BlockSpec((1, 8, block), lambda i, _: (i, 0, 0)),
            ],
            scratch_shapes=[
                pltpu.VMEM((block, vocab), jnp.bfloat16),
                pltpu.VMEM((block, 128), jnp.float32),
            ],
        ),
        out_shape=[
            jax.ShapeDtypeStruct((count, vocab), jnp.float32),
            jax.ShapeDtypeStruct((near, 8, block), jnp.float32),
        ],
        compiler_params=pltpu.CompilerParams(vmem_limit_bytes=56 * 1024 * 1024),
        cost_estimate=COST,
        name="head",
    )(place, rows, table_part, bias_part, *teach_parts)


def head_back_kernel(place_ref, logits_ref, stats_ref, scale_ref, table_ref, *refs):
    parts, (grad_ref, rows_ref, bias_ref, loss_ref, held) = refs[:-5], refs[-5:]
    teacher_rows(place_ref, parts, held)
    step = pl.program_id(0)
    stats = stats_ref[:, 0]
    tops, totals, teacher_tops, teacher_totals, crosses = (stats[:, i] for i in range(5))
    top = jnp.max(tops, axis=0, keepdims=True)
    total = jnp.sum(totals * jnp.exp(tops - top), axis=0, keepdims=True)
    teacher_top = jnp.max(teacher_tops, axis=0, keepdims=True)
    teacher_scale = jnp.exp(teacher_tops - teacher_top)
    teacher_total = jnp.sum(teacher_totals * teacher_scale, axis=0, keepdims=True)
    cross = jnp.sum(crosses * teacher_scale, axis=0, keepdims=True)
    student_lse = top + jnp.log(total)
    teacher_lse = teacher_top + jnp.log(teacher_total)
    loss_ref[0] = cross / teacher_total - teacher_lse + student_lse
    packed = jnp.concatenate(
        [student_lse, teacher_lse, scale_ref[0], jnp.zeros((5, top.shape[1]), jnp.float32)], 0
    ).T

    @pl.when(step == 0)
    def _():
        bias_ref[...] = jnp.zeros_like(bias_ref)

    for row in range(0, held.shape[0], HEAD_STRIP):
        part = slice(row, row + HEAD_STRIP)
        student = jnp.exp(logits_ref[part, :] - packed[part, 0:1])
        teach = jnp.exp(held[part, :].astype(jnp.float32) - packed[part, 1:2])
        grad = ((student - teach) * packed[part, 2:3]).astype(jnp.bfloat16)
        grad_ref[part, :] = grad
        bias_ref[...] += jnp.sum(grad.astype(jnp.float32), axis=0, keepdims=True)
    rows_ref[...] = lax.dot_general(
        grad_ref[...], table_ref[...], (((1,), (1,)), ((), ())), preferred_element_type=jnp.float32
    )


def head_back(place, logits, stats, scale, table_part, teach_parts, near):
    count, vocab = logits.shape
    width = table_part.shape[0]
    block = count // near
    members = stats.shape[0]
    whole = pl.BlockSpec((block, vocab), lambda i, _: (0, 0))
    return pl.pallas_call(
        head_back_kernel,
        grid_spec=pltpu.PrefetchScalarGridSpec(
            num_scalar_prefetch=1,
            grid=(near,),
            in_specs=[
                pl.BlockSpec((block, vocab), lambda i, _: (i, 0)),
                pl.BlockSpec((members, 1, 8, block), lambda i, _: (0, i, 0, 0)),
                pl.BlockSpec((1, 1, block), lambda i, _: (i, 0, 0)),
                pl.BlockSpec((width, vocab), lambda i, _: (0, 0)),
            ]
            + [whole] * near,
            out_specs=[
                pl.BlockSpec((block, vocab), lambda i, _: (i, 0)),
                pl.BlockSpec((block, width), lambda i, _: (i, 0)),
                pl.BlockSpec((1, vocab), lambda i, _: (0, 0)),
                pl.BlockSpec((1, 1, block), lambda i, _: (i, 0, 0)),
            ],
            scratch_shapes=[pltpu.VMEM((block, vocab), jnp.bfloat16)],
        ),
        out_shape=[
            jax.ShapeDtypeStruct((count, vocab), jnp.bfloat16),
            jax.ShapeDtypeStruct((count, width), jnp.float32),
            jax.ShapeDtypeStruct((1, vocab), jnp.float32),
            jax.ShapeDtypeStruct((near, 1, block), jnp.float32),
        ],
        compiler_params=pltpu.CompilerParams(vmem_limit_bytes=56 * 1024 * 1024),
        cost_estimate=COST,
        name="head_back",
    )(place, logits, stats, scale, table_part, *teach_parts)


def layer_forward(
    embedded,
    lengths,
    seqs,
    weight_qkv,
    weight_out,
    weight_up,
    weight_down_after,
    parts,
    before_attention,
):
    (
        gain_embed,
        shift_embed,
        gain_attn,
        shift_attn,
        gain_ffn,
        shift_ffn,
        bias_query,
        bias_value,
        bias_out,
        bias_hidden,
        bias_down,
    ) = parts
    normed = layer_norm(embedded, gain_embed, shift_embed)
    normed_low = normed.astype(jnp.bfloat16)
    qkv_bias = jnp.concatenate([bias_query, jnp.zeros_like(bias_query), bias_value])
    qkv_low = (project(normed_low, weight_qkv) + qkv_bias).astype(jnp.bfloat16)
    context_low = attend(qkv_low, lengths, seqs, *before_attention)
    first_sum = normed + project(context_low, weight_out) + bias_out
    first_out = layer_norm(first_sum, gain_attn, shift_attn)
    first_low = first_out.astype(jnp.bfloat16)
    pre_act = project(first_low, weight_up) + bias_hidden
    share = 0.5 + 0.5 * lax.erf(pre_act * math.sqrt(0.5))
    act_low = (pre_act * share).astype(jnp.bfloat16)
    weight_down = weight_down_after()
    slope = share + pre_act * jnp.exp(-0.5 * pre_act * pre_act) * (1.0 / math.sqrt(2.0 * math.pi))
    second_sum = first_out + project(act_low, weight_down) + bias_down
    final = layer_norm(second_sum, gain_ffn, shift_ffn)
    saved = (
        embedded,
        normed_low,
        qkv_low,
        context_low,
        first_sum,
        first_low,
        slope,
        act_low,
        second_sum,
    )
    return (final, saved, weight_down)


def layer_backward(
    grad_final,
    saved,
    lengths,
    seqs,
    weight_qkv,
    weight_out,
    weight_up,
    weight_down,
    parts,
    sums,
    line,
    embed_columns,
    stack_rows,
    down_rows,
):
    (
        gain_embed,
        shift_embed,
        gain_attn,
        shift_attn,
        gain_ffn,
        shift_ffn,
        bias_query,
        bias_value,
        bias_out,
        bias_hidden,
        bias_down,
    ) = parts
    (
        embedded,
        normed_low,
        qkv_low,
        context_low,
        first_sum,
        first_low,
        slope,
        act_low,
        second_sum,
    ) = saved
    width = embedded.shape[1]
    grad_second, grad_gain_ffn, grad_shift_ffn = norm_back(
        second_sum, gain_ffn, shift_ffn, grad_final
    )
    grad_down_low = grad_second.astype(jnp.bfloat16)
    sums.begin("down", [(grad_down_low, act_low)], down_rows)
    grad_pre_low = (
        project_back(grad_down_low, weight_down) * slope
    ).astype(jnp.bfloat16)
    grad_pre_low = lax.optimization_barrier(grad_pre_low)
    sums.begin("up", [(grad_pre_low, first_low)], stack_rows)
    grad_first = grad_second + project_back(grad_pre_low, weight_up)
    grad_first_sum, grad_gain_attn, grad_shift_attn = norm_back(
        first_sum, gain_attn, shift_attn, grad_first
    )
    grad_out_low = grad_first_sum.astype(jnp.bfloat16)
    grad_context_low = project_back(grad_out_low, weight_out).astype(jnp.bfloat16)
    sums.in_plane(("down", "up"))
    line_sends = line.step(grad_context_low) if line else []
    grad_qkv_low = attend_back(
        qkv_low, grad_context_low, lengths, seqs, *sums.sent("up"), *line_sends
    )
    grad_normed = grad_first_sum + project_back(grad_qkv_low, weight_qkv)
    grad_embed, grad_gain_embed, grad_shift_embed = norm_back(
        embedded, gain_embed, shift_embed, grad_normed
    )
    embed_t = embed_columns(grad_embed)
    sums.begin(
        "attention",
        [(grad_qkv_low, normed_low), (grad_out_low, context_low)],
        stack_rows,
    )
    sums.hold("attention", *(line.arrived() if line else []))
    sums.arrive(("down", "up"))
    if line:
        line.step(*sums.sent("attention"))
    vectors_grad = jnp.concatenate(
        [
            grad_gain_embed,
            grad_shift_embed,
            grad_gain_attn,
            grad_shift_attn,
            grad_gain_ffn,
            grad_shift_ffn,
            column_sum(grad_qkv_low[:, :width]),
            column_sum(grad_qkv_low[:, 2 * width :]),
            column_sum(grad_out_low),
            column_sum(grad_pre_low),
            column_sum(grad_down_low),
        ]
    )
    return (embed_t, vectors_grad)


class WeightSums:
    def __init__(self, near, far, width):
        self.near, self.staged, self.width = near, far == 4, width
        self.state = {}

    def begin(self, name, pairs, rows):
        if not self.staged:
            grads = [weight_grad(grad, given) for grad, given in pairs]
            self.state[name] = (jnp.concatenate(grads, 0), [])
        elif pairs[0][0].shape[1] % (2 * rows) or 2 * rows % 128:
            grads = [weight_grad(grad, given) for grad, given in pairs]
            self.state[name] = begin_pair_sum(jnp.concatenate(grads, 0), rows, self.near)
        else:
            keep, send = weight_sums(pairs, rows)
            shape = (-1, self.near) + keep.shape[1:]
            self.state[name] = (keep.reshape(shape), [send.reshape(shape)])

    def sent(self, name):
        return self.state[name][1] if self.staged else []

    def narrow(self, x):
        parts = [
            x[..., j : j + self.width] for j in range(0, x.shape[-1], self.width)
        ]
        return parts[0] if len(parts) == 1 else jnp.concatenate(parts, -2)

    def in_plane(self, names):
        if not self.staged:
            return
        p = lax.axis_index("fsdp") % self.near
        sends = [[] for _ in range(self.near)]
        for name in names:
            keep, pair_sends = self.state[name]
            arrived = swap(pair_sends[0], "vocab", 1)
            for k in range(self.near):
                part = lax.dynamic_index_in_dim(keep, p ^ k, 1, False)
                part = part + lax.dynamic_index_in_dim(arrived, p ^ k, 1, False).astype(jnp.float32)
                part = part.astype(jnp.bfloat16) if k else part
                sends[k].append(self.narrow(part).reshape(-1, self.width))
        own, *sends = [
            parts[0] if len(parts) == 1 else jnp.concatenate(parts, 0) for parts in sends
        ]
        for name in names:
            self.state[name] = (own, sends)

    def hold(self, name, *needed):
        if self.staged:
            keep, sends = self.state[name]
            self.state[name] = (keep, after(sends, *needed))

    def arrive(self, names):
        if not self.staged:
            return []
        sends = self.state[names[0]][1]
        self.arrived = [swap(send, "fsdp", k) for k, send in enumerate(sends, 1)]
        return self.arrived

    def plane_total(self, name, arrived):
        return added(self.state[name][0], arrived)


def adam(weight_matrix, grad, first, second, rate):
    first = BETA_ONE * first + (1.0 - BETA_ONE) * grad
    second = BETA_TWO * second + (1.0 - BETA_TWO) * grad * grad
    first_hat = first / (1.0 - BETA_ONE**STEP)
    second_hat = second / (1.0 - BETA_TWO**STEP)
    new = weight_matrix - rate * (
        first_hat / (jnp.sqrt(second_hat) + ADAM_EPS) + WEIGHT_DECAY * weight_matrix
    )
    return (first, second, new)


def local(
    token_ids,
    lengths,
    masked_pos,
    teacher,
    stack_index,
    down_index,
    stack_next,
    down_next,
    word_table,
    table_first,
    table_second,
    pos_table,
    pos_first,
    pos_second,
    proj_stack,
    stack_first,
    stack_second,
    ffn_down,
    down_first,
    down_second,
    vectors,
    vectors_first,
    vectors_second,
    head_bias,
    bias_first,
    bias_second_moment,
):
    size = lax.axis_size("fsdp")
    near = math.gcd(4, size)
    far = size // near
    width = proj_stack.shape[1]
    units = ffn_down.shape[1]
    pair_seqs, seq_len = token_ids.shape
    own_seqs = pair_seqs // 2
    own_rows = own_seqs * seq_len
    core = lax.axis_index("vocab")
    place = lax.axis_index("fsdp")
    p = place % near
    vocab_dev, columns = word_table.shape
    part = vocab_dev // near
    mask_slots = masked_pos.shape[1]

    table_t = word_table.T
    all_ids = lax.all_to_all(
        jnp.broadcast_to(token_ids[None], (size, pair_seqs, seq_len)), "fsdp", 0, 0, tiled=True
    ).reshape(size, 2, own_seqs, seq_len)
    local_ids = (
        jnp.concatenate(
            [
                lax.dynamic_index_in_dim(all_ids, core, 1, False),
                lax.dynamic_index_in_dim(all_ids, 1 - core, 1, False),
            ],
            0,
        ).reshape(2 * size * own_seqs, 1, seq_len)
        - core * vocab_dev
    )

    stack_mask = kept(stack_index)
    down_mask = kept(down_index)
    stack_rows = proj_stack.shape[0]
    down_rows = ffn_down.shape[0]
    small_count = vectors.shape[0]
    own_stack = jnp.where(stack_mask, proj_stack, 0.0).astype(jnp.bfloat16)
    own_down = jnp.where(down_mask, ffn_down, 0.0).astype(jnp.bfloat16)
    pos_rows = -(-(columns // 2) // 16) * 16
    own_stack = jnp.concatenate(
        [
            own_stack,
            jnp.pad(
                pos_table.T.astype(jnp.bfloat16),
                ((0, pos_rows - columns // 2), (0, width - seq_len)),
            ),
            jnp.pad(
                vectors.astype(jnp.bfloat16)[None], ((0, 15), (0, width - small_count))
            ),
        ],
        0,
    )
    table_low = table_t.astype(jnp.bfloat16)
    half = size * own_seqs
    table_blocks = table_low.reshape(columns, near, part).transpose(1, 0, 2)
    teacher_blocks = [
        lax.dynamic_slice_in_dim(teacher, (p ^ k) * part, part, 1) for k in range(near)
    ]
    teach_parts = teacher_blocks[:1] + [
        swap(block, "fsdp", k) for k, block in enumerate(teacher_blocks[1:], 1)
    ]
    if far == 4:
        own_stack = after(own_stack, all_ids)
        stack_line = [swap(own_stack, "fsdp", k * near) for k in range(1, far)]
        near_table = exchange(table_blocks, near_groups(near)).reshape(near * columns, part)
        other_found = lookup(table_t, local_ids[half:], own_stack)
        swapped = swap(other_found, "vocab", 1)
        own_found = lookup(table_t, local_ids[:half], other_found, near_table)
        stack_line = jnp.stack([own_stack] + after(stack_line, own_found))
        own_found = own_found + swapped
        stack_pieces = gather_pieces(stack_line)
        tokens_t = exchange(own_found.reshape(size, own_seqs, columns, seq_len), None)
        down_line = exchange(
            after(jnp.broadcast_to(own_down[None], (far,) + own_down.shape), tokens_t),
            far_groups(near),
        )
        own_blocks = exchange(
            jnp.broadcast_to(down_line[None], (near,) + down_line.shape), near_groups(near)
        )
        stack_others = [[swap(piece, "vocab", 1) for piece in half] for half in stack_pieces]
        own_blocks = exchange(
            after(
                jnp.broadcast_to(down_line[None], (near,) + down_line.shape),
                stack_pieces[0][3],
                stack_pieces[1][3],
            ),
            near_groups(near),
        )
        other_blocks = swap(own_blocks, "vocab", 1)
        before_attention = [own_blocks]
        qkv_blocks = 3 * width // stack_rows
        attention_blocks = 4 * width // stack_rows
        weight_qkv, weight_out, weight_up, small = place_blocks(
            [piece for group in (stack_pieces, stack_others) for half in group for piece in half],
            [
                (place ^ ((first + kz) * near + kp)) * 2 + (core ^ kc)
                for kc in range(2)
                for first in (0, far // 2)
                for kp in range(near)
                for kz in range(far // 2)
            ],
            (
                (0, qkv_blocks, 0, stack_rows),
                (qkv_blocks, attention_blocks, 0, stack_rows),
                (attention_blocks, 2 * size, 0, stack_rows),
                (0, 2 * size, stack_rows, pos_rows + 16),
            ),
        )
        weight_qkv = weight_qkv.reshape(-1, width)
        weight_out = weight_out.reshape(-1, width)
        weight_up = weight_up.reshape(-1, width)

        def weight_down_after():
            arrived = [own_blocks, other_blocks]
            (weight_down,) = place_blocks(
                [blocks.reshape((size,) + own_down.shape) for blocks in arrived],
                [
                    (kz * near + kp) * 2 + (core ^ kc)
                    for kc in range(2)
                    for kp in range(near)
                    for kz in range(far)
                ],
                ((0, 2 * size, 0, down_rows),),
            )
            return weight_down.reshape(-1, units)

    else:
        before_attention = []
        stack_all = lax.all_gather(own_stack, BOTH, axis=0)
        dense_stack = stack_all[:, :stack_rows].reshape(-1, width)
        small = stack_all[:, stack_rows:]
        weight_qkv = dense_stack[: 3 * width]
        weight_out = dense_stack[3 * width : 4 * width]
        weight_up = dense_stack[4 * width :]
        weight_down = lax.all_gather(own_down, BOTH, axis=0, tiled=True)

        def weight_down_after():
            return weight_down

        near_table = exchange(table_blocks, near_groups(near)).reshape(near * columns, part)
        found = lookup(table_t, local_ids)
        own_found = found[:half] + swap(found[half:], "vocab", 1)
        tokens_t = exchange(own_found.reshape(size, own_seqs, columns, seq_len), None)
    pos_all_t = small[:, : columns // 2, :seq_len].reshape(width, seq_len)
    vectors_all = small[:, pos_rows, :small_count].reshape(-1)
    parts = split_vectors(vectors_all.astype(jnp.float32), width)

    table_part = far_gather(near_table, near)
    tokens_t = tokens_t.transpose(1, 0, 2, 3).reshape(own_seqs, width, seq_len)
    embedded = (
        tokens_t.transpose(0, 2, 1).astype(jnp.float32)
        + pos_all_t.T.astype(jnp.float32)[None]
    ).reshape(own_rows, width)

    seq_start = place * pair_seqs + core * own_seqs
    own_lengths = lax.dynamic_slice_in_dim(lengths, seq_start, own_seqs)
    final, saved, weight_down = layer_forward(
        embedded,
        own_lengths,
        own_seqs,
        weight_qkv,
        weight_out,
        weight_up,
        weight_down_after,
        parts,
        before_attention,
    )
    own_pos = lax.dynamic_slice_in_dim(masked_pos, seq_start, own_seqs, 0)
    flat_rows = (jnp.arange(own_seqs, dtype=jnp.int32)[:, None] * seq_len + own_pos).reshape(-1)
    picked = jnp.take(final.reshape(own_rows, width), flat_rows, axis=0).astype(jnp.bfloat16)
    rows = join(picked, "vocab", 1).reshape(-1, width)
    rows = in_order(near_exchange(lambda q: rows, near), near).reshape(-1, width)

    bias_part = lax.dynamic_slice_in_dim(head_bias, p * part, part)
    own_place = p.astype(jnp.int32).reshape(1)
    output_logits, stats = head(
        own_place, rows, table_part, bias_part[None], teach_parts, near
    )
    stats = jnp.stack([stats, swap(stats, "vocab", 1)])
    stats = jnp.concatenate(near_exchange(lambda q: stats, near), 0)
    group_start = (place - p) * pair_seqs
    group_pos = lax.dynamic_slice_in_dim(masked_pos, group_start, near * pair_seqs, 0)
    group_lengths = lax.dynamic_slice_in_dim(lengths, group_start, near * pair_seqs)
    group_valid = (group_pos < group_lengths[:, None]).astype(jnp.float32).reshape(near, 1, -1)
    count = jnp.sum((masked_pos < lengths[:, None]).astype(jnp.float32))
    grad_logits, rows_grad, bias_part_grad, divergence = head_back(
        own_place, output_logits, stats, group_valid / count, table_part, teach_parts, near
    )
    group_loss = jnp.sum(divergence * group_valid) / (2 * near)
    rows_grad = halve(rows_grad.reshape(near, 2, -1, width).transpose(1, 0, 2, 3), "vocab", 1)
    rows_sends = [lax.dynamic_index_in_dim(rows_grad, p ^ k, 0, False) for k in range(near)]
    own_rows_grad = tree_sum(
        [rows_sends[0]] + [swap(send, "fsdp", k) for k, send in enumerate(rows_sends[1:], 1)]
    )
    grad_final = (
        jnp.zeros((own_rows, width), jnp.float32)
        .at[flat_rows]
        .add(own_rows_grad)
    )

    bias_full = lax.dynamic_update_slice_in_dim(
        jnp.zeros((vocab_dev,), jnp.float32), bias_part_grad[0], p * part, 0
    )
    head_grad = lax.dot_general(
        rows,
        grad_logits,
        (((0,), (0,)), ((), ())),
        preferred_element_type=jnp.float32,
    ).reshape(far, near, columns, part)
    if far == 4:
        line = FarLine(head_grad, near)
        line_sends = line.step()
        grad_final = after(grad_final, *line_sends)
    else:
        line = None

    def embed_columns(grad_embed):
        embed_t = grad_embed.reshape(own_seqs, seq_len, width).astype(jnp.bfloat16)
        embed_t = embed_t.transpose(0, 2, 1).reshape(own_seqs, size, columns, seq_len)
        return embed_t.transpose(1, 0, 2, 3)

    sums = WeightSums(near, far, width)
    embed_t, vectors_grad = layer_backward(
        grad_final,
        saved,
        own_lengths,
        own_seqs,
        weight_qkv,
        weight_out,
        weight_up,
        weight_down,
        parts,
        sums,
        line,
        embed_columns,
        stack_rows,
        down_rows,
    )

    embed_t = lax.all_to_all(embed_t, "fsdp", 0, 0, tiled=True).reshape(half, columns, seq_len)
    if far == 4:
        first_plane = sums.plane_total("up", sums.arrived)
        down_plane = first_plane[: far * (units // width) * down_rows].reshape(far, -1, width)
        up_plane = first_plane[far * (units // width) * down_rows :].reshape(-1, stack_rows, width)
        sums.in_plane(("attention",))
        attention_sends = sums.sent("attention")
        other_t = swap(embed_t, "vocab", 1)
        token_grad = spread_add(embed_t, local_ids[:half], vocab_dev, other_t, *attention_sends)
        head_grad = line.total(token_grad)
        blocks_sent = [
            lax.dynamic_index_in_dim(head_grad, p ^ k, 0, False) for k in range(near)
        ]
        blocks = [swap(block, "fsdp", k) for k, block in enumerate(blocks_sent[1:], 1)]
        attention_plane = sums.plane_total(
            "attention", after(sums.arrive(("attention",)), token_grad)
        ).reshape(-1, stack_rows, width)
        own = jnp.concatenate(
            [jnp.concatenate([attention_plane, up_plane], 0), down_plane], 1
        )
        far_low = own.astype(jnp.bfloat16)
        arrived = exchange(far_low, far_groups(near))
        last_grad = spread_add(
            other_t, local_ids[half:], vocab_dev, far_low, *blocks_sent
        )
        blocks = blocks_sent[:1] + after(blocks, last_grad)
        token_grad = token_grad + last_grad
        vectors_grad = after(vectors_grad, far_low)
        vectors_grad = vectors_grad + swap(vectors_grad, "vocab", 1)
        small_sums = jnp.concatenate([bias_full, vectors_grad])
        small_sums = tree_sum(near_exchange(lambda q: small_sums, near))
        small_sums = sum_far(small_sums, near)
        z = place // near
        other = lax.broadcasted_iota(jnp.int32, (far, 1, 1), 0) != z
        total = jnp.sum(jnp.where(other, arrived.astype(jnp.float32), own), axis=0)
        stack_total = total[:stack_rows]
        down_total = jnp.concatenate(
            jnp.split(total[stack_rows:], units // width, axis=0), 1
        )
        embed_t = jnp.concatenate([embed_t, other_t], 0)
    else:
        embed_t = jnp.concatenate([embed_t, swap(embed_t, "vocab", 1)], 0)
        token_grad = spread_add(embed_t, local_ids, vocab_dev)
        vectors_grad = vectors_grad + swap(vectors_grad, "vocab", 1)
        small_sums = jnp.concatenate([bias_full, vectors_grad])
        small_sums = tree_sum(near_exchange(lambda q: small_sums, near))
        small_sums = sum_far(small_sums, near)
        head_grad = far_reduce(head_grad, near)
        blocks = near_exchange(lambda q: lax.dynamic_index_in_dim(head_grad, q, 0, False), near)
        stack_grad = [sums.state[name][0] for name in ("attention", "up")]
        stack_total = lax.psum_scatter(
            jnp.concatenate(stack_grad, 0), BOTH, scatter_dimension=0, tiled=True
        )
        down_total = lax.psum_scatter(
            sums.state["down"][0], BOTH, scatter_dimension=0, tiled=True
        )
    bias_grad, vectors_grad = small_sums[:vocab_dev], small_sums[vocab_dev:]
    head_grad_t = jnp.concatenate(list(in_order(blocks, near)), 1).astype(jnp.float32)
    table_total = head_grad_t + token_grad
    pos_total = jnp.sum(embed_t.astype(jnp.float32), axis=0)
    pos_total = lax.dynamic_slice_in_dim(pos_total, core * (columns // 2), columns // 2, 0)
    vectors_total = lax.dynamic_slice_in_dim(
        vectors_grad, (2 * place + core) * small_count, small_count
    )

    stack_total = stack_total + jnp.where(stack_mask, 0.0, PRUNE_DECAY) * proj_stack
    down_total = down_total + jnp.where(down_mask, 0.0, PRUNE_DECAY) * ffn_down
    changes = jnp.sum((stack_mask != kept(stack_next)).astype(jnp.float32)) + jnp.sum(
        (down_mask != kept(down_next)).astype(jnp.float32)
    )
    squares = (
        jnp.sum(stack_total * stack_total)
        + jnp.sum(down_total * down_total)
        + jnp.sum(pos_total * pos_total)
        + jnp.sum(vectors_total * vectors_total)
        + jnp.sum(table_total * table_total)
        + jnp.sum(bias_grad * bias_grad) / size
    )
    scalars = jnp.stack([squares, group_loss, changes])
    scalars = sum_all(scalars, near)
    total_squares, loss_sum, change_total = scalars[0], scalars[1], scalars[2]
    grad_norm = jnp.sqrt(total_squares)
    factor = jnp.minimum(1.0, CLIP / (grad_norm + 1e-06))
    table_out = adam(table_t, table_total * factor, table_first.T, table_second.T, RATE_MATRIX)
    pos_out = adam(pos_table.T, pos_total * factor, pos_first.T, pos_second.T, RATE_MATRIX)
    stack_out = adam(proj_stack, stack_total * factor, stack_first, stack_second, RATE_MATRIX)
    down_out = adam(ffn_down, down_total * factor, down_first, down_second, RATE_MATRIX)
    vectors_out = adam(vectors, vectors_total * factor, vectors_first, vectors_second, RATE_VECTOR)
    bias_out = adam(head_bias, bias_grad * factor, bias_first, bias_second_moment, RATE_VECTOR)
    return (
        table_out[0].T,
        table_out[1].T,
        table_out[2].T,
        pos_out[0].T,
        pos_out[1].T,
        pos_out[2].T,
        stack_out[0],
        stack_out[1],
        stack_out[2],
        down_out[0],
        down_out[1],
        down_out[2],
        vectors_out[0],
        vectors_out[1],
        vectors_out[2],
        bias_out[0],
        bias_out[1],
        bias_out[2],
        loss_sum,
        count,
        grad_norm,
        change_total.astype(jnp.int32),
    )


def solution(mesh):
    in_specs = (
        P("fsdp", None),
        P(),
        P(),
        P("fsdp", "vocab"),
        P(("fsdp", "vocab"), None),
        P(("fsdp", "vocab"), None),
        P(("fsdp", "vocab"), None),
        P(("fsdp", "vocab"), None),
        P("vocab", "fsdp"),
        P("vocab", "fsdp"),
        P("vocab", "fsdp"),
        P(None, ("fsdp", "vocab")),
        P(None, ("fsdp", "vocab")),
        P(None, ("fsdp", "vocab")),
        P(("fsdp", "vocab"), None),
        P(("fsdp", "vocab"), None),
        P(("fsdp", "vocab"), None),
        P(("fsdp", "vocab"), None),
        P(("fsdp", "vocab"), None),
        P(("fsdp", "vocab"), None),
        P(("fsdp", "vocab")),
        P(("fsdp", "vocab")),
        P(("fsdp", "vocab")),
        P("vocab"),
        P("vocab"),
        P("vocab"),
    )
    out_specs = (
        P("vocab", "fsdp"),
        P("vocab", "fsdp"),
        P("vocab", "fsdp"),
        P(None, ("fsdp", "vocab")),
        P(None, ("fsdp", "vocab")),
        P(None, ("fsdp", "vocab")),
        P(("fsdp", "vocab"), None),
        P(("fsdp", "vocab"), None),
        P(("fsdp", "vocab"), None),
        P(("fsdp", "vocab"), None),
        P(("fsdp", "vocab"), None),
        P(("fsdp", "vocab"), None),
        P(("fsdp", "vocab")),
        P(("fsdp", "vocab")),
        P(("fsdp", "vocab")),
        P("vocab"),
        P("vocab"),
        P("vocab"),
        P(),
        P(),
        P(),
        P(),
    )
    return jax.shard_map(local, mesh=mesh, in_specs=in_specs, out_specs=out_specs, check_vma=False)
```
